128 devices in a mesh: dp: 128 (over x, y, z, core).
Axes of the slice: x: 4, y: 4, z: 4, core: 2. Of those that a mesh axis runs over, the one named last changes fastest.
Arguments:
- latent: bfloat16 [512, 6, 6, 6, 256], P('dp'), may hold values from -6 to 6
- out_grad: bfloat16 [512, 3, 3, 3, 256], P('dp'), may hold values from -6 to 6
- first_kernel: float32 [27, 65536], P(None, 'dp'), may hold values from -0.078125 to 0.078125
- first_mean: float32 [27, 65536], P(None, 'dp'), may hold values from -0.15625 to 0.15625
- first_square: float32 [27, 65536], P(None, 'dp'), may hold values from 0.0001 to 0.01
- second_kernel: float32 [27, 65536], P(None, 'dp'), may hold values from -0.078125 to 0.078125
- second_mean: float32 [27, 65536], P(None, 'dp'), may hold values from -0.15625 to 0.15625
- second_square: float32 [27, 65536], P(None, 'dp'), may hold values from 0.0001 to 0.01
Outputs:
- block_out: bfloat16 [512, 3, 3, 3, 256], P('dp')
- first_kernel_new: float32 [27, 65536], P(None, 'dp')
- first_mean_new: float32 [27, 65536], P(None, 'dp')
- first_square_new: float32 [27, 65536], P(None, 'dp')
- second_kernel_new: float32 [27, 65536], P(None, 'dp')
- second_mean_new: float32 [27, 65536], P(None, 'dp')
- second_square_new: float32 [27, 65536], P(None, 'dp')
The draws below stay inside these ranges and needn't reach their ends.
All inputs are finite; a program needn't handle non-finite values.
Results may differ from the reference program's by a relative error of at most 0.0042.
Values may be sent and summed in bfloat16 or wider, within the bound.
No kernel may reach another device: no remote copies, remote signals or barrier semaphores. Data moves between devices by JAX's collectives and lax.ppermute only.
A program may use at most 128 MiB of HBM per device.

```python
import math
import jax
import jax.numpy as jnp
from jax import lax

C = 256
PATCH = 6
OUTER = 3
SAMPLES = 512


def block_scale(stream_key, shape, pieces, low, top_value):
    factor_of = 1.0
    for axis_at, blocks in pieces:
        draws = jax.random.uniform(jax.random.fold_in(jax.random.fold_in(stream_key, 6), axis_at), (blocks,), jnp.float32, low / len(pieces), top_value / len(pieces))
        factor_of = factor_of * jnp.repeat(jnp.exp(draws), shape[axis_at] // blocks).reshape((-1,) + (1,) * (len(shape) - 1 - axis_at))
    return factor_of


def bell_draw(rng, extent, spread, bound, shards=(), kind=jnp.bfloat16):
    entries = spread * jax.random.normal(rng, extent, jnp.float32)
    if shards:
        entries = entries * block_scale(rng, extent, shards, -0.22, 0.18)
    return jnp.clip(entries, -bound, bound).astype(kind)


def setup_inputs(seed: int = 0) -> dict:
    keys = jax.random.split(jax.random.key(seed), 9)
    latent = bell_draw(keys[0], (SAMPLES, PATCH, PATCH, PATCH, C), 1.0, 6.0, ((0, 128),))
    out_grad = bell_draw(keys[1], (SAMPLES, OUTER, OUTER, OUTER, C), 1.0, 6.0, ((0, 128),))
    first_kernel = bell_draw(keys[2], (27, C * C), (27 * C) ** -0.5, 0.078125, ((1, 128),), jnp.float32)
    first_mean = bell_draw(keys[3], (27, C * C), 0.01, 0.15625, ((1, 128),), jnp.float32)
    first_square = jnp.clip(jnp.exp(math.log(0.01) - 4.6051702 * jax.random.uniform(keys[4], (27, C * C), jnp.float32) ** block_scale(keys[4], (27, C * C), ((1, 128),), -0.2, 0.2)), 0.0001, 0.01)
    second_kernel = bell_draw(keys[5], (27, C * C), (27 * C) ** -0.5, 0.078125, ((1, 128),), jnp.float32)
    second_mean = bell_draw(keys[6], (27, C * C), 0.01, 0.15625, ((1, 128),), jnp.float32)
    second_square = jnp.clip(jnp.exp(math.log(0.01) - 4.6051702 * jax.random.uniform(keys[7], (27, C * C), jnp.float32) ** block_scale(keys[7], (27, C * C), ((1, 128),), -0.2, 0.2)), 0.0001, 0.01)
    return dict(latent=latent, out_grad=out_grad, first_kernel=first_kernel, first_mean=first_mean, first_square=first_square, second_kernel=second_kernel, second_mean=second_mean, second_square=second_square)


DIMS = ('NDHWC', 'DHWIO', 'NDHWC')

def slope(value):
    sigma = jax.nn.sigmoid(value)
    return sigma * (1.0 + value * (1.0 - sigma))

def conv_one(inputs, kernel):
    return lax.conv_general_dilated(inputs, kernel, (1, 1, 1), ((1, 1), (1, 1), (1, 1)), dimension_numbers=DIMS, precision=lax.Precision.HIGHEST)

def conv_two(inputs, kernel):
    return lax.conv_general_dilated(inputs, kernel, (2, 2, 2), ((1, 1), (1, 1), (1, 1)), dimension_numbers=DIMS, precision=lax.Precision.HIGHEST)

def adam_update(weight, first, second, grad):
    first_new = 0.9 * first + 0.1 * grad
    second_new = 0.999 * second + 0.001 * grad * grad
    fix_first = 1.0 - 0.9 ** 10
    fix_second = 1.0 - 0.999 ** 10
    weight_new = weight - 0.05 * (first_new / fix_first) / (jnp.sqrt(second_new / fix_second) + 1e-08)
    return (weight_new, first_new, second_new)

def reference(latent, out_grad, first_kernel, first_mean, first_square, second_kernel, second_mean, second_square):
    kernel1 = first_kernel.astype(jnp.bfloat16).astype(jnp.float32).reshape(3, 3, 3, C, C)
    kernel2 = second_kernel.astype(jnp.bfloat16).astype(jnp.float32).reshape(3, 3, 3, C, C)
    source = latent.astype(jnp.float32)
    act = conv_one(source, kernel1)
    hidden = jax.nn.silu(act).astype(jnp.bfloat16).astype(jnp.float32)
    conv, pull_two = jax.vjp(conv_two, hidden, kernel2)
    pre = conv + source[:, ::2, ::2, ::2, :]
    block_out = jax.nn.silu(pre).astype(jnp.bfloat16)
    grad_pre = (out_grad.astype(jnp.float32) * slope(pre)).astype(jnp.bfloat16).astype(jnp.float32)
    grad_hidden, grad2 = pull_two(grad_pre)
    grad_act = (grad_hidden * slope(act)).astype(jnp.bfloat16).astype(jnp.float32)
    _, pull_one = jax.vjp(conv_one, source, kernel1)
    grad1 = pull_one(grad_act)[1]
    grad1 = grad1.reshape(27, C * C) / SAMPLES
    grad2 = grad2.reshape(27, C * C) / SAMPLES
    new_one = adam_update(first_kernel, first_mean, first_square, grad1)
    new_two = adam_update(second_kernel, second_mean, second_square, grad2)
    return (block_out, new_one[0], new_one[1], new_one[2], new_two[0], new_two[1], new_two[2])
```

```python
import functools
import itertools

import jax
import jax.numpy as jnp
import numpy as np
from jax import lax
from jax.experimental import pallas as pl
from jax.experimental.pallas import tpu as pltpu
from jax.sharding import PartitionSpec as P

C = 256
HALF = 128
EDGE = 6
OUTER = 3
TAPS = 27
SAMP = 4
ROWS = 32
ACT_ROWS = EDGE * EDGE * ROWS
PAD_ROWS = 64 * ROWS
OUT_ROWS = 16
PRE_ROWS = 9 * OUT_ROWS
VMEM_LIMIT = 56 * 1024 * 1024
BF = jnp.bfloat16
F32 = jnp.float32

VM = pl.BlockSpec(memory_space=pltpu.VMEM)


def dot(a, b):
    return jnp.dot(a, b, preferred_element_type=F32)


def dot_t(a, b):
    return lax.dot_general(a, b, (((1,), (1,)), ((), ())), preferred_element_type=F32)


def sigmoid(v):
    return 1.0 / (1.0 + jnp.exp(-v))


def load(ref, start, count, stride=1):
    return jnp.concatenate(
        [ref[half, pl.ds(start, count, stride=stride), :] for half in range(2)], axis=1
    )


def store(ref, start, count, value, stride=1):
    for half in range(2):
        ref[half, pl.ds(start, count, stride=stride), :] = value[
            :, half * HALF : (half + 1) * HALF
        ]


def one_hot(order_row):
    return (lax.broadcasted_iota(jnp.int32, (C, C), 0) == order_row).astype(BF)


def prep_kernel(latent, out_grad, order, x3, skip, cot, xs, og):
    xs[...] = jnp.zeros_like(xs)
    og[...] = jnp.zeros_like(og)
    for s in range(SAMP):
        for i in range(EDGE):
            for j in range(EDGE):
                base = 8 + ((i + 1) * 8 + j + 1) * ROWS + s * 8 + 1
                store(xs, base, EDGE, latent[s, i, j].astype(F32))
        for qi in range(OUTER):
            for qj in range(OUTER):
                base = (qi * 3 + qj) * OUT_ROWS + s * 4
                og[base : base + OUTER, :] = out_grad[s, qi, qj].astype(F32)
    cot[...] = og[...]
    for qi in range(OUTER):
        for qj in range(OUTER):
            base = 8 + ((2 * qi + 1) * 8 + 2 * qj + 1) * ROWS + 1
            skip[pl.ds((qi * 3 + qj) * OUT_ROWS, OUT_ROWS), :] = load(xs, base, OUT_ROWS, 2)
    perm = one_hot(order[...])
    for dl in range(3):
        for i in range(8):
            rows = load(xs, 7 + dl + i * 256, 256).astype(BF)
            x3[dl, i] = dot(rows, perm).astype(BF).reshape(8, ROWS, C)


def prep(latent, out_grad, order):
    return pl.pallas_call(
        prep_kernel,
        out_shape=(
            jax.ShapeDtypeStruct((3, 8, 8, ROWS, C), BF),
            jax.ShapeDtypeStruct((PRE_ROWS, C), F32),
            jax.ShapeDtypeStruct((PRE_ROWS, C), F32),
        ),
        in_specs=[VM] * 3,
        out_specs=(VM, VM, VM),
        scratch_shapes=[
            pltpu.VMEM((2, PAD_ROWS + 16, HALF), F32),
            pltpu.VMEM((PRE_ROWS, C), F32),
        ],
        compiler_params=pltpu.CompilerParams(vmem_limit_bytes=VMEM_LIMIT),
        cost_estimate=pl.CostEstimate(
            flops=2 * 3 * PAD_ROWS * C * C, bytes_accessed=8_000_000, transcendentals=0
        ),
        name="prep",
    )(latent, out_grad, order)


def swap_halves(value, core):
    swapped = jnp.concatenate([value[:, HALF:], value[:, :HALF]], axis=1)
    return jnp.where(core == 1, swapped, value)


def main_kernel(
    core_ref, x3, skip, cot, mine, recv, block_out, keep, send,
    act, hs, hsel, y, gh, gat, bo,
):
    core = core_ref[0]

    def weight(t):
        return jnp.concatenate(
            [mine[:, t].reshape(HALF, C), recv[:, t].reshape(HALF, C)], axis=0
        )

    def store_grad(t, grad_t):
        eye = (
            lax.broadcasted_iota(jnp.int32, (C, C), 0)
            == lax.broadcasted_iota(jnp.int32, (C, C), 1)
        ).astype(BF)
        grad = dot_t(eye, grad_t.astype(BF)).astype(BF)
        keep[:, t] = grad[:HALF].reshape(4, ROWS, C)
        send[:, t] = grad[HALF:].reshape(4, ROWS, C)

    act[...] = jnp.zeros_like(act)

    def first_step(n, carry):
        di, dj = n // 3, n % 3
        total = None
        for dl in range(3):
            window = x3[dl, pl.ds(di, EDGE), pl.ds(dj, EDGE)].reshape(ACT_ROWS, C)
            term = dot(window, weight(n * 3 + dl))
            total = term if total is None else total + term
        act[...] += total
        return carry

    lax.fori_loop(0, 9, first_step, 0)

    hsel[:, 0] = jnp.zeros_like(hsel[:, 0])
    hsel[:, :, 0] = jnp.zeros_like(hsel[:, :, 0])
    store(hs, ACT_ROWS, 8, jnp.zeros((8, C), F32))
    cell = lax.broadcasted_iota(jnp.int32, (EDGE * ROWS, C), 0) % 8
    inside = (cell >= 1) & (cell <= EDGE)
    for i in range(EDGE):
        part = pl.ds(i * EDGE * ROWS, EDGE * ROWS)
        value = swap_halves(act[part, :], core)
        act[part, :] = value
        hidden = jnp.where(inside, value * sigmoid(value), 0.0)
        store(hs, i * EDGE * ROWS, EDGE * ROWS, hidden.astype(BF).astype(F32))
    for dl in range(3):
        for i in range(EDGE):
            rows = load(hs, i * EDGE * ROWS + dl, EDGE * OUT_ROWS, 2)
            hsel[dl, i + 1, 1:] = rows.astype(BF).reshape(EDGE, OUT_ROWS, C)

    def strided_window(dl, di, dj):
        blocks = [
            hsel[dl, 2 * qi + di, 2 * qj + dj] for qi in range(OUTER) for qj in range(OUTER)
        ]
        return jnp.concatenate(blocks, axis=0)

    def second_step(n, total):
        di, dj = n // 3, n % 3
        for dl in range(3):
            total = total + dot(strided_window(dl, di, dj), weight(TAPS + n * 3 + dl))
        return total

    pre = lax.fori_loop(0, 9, second_step, skip[...])
    sigma = sigmoid(pre)
    bo[...] = pre * sigma
    for s in range(SAMP):
        for qi in range(OUTER):
            for qj in range(OUTER):
                base = (qi * 3 + qj) * OUT_ROWS + s * 4
                block_out[s, qi, qj] = bo[base : base + OUTER, :].astype(BF)
    grad_pre32 = (cot[...] * (sigma * (1.0 + pre * (1.0 - sigma)))).astype(BF).astype(F32)
    grad_pre = grad_pre32.astype(BF)
    grad_pre_t = grad_pre32.T.astype(BF)

    y[...] = jnp.zeros_like(y)

    def back_step(n, carry):
        di, dj = n // 3, n % 3
        for dl in range(3):
            t = TAPS + n * 3 + dl
            store_grad(t, dot(grad_pre_t, strided_window(dl, di, dj)))
            term = dot_t(grad_pre, weight(t)).reshape(9, OUT_ROWS, C)
            for qi in range(OUTER):
                for qj in range(OUTER):
                    y[dl, 2 * qi + di, 2 * qj + dj] += term[qi * 3 + qj]
        return carry

    lax.fori_loop(0, 9, back_step, 0)

    store(gh, ACT_ROWS, 8, jnp.zeros((8, C), F32))
    count = EDGE * OUT_ROWS
    for i in range(EDGE):
        base = i * EDGE * ROWS
        store(gh, base, count, y[0, i + 1, 1:].reshape(count, C), 2)
        store(gh, base + 1, count, y[1, i + 1, 1:].reshape(count, C), 2)
    for i in range(EDGE):
        base = i * EDGE * ROWS + 2
        total = load(gh, base, count, 2) + y[2, i + 1, 1:].reshape(count, C)
        store(gh, base, count, total, 2)
    for i in range(EDGE):
        part = pl.ds(i * EDGE * ROWS, EDGE * ROWS)
        value = act[part, :]
        sigma = sigmoid(value)
        grad = load(gh, i * EDGE * ROWS, EDGE * ROWS) * (sigma * (1.0 + value * (1.0 - sigma)))
        grad = swap_halves(jnp.where(inside, grad, 0.0), core)
        store(gh, i * EDGE * ROWS, EDGE * ROWS, grad.astype(BF).astype(F32))
    for n in range(ACT_ROWS // HALF):
        gat[:, n * HALF : (n + 1) * HALF] = load(gh, n * HALF, HALF).T.astype(BF)

    def first_back(n, carry):
        di, dj = n // 3, n % 3
        for dl in range(3):
            window = x3[dl, pl.ds(di, EDGE), pl.ds(dj, EDGE)].reshape(ACT_ROWS, C)
            store_grad(n * 3 + dl, dot(gat[...], window))
        return carry

    lax.fori_loop(0, 9, first_back, 0)


def block(core, x3, skip, cot, mine, recv):
    grads = jax.ShapeDtypeStruct((4, 2 * TAPS, ROWS, C), BF)
    return pl.pallas_call(
        main_kernel,
        out_shape=(
            jax.ShapeDtypeStruct((SAMP, OUTER, OUTER, OUTER, C), BF),
            grads,
            grads,
        ),
        in_specs=[pl.BlockSpec(memory_space=pltpu.SMEM)] + [VM] * 5,
        out_specs=(VM, VM, VM),
        scratch_shapes=[
            pltpu.VMEM((ACT_ROWS, C), F32),
            pltpu.VMEM((2, ACT_ROWS + 8, HALF), F32),
            pltpu.VMEM((3, 7, 7, OUT_ROWS, C), BF),
            pltpu.VMEM((3, 7, 7, OUT_ROWS, C), F32),
            pltpu.VMEM((2, ACT_ROWS + 8, HALF), F32),
            pltpu.VMEM((C, ACT_ROWS), BF),
            pltpu.VMEM((PRE_ROWS, C), F32),
        ],
        compiler_params=pltpu.CompilerParams(vmem_limit_bytes=VMEM_LIMIT),
        cost_estimate=pl.CostEstimate(
            flops=8_000_000_000, bytes_accessed=18_000_000, transcendentals=1_000_000
        ),
        name="block",
    )(core, x3, skip, cot, mine, recv)


def place(x, y, z, c):
    return ((x * 4 + y) * 4 + z) * 2 + c


def channel_orders():
    orders = []
    for c in range(2):
        order = []
        for a, b, d in itertools.product(range(4), repeat=3):
            x, y, z = (b, d, a) if c == 0 else (a, b, d)
            order += [2 * place(x, y, z, c), 2 * place(x, y, z, c) + 1]
        orders.append(order)
    zero, one = orders
    return np.array([zero + one, one + zero], np.int32).reshape(2, 1, C)


ORDERS = channel_orders()


def pack_kernel(first, second, order, out, flat):
    perm = one_hot(order[...])
    for i in range(2):
        lanes = slice(i * C, (i + 1) * C)
        flat[:TAPS, lanes] = dot(first[:, lanes].astype(BF), perm)
        flat[TAPS:, lanes] = second[:, lanes].astype(BF).astype(F32)
    shard = flat[...].astype(BF)
    for n in range(16):
        out[n] = shard


def pack(first, second, order):
    return pl.pallas_call(
        pack_kernel,
        out_shape=jax.ShapeDtypeStruct((16, 2 * TAPS, 2 * C), BF),
        in_specs=[VM] * 3,
        out_specs=VM,
        scratch_shapes=[pltpu.VMEM((2 * TAPS, 2 * C), F32)],
        compiler_params=pltpu.CompilerParams(vmem_limit_bytes=VMEM_LIMIT),
        name="pack",
    )(first, second, order)


def spread_kernel(shards, out, wide):
    for m in range(16):
        rows = shards[m].astype(F32)
        for i in range(2):
            store(wide, 2 * m + i, 2 * TAPS, rows[:, i * C : (i + 1) * C], ROWS)

    def step(t, carry):
        value = load(wide, pl.multiple_of(t * ROWS, ROWS), ROWS).astype(BF)
        for n in range(4):
            out[n, t] = value
        return carry

    lax.fori_loop(0, 2 * TAPS, step, 0)


def spread(shards):
    return pl.pallas_call(
        spread_kernel,
        out_shape=jax.ShapeDtypeStruct((4, 2 * TAPS, ROWS, C), BF),
        in_specs=[VM],
        out_specs=VM,
        scratch_shapes=[pltpu.VMEM((2, 2 * TAPS * ROWS, HALF), F32)],
        compiler_params=pltpu.CompilerParams(vmem_limit_bytes=VMEM_LIMIT),
        name="spread",
    )(shards)


def pair_kernel(one, two, out):
    def step(t, carry):
        for n in range(4):
            out[n, t] = (one[n, t].astype(F32) + two[n, t].astype(F32)).astype(BF)
        return carry

    lax.fori_loop(0, 2 * TAPS, step, 0)


def pair_sum(one, two):
    return pl.pallas_call(
        pair_kernel,
        out_shape=jax.ShapeDtypeStruct(one.shape, BF),
        in_specs=[VM] * 2,
        out_specs=VM,
        compiler_params=pltpu.CompilerParams(vmem_limit_bytes=VMEM_LIMIT),
        name="pair_sum",
    )(one, two)


def collect_kernel(parts, out, wide):
    def step(t, carry):
        total = parts[0, t].astype(F32)
        for n in range(1, 4):
            total = total + parts[n, t].astype(F32)
        store(wide, pl.multiple_of(t * ROWS, ROWS), ROWS, total)
        return carry

    lax.fori_loop(0, 2 * TAPS, step, 0)
    for m in range(16):
        for i in range(2):
            rows = load(wide, 2 * m + i, 2 * TAPS, ROWS)
            out[m, :, i * C : (i + 1) * C] = rows.astype(BF)


def collect(parts):
    return pl.pallas_call(
        collect_kernel,
        out_shape=jax.ShapeDtypeStruct((16, 2 * TAPS, 2 * C), BF),
        in_specs=[VM],
        out_specs=VM,
        scratch_shapes=[pltpu.VMEM((2, 2 * TAPS * ROWS, HALF), F32)],
        compiler_params=pltpu.CompilerParams(vmem_limit_bytes=VMEM_LIMIT),
        name="collect",
    )(parts)


def adam_update(weight, first, second, grad):
    first_new = 0.9 * first + 0.1 * grad
    second_new = 0.999 * second + 0.001 * grad * grad
    fix_first = 1.0 - 0.9**10
    fix_second = 1.0 - 0.999**10
    weight_new = weight - 0.05 * (first_new / fix_first) / (
        jnp.sqrt(second_new / fix_second) + 1e-08
    )
    return (weight_new, first_new, second_new)


def adam_kernel(scale, parts, order, k1, m1, v1, k2, m2, v2, k1n, m1n, v1n, k2n, m2n, v2n):
    total = parts[0].astype(F32)
    for n in range(1, 16):
        total = total + parts[n].astype(F32)
    total = total * scale
    back = one_hot(order[...]).astype(F32)
    for i in range(2):
        lanes = slice(i * C, (i + 1) * C)
        grad = lax.dot_general(
            total[:TAPS, lanes],
            back,
            (((1,), (1,)), ((), ())),
            precision=lax.Precision.HIGHEST,
            preferred_element_type=F32,
        )
        k1n[:, lanes], m1n[:, lanes], v1n[:, lanes] = adam_update(
            k1[:, lanes], m1[:, lanes], v1[:, lanes], grad
        )
    k2n[...], m2n[...], v2n[...] = adam_update(k2[...], m2[...], v2[...], total[TAPS:])


def adam(scale, parts, order, *state):
    return pl.pallas_call(
        functools.partial(adam_kernel, scale),
        out_shape=(jax.ShapeDtypeStruct((TAPS, 2 * C), F32),) * 6,
        in_specs=[VM] * 8,
        out_specs=(VM,) * 6,
        compiler_params=pltpu.CompilerParams(vmem_limit_bytes=VMEM_LIMIT),
        name="adam",
    )(parts, order, *state)


def lines(c, axes):
    rest = [a for a in "xyz" if a not in axes]
    groups = []
    for fixed in itertools.product(range(4), repeat=len(rest)):
        group = []
        for moving in itertools.product(range(4), repeat=len(axes)):
            at = dict(zip(rest, fixed)) | dict(zip(axes, moving))
            group.append(place(at["x"], at["y"], at["z"], c))
        groups.append(group)
    return groups


PLANES = lines(0, "xy") + lines(1, "yz")
LINES = lines(0, "z") + lines(1, "x")
PARTNERS = [(n, n ^ 1) for n in range(128)]


def exchange(value, groups):
    return lax.all_to_all(value, "dp", 0, 0, axis_index_groups=groups, tiled=True)


def body(latent, out_grad, k1, m1, v1, k2, m2, v2):
    total_samples = latent.shape[0] * lax.axis_size("dp")
    core = lax.axis_index("dp") % 2
    orders = jnp.asarray(ORDERS)
    fixed = orders[0]
    own = lax.dynamic_index_in_dim(orders, core, keepdims=False)
    shards = exchange(pack(k1, k2, fixed), PLANES)
    mine = exchange(spread(shards), LINES)
    recv = lax.ppermute(mine, "dp", PARTNERS)
    x3, skip, cot = prep(latent, out_grad, own)
    block_out, keep, send = block(core.reshape(1), x3, skip, cot, mine, recv)
    got = lax.ppermute(send, "dp", PARTNERS)
    parts = exchange(pair_sum(keep, got), LINES)
    parts = exchange(collect(parts), PLANES)
    return (block_out, *adam(1.0 / total_samples, parts, fixed, k1, m1, v1, k2, m2, v2))


def solution(mesh):
    wide = P("dp", None, None, None, None)
    flat = P(None, "dp")
    return jax.shard_map(
        body,
        mesh=mesh,
        in_specs=(wide, wide) + (flat,) * 6,
        out_specs=(wide,) + (flat,) * 6,
        check_vma=False,
    )
```

```python
import functools
import itertools

import jax
import jax.numpy as jnp
import numpy as np
from jax import lax
from jax.experimental import pallas as pl
from jax.experimental.pallas import tpu as pltpu
from jax.sharding import PartitionSpec as P

C = 256
HALF = 128
EDGE = 6
OUTER = 3
TAPS = 27
SAMP = 4
ROWS = 32
ACT_ROWS = EDGE * EDGE * ROWS
PAD_ROWS = 64 * ROWS
OUT_ROWS = 16
PRE_ROWS = 9 * OUT_ROWS
MIB = 1024 * 1024
BF = jnp.bfloat16
F32 = jnp.float32

VM = pl.BlockSpec(memory_space=pltpu.VMEM)
SM = pl.BlockSpec(memory_space=pltpu.SMEM)
ANY = pl.BlockSpec(memory_space=pl.ANY)


def shape(dims, dtype):
    return jax.ShapeDtypeStruct(dims, dtype)


def call(kernel, name, out_shape, in_specs, scratch, mib, flops, moved):
    single = not isinstance(out_shape, tuple)
    return pl.pallas_call(
        kernel,
        out_shape=out_shape,
        in_specs=in_specs,
        out_specs=VM if single else (VM,) * len(out_shape),
        scratch_shapes=scratch,
        compiler_params=pltpu.CompilerParams(vmem_limit_bytes=mib * MIB),
        cost_estimate=pl.CostEstimate(flops=flops, bytes_accessed=moved, transcendentals=0),
        name=name,
    )


def dot(a, b):
    return jnp.dot(a, b, preferred_element_type=F32)


def dot_t(a, b):
    return lax.dot_general(a, b, (((1,), (1,)), ((), ())), preferred_element_type=F32)


def sigmoid(v):
    return 1.0 / (1.0 + jnp.exp(-v))


def load(ref, start, count, stride=1):
    return jnp.concatenate(
        [ref[half, pl.ds(start, count, stride=stride), :] for half in range(2)], axis=1
    )


def store(ref, start, count, value, stride=1):
    for half in range(2):
        ref[half, pl.ds(start, count, stride=stride), :] = value[
            :, half * HALF : (half + 1) * HALF
        ]


def one_hot(order_row):
    return (lax.broadcasted_iota(jnp.int32, (C, C), 0) == order_row).astype(BF)


def fill_cells(source, xs):
    for i in range(EDGE):
        for j in range(EDGE):
            value = source[i, j].astype(F32)
            base = 8 + ((i + 1) * 8 + j + 1) * ROWS + 1
            for l in range(EDGE):
                store(xs, base + l, SAMP, value[l], 8)


def prep_kernel(latent, other, out_grad, order, x3a, x3b, x3o, skip, cot, xs, og):
    perm = one_hot(order[...])
    xs[...] = jnp.zeros_like(xs)
    og[...] = jnp.zeros_like(og)
    fill_cells(latent, xs)
    for qi in range(OUTER):
        for qj in range(OUTER):
            q = (qi * 3 + qj) * OUT_ROWS
            value = out_grad[qi, qj].astype(F32)
            for ql in range(OUTER):
                store(og, q + ql, SAMP, value[ql], 4)
            base = 8 + ((2 * qi + 1) * 8 + 2 * qj + 1) * ROWS + 1
            skip[q : q + OUT_ROWS, :] = load(xs, base, OUT_ROWS, 2)
    cot[...] = load(og, 0, PRE_ROWS)
    for i in range(8):
        for dl in range(3):
            rows = dot(load(xs, 7 + dl + i * 256, 256).astype(BF), perm).astype(BF)
            x3a[dl, i] = rows[:, :HALF].reshape(8, ROWS, HALF)
            x3b[dl, i] = rows[:, HALF:].reshape(8, ROWS, HALF)
    fill_cells(other, xs)
    for i in range(8):
        for dl in range(3):
            rows = dot(load(xs, 7 + dl + i * 256, 256).astype(BF), perm[:, :HALF])
            x3o[dl, i] = rows.astype(BF).reshape(8, ROWS, HALF)


def prep(latent, other, out_grad, order):
    wide = shape((3, 8, 8, ROWS, HALF), BF)
    pre = shape((PRE_ROWS, C), F32)
    return call(
        prep_kernel, "prep", (wide, wide, wide, pre, pre), [VM] * 4,
        [pltpu.VMEM((2, PAD_ROWS + 16, HALF), F32), pltpu.VMEM((2, PRE_ROWS, HALF), F32)],
        20, 2_000_000_000, 8_000_000,
    )(latent, other, out_grad, order)


def swap_halves(value, core):
    swapped = jnp.concatenate([value[:, HALF:], value[:, :HALF]], axis=1)
    return jnp.where(core == 1, swapped, value)


def cell_mask():
    cell = lax.broadcasted_iota(jnp.int32, (EDGE * ROWS, C), 0) % 8
    return (cell >= 1) & (cell <= EDGE)


def fetch_weights(mine, recv, first, weights, sems):
    copies = []
    for di in range(3):
        for half, source in enumerate((mine, recv)):
            copies.append(
                pltpu.make_async_copy(
                    source.at[:, pl.ds(first + 9 * di, 9)],
                    weights.at[half, :, pl.ds(9 * di, 9)],
                    sems.at[2 * di + half],
                )
            )
            copies[-1].start()
    return copies


def weight(weights, t):
    return jnp.concatenate([weights[half, :, t].reshape(HALF, C) for half in range(2)], axis=0)


WEIGHTS = [pltpu.VMEM((2, 4, TAPS, ROWS, C), BF), pltpu.SemaphoreType.DMA((6,))]


def conv1_kernel(core_ref, x3a, x3b, mine, recv, act, hsel, hsend, weights, sems, hs):
    core = core_ref[0]
    copies = fetch_weights(mine, recv, 0, weights, sems)
    for di in range(3):
        copies[2 * di].wait()
        copies[2 * di + 1].wait()

        def step(dj, carry):
            total = None
            for dl in range(3):
                window = jnp.concatenate(
                    [
                        half[dl, pl.ds(di, EDGE), pl.ds(dj, EDGE)].reshape(ACT_ROWS, HALF)
                        for half in (x3a, x3b)
                    ],
                    axis=1,
                )
                term = dot(window, weight(weights, di * 9 + dj * 3 + dl))
                total = term if total is None else total + term
            if di == 0:
                act[...] = jnp.where(dj == 0, 0.0, act[...]) + total
            else:
                act[...] += total
            return carry

        lax.fori_loop(0, 3, step, 0)

    hsel[:, 0] = jnp.zeros_like(hsel[:, 0])
    hsel[:, :, 0] = jnp.zeros_like(hsel[:, :, 0])
    hsend[:, 0] = jnp.zeros_like(hsend[:, 0])
    hsend[:, :, 0] = jnp.zeros_like(hsend[:, :, 0])
    store(hs, ACT_ROWS, 8, jnp.zeros((8, C), F32))
    inside = cell_mask()
    for i in range(EDGE):
        part = pl.ds(i * EDGE * ROWS, EDGE * ROWS)
        value = swap_halves(act[part, :], core)
        act[part, :] = value
        hidden = jnp.where(inside, value * sigmoid(value), 0.0)
        store(hs, i * EDGE * ROWS, EDGE * ROWS, hidden.astype(BF).astype(F32))
    for dl in range(3):
        for i in range(EDGE):
            rows = load(hs, i * EDGE * ROWS + dl, EDGE * OUT_ROWS, 2)
            rows = rows.astype(BF).reshape(EDGE, OUT_ROWS, C)
            hsel[dl, i + 1, 1:] = rows
            hsend[dl, i + 1, 1:] = rows[..., HALF:]


def conv1(core, x3a, x3b, mine, recv):
    return call(
        conv1_kernel, "conv1",
        (
            shape((ACT_ROWS, C), F32),
            shape((3, 7, 7, OUT_ROWS, C), BF),
            shape((3, 7, 7, OUT_ROWS, HALF), BF),
        ),
        [SM, VM, VM, ANY, ANY],
        WEIGHTS + [pltpu.VMEM((2, ACT_ROWS + 8, HALF), F32)],
        24, 4_000_000_000, 10_000_000,
    )(core, x3a, x3b, mine, recv)


def strided_window(hsel, dl, di, dj, lanes=slice(None)):
    blocks = [
        hsel[dl, 2 * qi + di, 2 * qj + dj, :, lanes] for qi in range(OUTER) for qj in range(OUTER)
    ]
    return jnp.concatenate(blocks, axis=0)


def conv2_kernel(skip, cot, hsel, mine, recv, block_out, grad_pre, grad_pre_t, weights, sems, bo):
    copies = fetch_weights(mine, recv, TAPS, weights, sems)
    pre = skip[...]
    for di in range(3):
        copies[2 * di].wait()
        copies[2 * di + 1].wait()
        for dj in range(3):
            for dl in range(3):
                pre = pre + dot(
                    strided_window(hsel, dl, di, dj), weight(weights, di * 9 + dj * 3 + dl)
                )
    sigma = sigmoid(pre)
    store(bo, 0, PRE_ROWS, pre * sigma)
    for qi in range(OUTER):
        for qj in range(OUTER):
            for ql in range(OUTER):
                base = (qi * 3 + qj) * OUT_ROWS + ql
                block_out[qi, qj, ql] = load(bo, base, SAMP, 4).astype(BF)
    grad = (cot[...] * (sigma * (1.0 + pre * (1.0 - sigma)))).astype(BF)
    grad_pre[...] = grad
    grad_pre_t[...] = grad.astype(F32).T.astype(BF)


def conv2(skip, cot, hsel, mine, recv):
    return call(
        conv2_kernel, "conv2",
        (
            shape((OUTER, OUTER, OUTER, SAMP, C), BF),
            shape((PRE_ROWS, C), BF),
            shape((C, PRE_ROWS), BF),
        ),
        [VM, VM, VM, ANY, ANY],
        WEIGHTS + [pltpu.VMEM((2, PRE_ROWS, HALF), F32)],
        16, 1_500_000_000, 6_000_000,
    )(skip, cot, hsel, mine, recv)


def back_kernel(core_ref, act, grad_pre, mine, recv, gat, weights, sems, y, gh):
    core = core_ref[0]
    copies = fetch_weights(mine, recv, TAPS, weights, sems)
    y[...] = jnp.zeros_like(y)
    grad = grad_pre[...]
    for di in range(3):
        copies[2 * di].wait()
        copies[2 * di + 1].wait()
        for dj in range(3):
            for dl in range(3):
                term = dot_t(grad, weight(weights, di * 9 + dj * 3 + dl))
                term = term.reshape(9, OUT_ROWS, C)
                for qi in range(OUTER):
                    for qj in range(OUTER):
                        y[dl, 2 * qi + di, 2 * qj + dj] += term[qi * 3 + qj]
    store(gh, ACT_ROWS, 8, jnp.zeros((8, C), F32))
    count = EDGE * OUT_ROWS
    for i in range(EDGE):
        base = i * EDGE * ROWS
        store(gh, base, count, y[0, i + 1, 1:].reshape(count, C), 2)
        store(gh, base + 1, count, y[1, i + 1, 1:].reshape(count, C), 2)
    for i in range(EDGE):
        base = i * EDGE * ROWS + 2
        total = load(gh, base, count, 2) + y[2, i + 1, 1:].reshape(count, C)
        store(gh, base, count, total, 2)
    inside = cell_mask()
    for i in range(EDGE):
        value = act[pl.ds(i * EDGE * ROWS, EDGE * ROWS), :]
        sigma = sigmoid(value)
        part = load(gh, i * EDGE * ROWS, EDGE * ROWS) * (sigma * (1.0 + value * (1.0 - sigma)))
        part = swap_halves(jnp.where(inside, part, 0.0), core)
        store(gh, i * EDGE * ROWS, EDGE * ROWS, part)
    for n in range(ACT_ROWS // HALF):
        gat[:, n * HALF : (n + 1) * HALF] = load(gh, n * HALF, HALF).T.astype(BF)


def back(core, act, grad_pre, mine, recv):
    return call(
        back_kernel, "back", shape((C, ACT_ROWS), BF),
        [SM, VM, VM, ANY, ANY],
        WEIGHTS
        + [
            pltpu.VMEM((3, 7, 7, OUT_ROWS, C), F32),
            pltpu.VMEM((2, ACT_ROWS + 8, HALF), F32),
        ],
        18, 1_500_000_000, 8_000_000,
    )(core, act, grad_pre, mine, recv)


def grad_loop(out, lefts, windows):
    eye = (
        lax.broadcasted_iota(jnp.int32, (C, C), 0) == lax.broadcasted_iota(jnp.int32, (C, C), 1)
    ).astype(BF)

    def product(taps):
        total = None
        for left, window in zip(lefts, windows):
            right = jnp.concatenate([window(t // 9, t // 3 % 3, t % 3) for t in taps], axis=1)
            term = dot(left[...], right)
            total = term if total is None else total + term
        width = HALF * len(taps)
        turned = dot_t(eye[:width, :width], total.astype(BF)).astype(BF)
        for n, t in enumerate(taps):
            out[:, t] = turned[n * HALF : (n + 1) * HALF].reshape(4, ROWS, C)

    def step(n, carry):
        product((2 * n, 2 * n + 1))
        return carry

    lax.fori_loop(0, TAPS // 2, step, 0)
    product((TAPS - 1,))


def grad2_kernel(grad_t, grad_t_other, hsel, hsel_other, out):
    grad_loop(
        out,
        (grad_t, grad_t_other),
        (
            lambda di, dj, dl: strided_window(hsel, dl, di, dj, slice(0, HALF)),
            lambda di, dj, dl: strided_window(hsel_other, dl, di, dj),
        ),
    )


def grad2(grad_t, grad_t_other, hsel, hsel_other):
    return call(
        grad2_kernel, "grad2", shape((4, TAPS, ROWS, C), BF), [VM] * 4, [],
        8, 1_000_000_000, 4_000_000,
    )(grad_t, grad_t_other, hsel, hsel_other)


def same_window(x3):
    def window(di, dj, dl):
        return x3[dl, pl.ds(di, EDGE), pl.ds(dj, EDGE)].reshape(ACT_ROWS, HALF)

    return window


def grad1_kernel(gat, gat_other, x3a, x3o, out):
    grad_loop(out, (gat, gat_other), (same_window(x3a), same_window(x3o)))


def grad1(gat, gat_other, x3a, x3o):
    return call(
        grad1_kernel, "grad1", shape((4, TAPS, ROWS, C), BF), [VM] * 4, [],
        12, 4_000_000_000, 7_000_000,
    )(gat, gat_other, x3a, x3o)


def pack_kernel(first, second, order, out, flat):
    perm = one_hot(order[...])
    for i in range(2):
        lanes = slice(i * C, (i + 1) * C)
        flat[:TAPS, lanes] = dot(first[:, lanes].astype(BF), perm)
        flat[TAPS:, lanes] = second[:, lanes].astype(BF).astype(F32)
    shard = flat[...].astype(BF)
    for n in range(16):
        out[n] = shard


def pack(first, second, order):
    return call(
        pack_kernel, "pack", shape((16, 2 * TAPS, 2 * C), BF), [VM] * 3,
        [pltpu.VMEM((2 * TAPS, 2 * C), F32)], 4, 10_000_000, 1_000_000,
    )(first, second, order)


def spread_kernel(shards, out, wide):
    for m in range(16):
        rows = shards[m].astype(F32)
        for i in range(2):
            store(wide, 2 * m + i, 2 * TAPS, rows[:, i * C : (i + 1) * C], ROWS)

    def step(t, carry):
        value = load(wide, pl.multiple_of(t * ROWS, ROWS), ROWS).astype(BF)
        for n in range(4):
            out[n, t] = value
        return carry

    lax.fori_loop(0, 2 * TAPS, step, 0)


def spread(shards):
    return call(
        spread_kernel, "spread", shape((4, 2 * TAPS, ROWS, C), BF), [VM],
        [pltpu.VMEM((2, 2 * TAPS * ROWS, HALF), F32)], 10, 1_000_000, 5_000_000,
    )(shards)


def collect_kernel(parts, out, wide):
    def step(t, carry):
        total = parts[0, t].astype(F32)
        for n in range(1, 4):
            total = total + parts[n, t].astype(F32)
        store(wide, pl.multiple_of(t * ROWS, ROWS), ROWS, total)
        return carry

    lax.fori_loop(0, TAPS, step, 0)
    for m in range(16):
        for i in range(2):
            rows = load(wide, 2 * m + i, TAPS, ROWS)
            out[m, :, i * C : (i + 1) * C] = rows.astype(BF)


def collect(parts):
    return call(
        collect_kernel, "collect", shape((16, TAPS, 2 * C), BF), [VM],
        [pltpu.VMEM((2, TAPS * ROWS, HALF), F32)], 6, 1_000_000, 3_000_000,
    )(parts)


def adam_update(weight, first, second, grad):
    first_new = 0.9 * first + 0.1 * grad
    second_new = 0.999 * second + 0.001 * grad * grad
    fix_first = 1.0 - 0.9**10
    fix_second = 1.0 - 0.999**10
    weight_new = weight - 0.05 * (first_new / fix_first) / (
        jnp.sqrt(second_new / fix_second) + 1e-08
    )
    return (weight_new, first_new, second_new)


def adam_kernel(scale, turn_back, parts, order, k, m, v, kn, mn, vn):
    total = parts[0].astype(F32)
    for n in range(1, 16):
        total = total + parts[n].astype(F32)
    total = total * scale
    back = one_hot(order[...]).astype(F32)
    for i in range(2):
        lanes = slice(i * C, (i + 1) * C)
        grad = total[:, lanes]
        if turn_back:
            grad = lax.dot_general(
                grad,
                back,
                (((1,), (1,)), ((), ())),
                precision=lax.Precision.HIGHEST,
                preferred_element_type=F32,
            )
        kn[:, lanes], mn[:, lanes], vn[:, lanes] = adam_update(
            k[:, lanes], m[:, lanes], v[:, lanes], grad
        )


def adam(scale, turn_back, parts, order, *state):
    return call(
        functools.partial(adam_kernel, scale, turn_back), "adam",
        (shape((TAPS, 2 * C), F32),) * 3, [VM] * 5, [], 6, 10_000_000, 1_000_000,
    )(parts, order, *state)


def place(x, y, z, c):
    return ((x * 4 + y) * 4 + z) * 2 + c


def channel_orders():
    orders = []
    for c in range(2):
        order = []
        for a, b, d in itertools.product(range(4), repeat=3):
            x, y, z = (b, d, a) if c == 0 else (a, b, d)
            order += [2 * place(x, y, z, c), 2 * place(x, y, z, c) + 1]
        orders.append(order)
    zero, one = orders
    return np.array([zero + one, one + zero], np.int32).reshape(2, 1, C)


def lines(c, axes):
    rest = [a for a in "xyz" if a not in axes]
    groups = []
    for fixed in itertools.product(range(4), repeat=len(rest)):
        group = []
        for moving in itertools.product(range(4), repeat=len(axes)):
            at = dict(zip(rest, fixed)) | dict(zip(axes, moving))
            group.append(place(at["x"], at["y"], at["z"], c))
        groups.append(group)
    return groups


ORDERS = channel_orders()
PLANES = lines(0, "xy") + lines(1, "yz")
LINES = lines(0, "z") + lines(1, "x")
PARTNERS = [(n, n ^ 1) for n in range(128)]


def exchange(value, groups):
    return lax.all_to_all(value, "dp", 0, 0, axis_index_groups=groups, tiled=True)


def swap(value):
    return lax.ppermute(value, "dp", PARTNERS)


def body(latent, out_grad, k1, m1, v1, k2, m2, v2):
    scale = 1.0 / (latent.shape[0] * lax.axis_size("dp"))
    core = lax.axis_index("dp") % 2
    orders = jnp.asarray(ORDERS)
    fixed = orders[0]
    own = jnp.where(core == 0, orders[0], orders[1])
    core = core.reshape(1)

    shards = pack(k1, k2, fixed)
    latent = latent.transpose(1, 2, 3, 0, 4)
    cells = prep(latent, swap(latent), out_grad.transpose(1, 2, 3, 0, 4), own)
    shards, cells = lax.optimization_barrier((exchange(shards, PLANES), cells))
    x3a, x3b, x3o, skip, cot = cells
    mine = exchange(spread(shards), LINES)
    recv = swap(mine)

    act, hsel, hsend = conv1(core, x3a, x3b, mine, recv)
    hsel_other = swap(hsend)
    block_out, grad_pre, grad_pre_t = conv2(skip, cot, hsel, mine, recv)
    grad_pre_t_other = swap(grad_pre_t)
    gat = back(core, act, grad_pre, mine, recv)
    gat_other = swap(gat)
    parts2 = exchange(grad2(grad_pre_t, grad_pre_t_other, hsel, hsel_other), LINES)
    parts1 = exchange(grad1(gat, gat_other, x3a, x3o), LINES)
    new_two = adam(scale, False, exchange(collect(parts2), PLANES), fixed, k2, m2, v2)
    new_one = adam(scale, True, exchange(collect(parts1), PLANES), fixed, k1, m1, v1)
    return (block_out.transpose(3, 0, 1, 2, 4), *new_one, *new_two)


def solution(mesh):
    wide = P("dp", None, None, None, None)
    flat = P(None, "dp")
    return jax.shard_map(
        body,
        mesh=mesh,
        in_specs=(wide, wide) + (flat,) * 6,
        out_specs=(wide,) + (flat,) * 6,
        check_vma=False,
    )
```

```python
import functools
import itertools

import jax
import jax.numpy as jnp
import numpy as np
from jax import lax
from jax.experimental import pallas as pl
from jax.experimental.pallas import tpu as pltpu
from jax.sharding import PartitionSpec as P

C = 256
HALF = 128
EDGE = 6
OUTER = 3
TAPS = 27
SAMP = 4
ROWS = 32
ACT_ROWS = EDGE * EDGE * ROWS
PAD_ROWS = 64 * ROWS
OUT_ROWS = 16
PRE_ROWS = 9 * OUT_ROWS
MIB = 1024 * 1024
BF = jnp.bfloat16
F32 = jnp.float32

MEMBERS = 8
BLOCK = 16

VM = pl.BlockSpec(memory_space=pltpu.VMEM)
SM = pl.BlockSpec(memory_space=pltpu.SMEM)
ANY = pl.BlockSpec(memory_space=pl.ANY)


def shape(dims, dtype):
    return jax.ShapeDtypeStruct(dims, dtype)


def call(kernel, name, out_shape, in_specs, scratch, mib, flops, moved):
    single = not isinstance(out_shape, tuple)
    return pl.pallas_call(
        kernel,
        out_shape=out_shape,
        in_specs=in_specs,
        out_specs=VM if single else (VM,) * len(out_shape),
        scratch_shapes=scratch,
        compiler_params=pltpu.CompilerParams(vmem_limit_bytes=mib * MIB),
        cost_estimate=pl.CostEstimate(flops=flops, bytes_accessed=moved, transcendentals=0),
        name=name,
    )


def dot(a, b):
    return jnp.dot(a, b, preferred_element_type=F32)


def dot_t(a, b):
    return lax.dot_general(a, b, (((1,), (1,)), ((), ())), preferred_element_type=F32)


def sigmoid(v):
    return 1.0 / (1.0 + jnp.exp(-v))


def load(ref, start, count, stride=1):
    return jnp.concatenate(
        [ref[half, pl.ds(start, count, stride=stride), :] for half in range(2)], axis=1
    )


def store(ref, start, count, value, stride=1):
    for half in range(2):
        ref[half, pl.ds(start, count, stride=stride), :] = value[
            :, half * HALF : (half + 1) * HALF
        ]


def one_hot(order_row):
    return (lax.broadcasted_iota(jnp.int32, (C, C), 0) == order_row).astype(BF)


def fill_cells(source, xs):
    for i in range(EDGE):
        for j in range(EDGE):
            value = source[i, j].astype(F32)
            base = 8 + ((i + 1) * 8 + j + 1) * ROWS + 1
            for l in range(EDGE):
                store(xs, base + l, SAMP, value[l], 8)


def prep_kernel(latent, other, out_grad, order, x3a, x3b, x3o, skip, cot, xs, og):
    perm = one_hot(order[...])
    xs[...] = jnp.zeros_like(xs)
    og[...] = jnp.zeros_like(og)
    fill_cells(latent, xs)
    for qi in range(OUTER):
        for qj in range(OUTER):
            q = (qi * 3 + qj) * OUT_ROWS
            value = out_grad[qi, qj].astype(F32)
            for ql in range(OUTER):
                store(og, q + ql, SAMP, value[ql], 4)
            base = 8 + ((2 * qi + 1) * 8 + 2 * qj + 1) * ROWS + 1
            skip[q : q + OUT_ROWS, :] = load(xs, base, OUT_ROWS, 2)
    cot[...] = load(og, 0, PRE_ROWS)
    for i in range(8):
        for dl in range(3):
            rows = dot(load(xs, 7 + dl + i * 256, 256).astype(BF), perm).astype(BF)
            x3a[dl, i] = rows[:, :HALF].reshape(8, ROWS, HALF)
            x3b[dl, i] = rows[:, HALF:].reshape(8, ROWS, HALF)
    fill_cells(other, xs)
    for i in range(8):
        for dl in range(3):
            rows = dot(load(xs, 7 + dl + i * 256, 256).astype(BF), perm[:, :HALF])
            x3o[dl, i] = rows.astype(BF).reshape(8, ROWS, HALF)


def prep(latent, other, out_grad, order):
    wide = shape((3, 8, 8, ROWS, HALF), BF)
    pre = shape((PRE_ROWS, C), F32)
    return call(
        prep_kernel, "prep", (wide, wide, wide, pre, pre), [VM] * 4,
        [pltpu.VMEM((2, PAD_ROWS + 16, HALF), F32), pltpu.VMEM((2, PRE_ROWS, HALF), F32)],
        20, 2_000_000_000, 8_000_000,
    )(latent, other, out_grad, order)


def swap_halves(value, core):
    swapped = jnp.concatenate([value[:, HALF:], value[:, :HALF]], axis=1)
    return jnp.where(core == 1, swapped, value)


def cell_mask():
    cell = lax.broadcasted_iota(jnp.int32, (EDGE * ROWS, C), 0) % 8
    return (cell >= 1) & (cell <= EDGE)


def fetch_weights(source, first, weights, sems):
    copies = []
    for di in range(3):
        copies.append(
            pltpu.make_async_copy(
                source.at[:, pl.ds(first + 9 * di, 9)],
                weights.at[:, pl.ds(9 * di, 9)],
                sems.at[di],
            )
        )
        copies[-1].start()
    return copies


def half_weight(weights, t):
    return weights[:, t].reshape(HALF, C)


HALF_WEIGHTS = [pltpu.VMEM((MEMBERS, TAPS, BLOCK, C), BF), pltpu.SemaphoreType.DMA((3,))]
WEIGHTS = HALF_WEIGHTS + HALF_WEIGHTS


def half_conv(x3, weights, copies, act, start):
    for di in range(3):
        copies[di].wait()
        taps = range(9 * di, 9 * di + 9)
        windows = [
            x3[t % 3, di : di + EDGE, t // 3 % 3 : t // 3 % 3 + EDGE].reshape(ACT_ROWS, HALF)
            for t in taps
        ]
        total = dot(
            jnp.concatenate(windows, axis=1),
            jnp.concatenate([half_weight(weights, t) for t in taps], axis=0),
        )
        act[...] = (start if di == 0 else act)[...] + total if start is not None or di else total


def conv1_own_kernel(x3a, mine, act, weights, sems):
    half_conv(x3a, weights, fetch_weights(mine, 0, weights, sems), act, None)


def conv1_own(x3a, mine):
    return call(
        conv1_own_kernel, "conv1_own", shape((ACT_ROWS, C), F32), [VM, ANY], HALF_WEIGHTS,
        12, 2_000_000_000, 5_000_000,
    )(x3a, mine)


def conv1_kernel(core_ref, x3b, recv, part_act, act, hsel, hsend, weights, sems, hs):
    core = core_ref[0]
    half_conv(x3b, weights, fetch_weights(recv, 0, weights, sems), act, part_act)

    hsel[:, 0] = jnp.zeros_like(hsel[:, 0])
    hsel[:, :, 0] = jnp.zeros_like(hsel[:, :, 0])
    hsend[:, 0] = jnp.zeros_like(hsend[:, 0])
    hsend[:, :, 0] = jnp.zeros_like(hsend[:, :, 0])
    store(hs, ACT_ROWS, 8, jnp.zeros((8, C), F32))
    inside = cell_mask()
    for i in range(EDGE):
        part = pl.ds(i * EDGE * ROWS, EDGE * ROWS)
        value = swap_halves(act[part, :], core)
        act[part, :] = value
        hidden = jnp.where(inside, value * sigmoid(value), 0.0)
        store(hs, i * EDGE * ROWS, EDGE * ROWS, hidden.astype(BF).astype(F32))
    for dl in range(3):
        for i in range(EDGE):
            rows = load(hs, i * EDGE * ROWS + dl, EDGE * OUT_ROWS, 2)
            rows = rows.astype(BF).reshape(EDGE, OUT_ROWS, C)
            hsel[dl, i + 1, 1:] = rows
            hsend[dl, i + 1, 1:] = rows[..., HALF:]


def conv1(core, x3b, recv, part_act):
    return call(
        conv1_kernel, "conv1",
        (
            shape((ACT_ROWS, C), F32),
            shape((3, 7, 7, OUT_ROWS, C), BF),
            shape((3, 7, 7, OUT_ROWS, HALF), BF),
        ),
        [SM, VM, ANY, VM],
        HALF_WEIGHTS + [pltpu.VMEM((2, ACT_ROWS + 8, HALF), F32)],
        24, 2_000_000_000, 7_000_000,
    )(core, x3b, recv, part_act)


def weight(wa, wb, t):
    return jnp.concatenate([half_weight(wa, t), half_weight(wb, t)], axis=0)


def strided_window(hsel, dl, di, dj, lanes=slice(None)):
    blocks = [
        hsel[dl, 2 * qi + di, 2 * qj + dj, :, lanes] for qi in range(OUTER) for qj in range(OUTER)
    ]
    return jnp.concatenate(blocks, axis=0)


def conv2_kernel(skip, cot, hsel, mine, recv, block_out, grad_pre, grad_pre_t, wa, sa, wb, sb, bo):
    halves = (fetch_weights(mine, TAPS, wa, sa), fetch_weights(recv, TAPS, wb, sb))
    pre = skip[...]
    for di in range(3):
        for copies in halves:
            copies[di].wait()
        for dj in range(3):
            for dl in range(3):
                pre = pre + dot(
                    strided_window(hsel, dl, di, dj), weight(wa, wb, di * 9 + dj * 3 + dl)
                )
    sigma = sigmoid(pre)
    store(bo, 0, PRE_ROWS, pre * sigma)
    for qi in range(OUTER):
        for qj in range(OUTER):
            for ql in range(OUTER):
                base = (qi * 3 + qj) * OUT_ROWS + ql
                block_out[qi, qj, ql] = load(bo, base, SAMP, 4).astype(BF)
    grad = (cot[...] * (sigma * (1.0 + pre * (1.0 - sigma)))).astype(BF)
    grad_pre[...] = grad
    grad_pre_t[...] = grad.astype(F32).T.astype(BF)


def conv2(skip, cot, hsel, mine, recv):
    return call(
        conv2_kernel, "conv2",
        (
            shape((OUTER, OUTER, OUTER, SAMP, C), BF),
            shape((PRE_ROWS, C), BF),
            shape((C, PRE_ROWS), BF),
        ),
        [VM, VM, VM, ANY, ANY],
        WEIGHTS + [pltpu.VMEM((2, PRE_ROWS, HALF), F32)],
        16, 1_500_000_000, 6_000_000,
    )(skip, cot, hsel, mine, recv)


def back_kernel(core_ref, act, grad_pre, mine, recv, gat, wa, sa, wb, sb, y, gh):
    core = core_ref[0]
    halves = (fetch_weights(mine, TAPS, wa, sa), fetch_weights(recv, TAPS, wb, sb))
    y[...] = jnp.zeros_like(y)
    grad = grad_pre[...]
    for di in range(3):
        for copies in halves:
            copies[di].wait()
        for dj in range(3):
            for dl in range(3):
                term = dot_t(grad, weight(wa, wb, di * 9 + dj * 3 + dl))
                term = term.reshape(9, OUT_ROWS, C)
                for qi in range(OUTER):
                    for qj in range(OUTER):
                        y[dl, 2 * qi + di, 2 * qj + dj] += term[qi * 3 + qj]
    store(gh, ACT_ROWS, 8, jnp.zeros((8, C), F32))
    count = EDGE * OUT_ROWS
    for i in range(EDGE):
        base = i * EDGE * ROWS
        store(gh, base, count, y[0, i + 1, 1:].reshape(count, C), 2)
        store(gh, base + 1, count, y[1, i + 1, 1:].reshape(count, C), 2)
    for i in range(EDGE):
        base = i * EDGE * ROWS + 2
        total = load(gh, base, count, 2) + y[2, i + 1, 1:].reshape(count, C)
        store(gh, base, count, total, 2)
    inside = cell_mask()
    for i in range(EDGE):
        value = act[pl.ds(i * EDGE * ROWS, EDGE * ROWS), :]
        sigma = sigmoid(value)
        part = load(gh, i * EDGE * ROWS, EDGE * ROWS) * (sigma * (1.0 + value * (1.0 - sigma)))
        part = swap_halves(jnp.where(inside, part, 0.0), core)
        store(gh, i * EDGE * ROWS, EDGE * ROWS, part)
    for n in range(ACT_ROWS // HALF):
        gat[:, n * HALF : (n + 1) * HALF] = load(gh, n * HALF, HALF).T.astype(BF)


def back(core, act, grad_pre, mine, recv):
    return call(
        back_kernel, "back", shape((C, ACT_ROWS), BF),
        [SM, VM, VM, ANY, ANY],
        WEIGHTS
        + [
            pltpu.VMEM((3, 7, 7, OUT_ROWS, C), F32),
            pltpu.VMEM((2, ACT_ROWS + 8, HALF), F32),
        ],
        18, 1_500_000_000, 8_000_000,
    )(core, act, grad_pre, mine, recv)


def grad_loop(out, lefts, windows, unroll):
    eye = (
        lax.broadcasted_iota(jnp.int32, (C, C), 0) == lax.broadcasted_iota(jnp.int32, (C, C), 1)
    ).astype(BF)

    def product(taps):
        total = None
        for left, window in zip(lefts, windows):
            right = jnp.concatenate([window(t // 9, t // 3 % 3, t % 3) for t in taps], axis=1)
            term = dot(left[...], right)
            total = term if total is None else total + term
        width = HALF * len(taps)
        turned = dot_t(eye[:width, :width], total.astype(BF)).astype(BF)
        for n, t in enumerate(taps):
            out[:, t] = turned[n * HALF : (n + 1) * HALF].reshape(MEMBERS, BLOCK, C)

    def step(n, carry):
        for k in range(0, unroll, 2):
            product((unroll * n + k, unroll * n + k + 1))
        return carry

    whole = TAPS // unroll
    if whole > 1:
        lax.fori_loop(0, whole, step, 0)
    for t in range(unroll * whole if whole > 1 else 0, TAPS, 2):
        product(tuple(range(t, min(t + 2, TAPS))))


def grad2_kernel(grad_t, grad_t_other, hsel, hsel_other, out):
    grad_loop(
        out,
        (grad_t, grad_t_other),
        (
            lambda di, dj, dl: strided_window(hsel, dl, di, dj, slice(0, HALF)),
            lambda di, dj, dl: strided_window(hsel_other, dl, di, dj),
        ),
        TAPS,
    )


def grad2(grad_t, grad_t_other, hsel, hsel_other):
    return call(
        grad2_kernel, "grad2", shape((MEMBERS, TAPS, BLOCK, C), BF), [VM] * 4, [],
        8, 1_000_000_000, 4_000_000,
    )(grad_t, grad_t_other, hsel, hsel_other)


def same_window(x3):
    def window(di, dj, dl):
        return x3[dl, pl.ds(di, EDGE), pl.ds(dj, EDGE)].reshape(ACT_ROWS, HALF)

    return window


def grad1_kernel(gat, gat_other, x3a, x3o, out):
    grad_loop(out, (gat, gat_other), (same_window(x3a), same_window(x3o)), 2)


def grad1(gat, gat_other, x3a, x3o):
    return call(
        grad1_kernel, "grad1", shape((MEMBERS, TAPS, BLOCK, C), BF), [VM] * 4, [],
        12, 4_000_000_000, 7_000_000,
    )(gat, gat_other, x3a, x3o)


def pack_kernel(first, second, order, out):
    perm = one_hot(order[...])
    for i in range(2):
        lanes = slice(i * C, (i + 1) * C)
        one = dot(first[:, lanes].astype(BF), perm).astype(BF)
        two = second[:, lanes].astype(BF)
        for n in range(MEMBERS):
            out[n, 0, :, lanes] = one
            out[n, 1, :, lanes] = two


def pack(first, second, order):
    return call(
        pack_kernel, "pack", shape((MEMBERS, 2, TAPS, 2 * C), BF), [VM] * 3,
        [], 56, 10_000_000, 1_000_000,
    )(first, second, order)


def spread_kernel(shards, out, wide):
    for m in range(MEMBERS):
        for k in range(2):
            rows = shards[m, k].astype(F32)
            for i in range(2):
                start = k * TAPS * BLOCK + 2 * m + i
                store(wide, start, TAPS, rows[:, i * C : (i + 1) * C], BLOCK)

    def step(t, carry):
        value = load(wide, pl.multiple_of(t * BLOCK, BLOCK), BLOCK).astype(BF)
        for n in range(MEMBERS):
            out[n, t] = value
        return carry

    lax.fori_loop(0, 2 * TAPS, step, 0)


def spread(shards):
    return call(
        spread_kernel, "spread", shape((MEMBERS, 2 * TAPS, BLOCK, C), BF), [VM],
        [pltpu.VMEM((2, 2 * TAPS * BLOCK, HALF), F32)], 10, 1_000_000, 5_000_000,
    )(shards)


def collect_one(parts, wide, write):
    def step(t, carry):
        total = parts[0, t].astype(F32)
        for n in range(1, MEMBERS):
            total = total + parts[n, t].astype(F32)
        store(wide, pl.multiple_of(t * BLOCK, BLOCK), BLOCK, total)
        return carry

    lax.fori_loop(0, TAPS, step, 0)
    for m in range(MEMBERS):
        for i in range(2):
            rows = load(wide, 2 * m + i, TAPS, BLOCK).astype(BF)
            write(m, slice(i * C, (i + 1) * C), rows)


def collect2_kernel(parts, out, wide):
    def write(m, lanes, rows):
        out[m, :, lanes] = rows

    collect_one(parts, wide, write)


def collect2(parts):
    return call(
        collect2_kernel, "collect2", shape((MEMBERS, TAPS, 2 * C), BF), [VM],
        [pltpu.VMEM((2, TAPS * BLOCK, HALF), F32)], 6, 1_000_000, 3_000_000,
    )(parts)


def collect_kernel(parts, second, out, wide):
    def write(m, lanes, rows):
        out[m, 0, :, lanes] = rows

    for m in range(MEMBERS):
        out[m, 1] = second[m]
    collect_one(parts, wide, write)


def collect(parts, second):
    return call(
        collect_kernel, "collect", shape((MEMBERS, 2, TAPS, 2 * C), BF), [VM] * 2,
        [pltpu.VMEM((2, TAPS * BLOCK, HALF), F32)], 8, 1_000_000, 3_000_000,
    )(parts, second)


def adam_update(weight, first, second, grad):
    first_new = 0.9 * first + 0.1 * grad
    second_new = 0.999 * second + 0.001 * grad * grad
    fix_first = 1.0 - 0.9**10
    fix_second = 1.0 - 0.999**10
    weight_new = weight - 0.05 * (first_new / fix_first) / (
        jnp.sqrt(second_new / fix_second) + 1e-08
    )
    return (weight_new, first_new, second_new)


def adam_kernel(
    scale, parts, order, k1, m1, v1, k2, m2, v2, k1n, m1n, v1n, k2n, m2n, v2n
):
    back = one_hot(order[...]).astype(F32)
    state = ((k1, m1, v1, k1n, m1n, v1n), (k2, m2, v2, k2n, m2n, v2n))
    for i in range(2):
        lanes = slice(i * C, (i + 1) * C)
        for which, (k, m, v, kn, mn, vn) in enumerate(state):
            grad = parts[0, which, :, lanes].astype(F32)
            for n in range(1, MEMBERS):
                grad = grad + parts[n, which, :, lanes].astype(F32)
            grad = grad * scale
            if which == 0:
                grad = lax.dot_general(
                    grad,
                    back,
                    (((1,), (1,)), ((), ())),
                    precision=lax.Precision.HIGHEST,
                    preferred_element_type=F32,
                )
            kn[:, lanes], mn[:, lanes], vn[:, lanes] = adam_update(
                k[:, lanes], m[:, lanes], v[:, lanes], grad
            )


def adam(scale, parts, order, *state):
    return call(
        functools.partial(adam_kernel, scale), "adam",
        (shape((TAPS, 2 * C), F32),) * 6, [VM] * 8, [], 6, 10_000_000, 1_000_000,
    )(parts, order, *state)


def place(x, y, z, c):
    return ((x * 4 + y) * 4 + z) * 2 + c


LINE = [[0, 1, 2, 3]]
ONE = [[0], [1], [2], [3]]
EVEN_PAIRS = [[0, 1], [2, 3]]
ODD_PAIRS = [[1, 2], [3, 0]]
FAR_PAIRS = [[0, 2], [1, 3]]


def groups(c, xs, ys, zs):
    return [
        [place(x, y, z, c) for x in gx for y in gy for z in gz]
        for gx, gy, gz in itertools.product(xs, ys, zs)
    ]


NEAR = groups(0, LINE, EVEN_PAIRS, ONE) + groups(1, ONE, ODD_PAIRS, LINE)
FAR = groups(0, ONE, FAR_PAIRS, LINE) + groups(1, LINE, FAR_PAIRS, ONE)
PARTNERS = [(n, n ^ 1) for n in range(128)]


def channel_orders():
    orders = []
    for c in range(2):
        near = next(group for group in NEAR if group[0] % 2 == c)
        order = []
        for member in near:
            far = next(group for group in FAR if member in group)
            order += [2 * device + i for device in far for i in range(2)]
        orders.append(order)
    zero, one = orders
    return np.array([zero + one, one + zero], np.int32).reshape(2, 1, C)


ORDERS = channel_orders()


def exchange(value, groups):
    return lax.all_to_all(value, "dp", 0, 0, axis_index_groups=groups, tiled=True)


def swap(value):
    return lax.ppermute(value, "dp", PARTNERS)


def body(latent, out_grad, k1, m1, v1, k2, m2, v2):
    scale = 1.0 / (latent.shape[0] * lax.axis_size("dp"))
    core = lax.axis_index("dp") % 2
    orders = jnp.asarray(ORDERS)
    fixed = orders[0]
    own = jnp.where(core == 0, orders[0], orders[1])
    core = core.reshape(1)

    shards = pack(k1, k2, fixed)
    latent = latent.transpose(1, 2, 3, 0, 4)
    cells = prep(latent, swap(latent), out_grad.transpose(1, 2, 3, 0, 4), own)
    shards, cells = lax.optimization_barrier((exchange(shards, FAR), cells))
    x3a, x3b, x3o, skip, cot = cells
    mine = exchange(spread(shards), NEAR)
    recv = swap(mine)

    act, hsel, hsend = conv1(core, x3b, recv, conv1_own(x3a, mine))
    hsel_other = swap(hsend)
    block_out, grad_pre, grad_pre_t = conv2(skip, cot, hsel, mine, recv)
    second = grad2(grad_pre_t, swap(grad_pre_t), hsel, hsel_other)
    second, grad_pre = lax.optimization_barrier((second, grad_pre))
    parts2 = exchange(second, NEAR)
    gat = back(core, act, grad_pre, mine, recv)
    parts1 = exchange(grad1(gat, swap(gat), x3a, x3o), NEAR)
    parts = exchange(collect(parts1, collect2(parts2)), FAR)
    new = adam(scale, parts, fixed, k1, m1, v1, k2, m2, v2)
    return (block_out.transpose(3, 0, 1, 2, 4), *new)


def solution(mesh):
    wide = P("dp", None, None, None, None)
    flat = P(None, "dp")
    return jax.shard_map(
        body,
        mesh=mesh,
        in_specs=(wide, wide) + (flat,) * 6,
        out_specs=(wide,) + (flat,) * 6,
        check_vma=False,
    )
```

```python
import functools
import itertools

import jax
import jax.numpy as jnp
import numpy as np
from jax import lax
from jax.experimental import pallas as pl
from jax.experimental.pallas import tpu as pltpu
from jax.sharding import PartitionSpec as P

C = 256
HALF = 128
EDGE = 6
OUTER = 3
TAPS = 27
SAMP = 4
ROWS = 32
ACT_ROWS = EDGE * EDGE * ROWS
PAD_ROWS = 64 * ROWS
OUT_ROWS = 16
PRE_ROWS = 9 * OUT_ROWS
MIB = 1024 * 1024
BF = jnp.bfloat16
F32 = jnp.float32

MEMBERS = 8
GROUP = 6
BLOCK = 16

VM = pl.BlockSpec(memory_space=pltpu.VMEM)
SM = pl.BlockSpec(memory_space=pltpu.SMEM)
HB = pl.BlockSpec(memory_space=pltpu.HBM)


def shape(dims, dtype):
    return jax.ShapeDtypeStruct(dims, dtype)


def call(kernel, name, out_shape, in_specs, scratch, mib, flops, moved, out_spec=VM):
    single = not isinstance(out_shape, tuple)
    return pl.pallas_call(
        kernel,
        out_shape=out_shape,
        in_specs=in_specs,
        out_specs=out_spec if single else (out_spec,) * len(out_shape),
        scratch_shapes=scratch,
        compiler_params=pltpu.CompilerParams(vmem_limit_bytes=mib * MIB),
        cost_estimate=pl.CostEstimate(flops=flops, bytes_accessed=moved, transcendentals=0),
        name=name,
    )


def dot(a, b):
    return jnp.dot(a, b, preferred_element_type=F32)


def dot_t(a, b):
    return lax.dot_general(a, b, (((1,), (1,)), ((), ())), preferred_element_type=F32)


def sigmoid(v):
    return 1.0 / (1.0 + jnp.exp(-v))


def load(ref, start, count, stride=1):
    return jnp.concatenate(
        [ref[half, pl.ds(start, count, stride=stride), :] for half in range(2)], axis=1
    )


def store(ref, start, count, value, stride=1):
    for half in range(2):
        ref[half, pl.ds(start, count, stride=stride), :] = value[
            :, half * HALF : (half + 1) * HALF
        ]


def one_hot(order_row):
    return (lax.broadcasted_iota(jnp.int32, (C, C), 0) == order_row).astype(BF)


def fill_cells(source, xs):
    for i in range(EDGE):
        for j in range(EDGE):
            value = source[i, j].astype(F32)
            base = 8 + ((i + 1) * 8 + j + 1) * ROWS + 1
            for l in range(EDGE):
                store(xs, base + l, SAMP, value[l], 8)


def prep_kernel(latent, other, out_grad, order, x3a, x3b, x3o, skip, cot, xs, og):
    perm = one_hot(order[...])
    xs[...] = jnp.zeros_like(xs)
    og[...] = jnp.zeros_like(og)
    fill_cells(latent, xs)
    for qi in range(OUTER):
        for qj in range(OUTER):
            q = (qi * 3 + qj) * OUT_ROWS
            value = out_grad[qi, qj].astype(F32)
            for ql in range(OUTER):
                store(og, q + ql, SAMP, value[ql], 4)
            base = 8 + ((2 * qi + 1) * 8 + 2 * qj + 1) * ROWS + 1
            skip[q : q + OUT_ROWS, :] = load(xs, base, OUT_ROWS, 2)
    cot[...] = load(og, 0, PRE_ROWS)
    for i in range(8):
        for dl in range(3):
            rows = dot(load(xs, 7 + dl + i * 256, 256).astype(BF), perm).astype(BF)
            x3a[dl, i] = rows[:, :HALF].reshape(8, ROWS, HALF)
            x3b[dl, i] = rows[:, HALF:].reshape(8, ROWS, HALF)
    fill_cells(other, xs)
    for i in range(8):
        for dl in range(3):
            rows = dot(load(xs, 7 + dl + i * 256, 256).astype(BF), perm[:, :HALF])
            x3o[dl, i] = rows.astype(BF).reshape(8, ROWS, HALF)


def prep(latent, other, out_grad, order):
    wide = shape((3, 8, 8, ROWS, HALF), BF)
    pre = shape((PRE_ROWS, C), F32)
    return call(
        prep_kernel, "prep", (wide, wide, wide, pre, pre), [VM] * 4,
        [pltpu.VMEM((2, PAD_ROWS + 16, HALF), F32), pltpu.VMEM((2, PRE_ROWS, HALF), F32)],
        56, 2_000_000_000, 8_000_000,
    )(latent, other, out_grad, order)


def swap_halves(value, core):
    swapped = jnp.concatenate([value[:, HALF:], value[:, :HALF]], axis=1)
    return jnp.where(core == 1, swapped, value)


def cell_mask():
    cell = lax.broadcasted_iota(jnp.int32, (EDGE * ROWS, C), 0) % 8
    return (cell >= 1) & (cell <= EDGE)


def fetch_weights(source, first, weights, sems):
    copies = []
    for di in range(3):
        copies.append(
            pltpu.make_async_copy(
                source.at[:, pl.ds(first + 9 * di, 9)],
                weights.at[:, pl.ds(9 * di, 9)],
                sems.at[di],
            )
        )
        copies[-1].start()
    return copies


def half_weight(weights, t):
    return weights[:, t].reshape(HALF, C)


HALF_WEIGHTS = [pltpu.VMEM((MEMBERS, TAPS, BLOCK, C), BF), pltpu.SemaphoreType.DMA((3,))]
WEIGHTS = HALF_WEIGHTS + HALF_WEIGHTS


def half_conv(x3, weights, copies, act, start):
    for first in range(0, TAPS, GROUP):
        taps = range(first, min(first + GROUP, TAPS))
        for di in range(3):
            if first <= 9 * di < first + GROUP or (first, di) == (0, 0):
                copies[di].wait()
        windows = [
            x3[t % 3, t // 9 : t // 9 + EDGE, t // 3 % 3 : t // 3 % 3 + EDGE] for t in taps
        ]
        total = dot(
            jnp.concatenate([window.reshape(ACT_ROWS, HALF) for window in windows], axis=1),
            jnp.concatenate([half_weight(weights, t) for t in taps], axis=0),
        )
        before = act if first else start
        act[...] = total if before is None else before[...] + total


def conv1_own_kernel(x3a, mine, act, weights, sems):
    half_conv(x3a, weights, fetch_weights(mine, 0, weights, sems), act, None)


def conv1_own(x3a, mine):
    return call(
        conv1_own_kernel, "conv1_own", shape((ACT_ROWS, C), F32), [VM, HB], HALF_WEIGHTS,
        12, 2_000_000_000, 5_000_000,
    )(x3a, mine)


def conv1_kernel(core_ref, x3b, recv, part_act, act, hsel, hsend, weights, sems, hs):
    core = core_ref[0]
    half_conv(x3b, weights, fetch_weights(recv, 0, weights, sems), act, part_act)

    hsel[:, 0] = jnp.zeros_like(hsel[:, 0])
    hsel[:, :, 0] = jnp.zeros_like(hsel[:, :, 0])
    hsend[:, 0] = jnp.zeros_like(hsend[:, 0])
    hsend[:, :, 0] = jnp.zeros_like(hsend[:, :, 0])
    store(hs, ACT_ROWS, 8, jnp.zeros((8, C), F32))
    inside = cell_mask()
    for i in range(EDGE):
        part = pl.ds(i * EDGE * ROWS, EDGE * ROWS)
        value = swap_halves(act[part, :], core)
        act[part, :] = value
        hidden = jnp.where(inside, value * sigmoid(value), 0.0)
        store(hs, i * EDGE * ROWS, EDGE * ROWS, hidden.astype(BF).astype(F32))
    for dl in range(3):
        for i in range(EDGE):
            rows = load(hs, i * EDGE * ROWS + dl, EDGE * OUT_ROWS, 2)
            rows = rows.astype(BF).reshape(EDGE, OUT_ROWS, C)
            hsel[dl, i + 1, 1:] = rows
            hsend[dl, i + 1, 1:] = rows[..., HALF:]


def conv1(core, x3b, recv, part_act):
    return call(
        conv1_kernel, "conv1",
        (
            shape((ACT_ROWS, C), F32),
            shape((3, 7, 7, OUT_ROWS, C), BF),
            shape((3, 7, 7, OUT_ROWS, HALF), BF),
        ),
        [SM, VM, HB, VM],
        HALF_WEIGHTS + [pltpu.VMEM((2, ACT_ROWS + 8, HALF), F32)],
        24, 2_000_000_000, 7_000_000,
    )(core, x3b, recv, part_act)


def weight(wa, wb, t):
    return jnp.concatenate([half_weight(wa, t), half_weight(wb, t)], axis=0)


def strided_window(hsel, dl, di, dj, lanes=slice(None)):
    blocks = [
        hsel[dl, 2 * qi + di, 2 * qj + dj, :, lanes] for qi in range(OUTER) for qj in range(OUTER)
    ]
    return jnp.concatenate(blocks, axis=0)


def conv2_kernel(skip, cot, hsel, mine, recv, block_out, grad_pre, grad_pre_t, wa, sa, wb, sb, bo):
    halves = (fetch_weights(mine, TAPS, wa, sa), fetch_weights(recv, TAPS, wb, sb))
    pre = skip[...]
    for di in range(3):
        for copies in halves:
            copies[di].wait()
        for dj in range(3):
            for dl in range(3):
                pre = pre + dot(
                    strided_window(hsel, dl, di, dj), weight(wa, wb, di * 9 + dj * 3 + dl)
                )
    sigma = sigmoid(pre)
    store(bo, 0, PRE_ROWS, pre * sigma)
    for qi in range(OUTER):
        for qj in range(OUTER):
            for ql in range(OUTER):
                base = (qi * 3 + qj) * OUT_ROWS + ql
                block_out[qi, qj, ql] = load(bo, base, SAMP, 4).astype(BF)
    grad = (cot[...] * (sigma * (1.0 + pre * (1.0 - sigma)))).astype(BF)
    grad_pre[...] = grad
    grad_pre_t[...] = grad.astype(F32).T.astype(BF)


def conv2(skip, cot, hsel, mine, recv):
    return call(
        conv2_kernel, "conv2",
        (
            shape((OUTER, OUTER, OUTER, SAMP, C), BF),
            shape((PRE_ROWS, C), BF),
            shape((C, PRE_ROWS), BF),
        ),
        [VM, VM, VM, HB, HB],
        WEIGHTS + [pltpu.VMEM((2, PRE_ROWS, HALF), F32)],
        16, 1_500_000_000, 6_000_000,
    )(skip, cot, hsel, mine, recv)


def back_kernel(
    core_ref, act_far, grad_far, mine, recv, gat, wa, sa, wb, sb, y, gh, act, grad_pre, sems
):
    core = core_ref[0]
    fetch_grad = pltpu.make_async_copy(grad_far, grad_pre, sems.at[0])
    fetch_act = pltpu.make_async_copy(act_far, act, sems.at[1])
    fetch_grad.start()
    halves = (fetch_weights(mine, TAPS, wa, sa), fetch_weights(recv, TAPS, wb, sb))
    fetch_act.start()
    y[...] = jnp.zeros_like(y)
    fetch_grad.wait()
    grad = grad_pre[...]
    for di in range(3):
        for copies in halves:
            copies[di].wait()
        for dj in range(3):
            for dl in range(3):
                term = dot_t(grad, weight(wa, wb, di * 9 + dj * 3 + dl))
                term = term.reshape(9, OUT_ROWS, C)
                for qi in range(OUTER):
                    for qj in range(OUTER):
                        y[dl, 2 * qi + di, 2 * qj + dj] += term[qi * 3 + qj]
    store(gh, ACT_ROWS, 8, jnp.zeros((8, C), F32))
    count = EDGE * OUT_ROWS
    for i in range(EDGE):
        base = i * EDGE * ROWS
        store(gh, base, count, y[0, i + 1, 1:].reshape(count, C), 2)
        store(gh, base + 1, count, y[1, i + 1, 1:].reshape(count, C), 2)
    for i in range(EDGE):
        base = i * EDGE * ROWS + 2
        total = load(gh, base, count, 2) + y[2, i + 1, 1:].reshape(count, C)
        store(gh, base, count, total, 2)
    inside = cell_mask()
    fetch_act.wait()
    for i in range(EDGE):
        value = act[pl.ds(i * EDGE * ROWS, EDGE * ROWS), :]
        sigma = sigmoid(value)
        part = load(gh, i * EDGE * ROWS, EDGE * ROWS) * (sigma * (1.0 + value * (1.0 - sigma)))
        part = swap_halves(jnp.where(inside, part, 0.0), core)
        store(gh, i * EDGE * ROWS, EDGE * ROWS, part)
    for n in range(ACT_ROWS // HALF):
        gat[:, n * HALF : (n + 1) * HALF] = load(gh, n * HALF, HALF).T.astype(BF)


def back(core, act, grad_pre, mine, recv):
    return call(
        back_kernel, "back", shape((C, ACT_ROWS), BF),
        [SM, HB, HB, HB, HB],
        WEIGHTS
        + [
            pltpu.VMEM((3, 7, 7, OUT_ROWS, C), F32),
            pltpu.VMEM((2, ACT_ROWS + 8, HALF), F32),
            pltpu.VMEM((ACT_ROWS, C), F32),
            pltpu.VMEM((PRE_ROWS, C), BF),
            pltpu.SemaphoreType.DMA((2,)),
        ],
        20, 1_500_000_000, 8_000_000,
    )(core, act, grad_pre, mine, recv)


def grad_loop(far_out, out, sems, left, windows):
    eye = (
        lax.broadcasted_iota(jnp.int32, (C, C), 0) == lax.broadcasted_iota(jnp.int32, (C, C), 1)
    ).astype(BF)

    def send(n, count):
        part = pl.ds(GROUP * n, count)
        return pltpu.make_async_copy(out.at[:, part], far_out.at[:, part], sems.at[n])

    def product(taps):
        right = [
            jnp.concatenate([window(t // 9, t // 3 % 3, t % 3) for t in taps], axis=1)
            for window in windows
        ]
        total = dot(left[...], jnp.concatenate(right, axis=0)).astype(BF)
        for n in range(0, len(taps), 2):
            two = taps[n : n + 2]
            width = HALF * len(two)
            turned = dot_t(eye[:width, :width], total[:, n * HALF : n * HALF + width]).astype(BF)
            for m, t in enumerate(two):
                out[:, t] = turned[m * HALF : (m + 1) * HALF].reshape(MEMBERS, BLOCK, C)

    def step(n, carry):
        product([GROUP * n + k for k in range(GROUP)])
        send(n, GROUP).start()
        return carry

    whole = TAPS // GROUP
    lax.fori_loop(0, whole, step, 0)
    product(list(range(GROUP * whole, TAPS)))
    send(whole, TAPS - GROUP * whole).start()
    for n in range(whole):
        send(n, GROUP).wait()
    send(whole, TAPS - GROUP * whole).wait()


GRAD = (MEMBERS, TAPS, BLOCK, C)
STAGING = [pltpu.VMEM(GRAD, BF), pltpu.SemaphoreType.DMA((-(-TAPS // GROUP),))]


def grad2_kernel(grad_t, grad_t_other, hsel, hsel_other, far_out, out, sems, left):
    left[:, :PRE_ROWS] = grad_t[...]
    left[:, PRE_ROWS:] = grad_t_other[...]
    grad_loop(
        far_out,
        out,
        sems,
        left,
        (
            lambda di, dj, dl: strided_window(hsel, dl, di, dj, slice(0, HALF)),
            lambda di, dj, dl: strided_window(hsel_other, dl, di, dj),
        ),
    )


def grad2(grad_t, grad_t_other, hsel, hsel_other):
    return call(
        grad2_kernel, "grad2", shape(GRAD, BF), [VM] * 4,
        STAGING + [pltpu.VMEM((C, 2 * PRE_ROWS), BF)], 12, 1_000_000_000, 4_000_000, HB,
    )(grad_t, grad_t_other, hsel, hsel_other)


def same_window(x3):
    def window(di, dj, dl):
        return x3[dl, pl.ds(di, EDGE), pl.ds(dj, EDGE)].reshape(ACT_ROWS, HALF)

    return window


def grad1_kernel(gat, gat_other, x3a, x3o, far_out, out, sems, left):
    left[:, :ACT_ROWS] = gat[...]
    left[:, ACT_ROWS:] = gat_other[...]
    grad_loop(far_out, out, sems, left, (same_window(x3a), same_window(x3o)))


def grad1(gat, gat_other, x3a, x3o):
    return call(
        grad1_kernel, "grad1", shape(GRAD, BF), [VM] * 4,
        STAGING + [pltpu.VMEM((C, 2 * ACT_ROWS), BF)], 16, 4_000_000_000, 7_000_000, HB,
    )(gat, gat_other, x3a, x3o)


def pack_kernel(first, second, order, out):
    perm = one_hot(order[...])
    for i in range(2):
        lanes = slice(i * C, (i + 1) * C)
        one = dot(first[:, lanes].astype(BF), perm)
        both = jnp.concatenate([one, second[:, lanes]], axis=0).astype(BF)
        for n in range(MEMBERS):
            out[n, :, lanes] = both


def pack(first, second, order):
    return call(
        pack_kernel, "pack", shape((MEMBERS, 2 * TAPS, 2 * C), BF), [VM] * 3,
        [], 56, 10_000_000, 1_000_000,
    )(first, second, order)


def spread_kernel(shards, out, wide):
    for m in range(MEMBERS):
        rows = shards[m].astype(F32)
        for i in range(2):
            store(wide, 2 * m + i, 2 * TAPS, rows[:, i * C : (i + 1) * C], BLOCK)

    def step(t, carry):
        value = load(wide, pl.multiple_of(t * BLOCK, BLOCK), BLOCK).astype(BF)
        for n in range(MEMBERS):
            out[n, t] = value
        return carry

    lax.fori_loop(0, 2 * TAPS, step, 0)


def spread(shards):
    return call(
        spread_kernel, "spread", shape((MEMBERS, 2 * TAPS, BLOCK, C), BF), [VM],
        [pltpu.VMEM((2, 2 * TAPS * BLOCK, HALF), F32)], 10, 1_000_000, 5_000_000,
    )(shards)


def add_parts(parts, wide):
    def step(t, carry):
        total = parts[0, t].astype(F32)
        for n in range(1, MEMBERS):
            total = total + parts[n, t].astype(F32)
        store(wide, pl.multiple_of(t * BLOCK, BLOCK), BLOCK, total)
        return carry

    lax.fori_loop(0, TAPS, step, 0)


def collect2(parts):
    return call(
        add_parts, "collect2", shape((2, TAPS * BLOCK, HALF), F32), [VM], [],
        6, 1_000_000, 3_000_000,
    )(parts)


def collect_kernel(parts, second, out, wide):
    wide[:, TAPS * BLOCK :] = second[...]
    add_parts(parts, wide)
    for m in range(MEMBERS):
        for i in range(2):
            rows = load(wide, 2 * m + i, 2 * TAPS, BLOCK)
            out[m, :, i * C : (i + 1) * C] = rows.astype(BF)


def collect(parts, second):
    return call(
        collect_kernel, "collect", shape((MEMBERS, 2 * TAPS, 2 * C), BF), [VM] * 2,
        [pltpu.VMEM((2, 2 * TAPS * BLOCK, HALF), F32)], 8, 1_000_000, 3_000_000,
    )(parts, second)


def adam_update(weight, first, second, grad):
    first_new = 0.9 * first + 0.1 * grad
    second_new = 0.999 * second + 0.001 * grad * grad
    fix_first = 1.0 - 0.9**10
    fix_second = 1.0 - 0.999**10
    weight_new = weight - 0.05 * (first_new / fix_first) / (
        jnp.sqrt(second_new / fix_second) + 1e-08
    )
    return (weight_new, first_new, second_new)


def adam_kernel(
    scale, parts, order, k1, m1, v1, k2, m2, v2, k1n, m1n, v1n, k2n, m2n, v2n
):
    back = one_hot(order[...]).astype(F32)
    for i in range(2):
        lanes = slice(i * C, (i + 1) * C)
        total = parts[0, :, lanes].astype(F32)
        for n in range(1, MEMBERS):
            total = total + parts[n, :, lanes].astype(F32)
        total = total * scale
        grad = lax.dot_general(
            total[:TAPS],
            back,
            (((1,), (1,)), ((), ())),
            precision=lax.Precision.HIGHEST,
            preferred_element_type=F32,
        )
        k1n[:, lanes], m1n[:, lanes], v1n[:, lanes] = adam_update(
            k1[:, lanes], m1[:, lanes], v1[:, lanes], grad
        )
        k2n[:, lanes], m2n[:, lanes], v2n[:, lanes] = adam_update(
            k2[:, lanes], m2[:, lanes], v2[:, lanes], total[TAPS:]
        )


def adam(scale, parts, order, *state):
    return call(
        functools.partial(adam_kernel, scale), "adam",
        (shape((TAPS, 2 * C), F32),) * 6, [VM] * 8, [], 6, 10_000_000, 1_000_000,
    )(parts, order, *state)


def place(x, y, z, c):
    return ((x * 4 + y) * 4 + z) * 2 + c


LINE = [[0, 1, 2, 3]]
ONE = [[0], [1], [2], [3]]
EVEN_PAIRS = [[0, 1], [2, 3]]
ODD_PAIRS = [[1, 2], [3, 0]]
FAR_PAIRS = [[0, 2], [1, 3]]


def groups(c, xs, ys, zs):
    return [
        [place(x, y, z, c) for x in gx for y in gy for z in gz]
        for gx, gy, gz in itertools.product(xs, ys, zs)
    ]


NEAR = groups(0, LINE, EVEN_PAIRS, ONE) + groups(1, ONE, ODD_PAIRS, LINE)
FAR = groups(0, ONE, FAR_PAIRS, LINE) + groups(1, LINE, FAR_PAIRS, ONE)
PARTNERS = [(n, n ^ 1) for n in range(128)]


def channel_orders():
    orders = []
    for c in range(2):
        near = next(group for group in NEAR if group[0] % 2 == c)
        order = []
        for member in near:
            far = next(group for group in FAR if member in group)
            order += [2 * device + i for device in far for i in range(2)]
        orders.append(order)
    zero, one = orders
    return np.array([zero + one, one + zero], np.int32).reshape(2, 1, C)


ORDERS = channel_orders()


def exchange(value, groups):
    return lax.all_to_all(value, "dp", 0, 0, axis_index_groups=groups, tiled=True)


def swap(value):
    return lax.ppermute(value, "dp", PARTNERS)


def body(latent, out_grad, k1, m1, v1, k2, m2, v2):
    scale = 1.0 / (latent.shape[0] * lax.axis_size("dp"))
    core = lax.axis_index("dp") % 2
    orders = jnp.asarray(ORDERS)
    fixed = orders[0]
    own = jnp.where(core == 0, orders[0], orders[1])
    core = core.reshape(1)

    shards = pack(k1, k2, fixed)
    latent = latent.transpose(1, 2, 3, 0, 4)
    cells = prep(latent, swap(latent), out_grad.transpose(1, 2, 3, 0, 4), own)
    shards, cells = lax.optimization_barrier((exchange(shards, FAR), cells))
    x3a, x3b, x3o, skip, cot = cells
    mine = exchange(spread(shards), NEAR)
    recv = swap(mine)

    act, hsel, hsend = conv1(core, x3b, recv, conv1_own(x3a, mine))
    hsel_other = swap(hsend)
    block_out, grad_pre, grad_pre_t = conv2(skip, cot, hsel, mine, recv)
    second = grad2(grad_pre_t, swap(grad_pre_t), hsel, hsel_other)
    second, grad_pre = lax.optimization_barrier((second, grad_pre))
    parts2 = exchange(second, NEAR)
    gat = back(core, act, grad_pre, mine, recv)
    parts1 = exchange(grad1(gat, swap(gat), x3a, x3o), NEAR)
    parts = exchange(collect(parts1, collect2(parts2)), FAR)
    new = adam(scale, parts, fixed, k1, m1, v1, k2, m2, v2)
    return (block_out.transpose(3, 0, 1, 2, 4), *new)


def solution(mesh):
    wide = P("dp", None, None, None, None)
    flat = P(None, "dp")
    return jax.shard_map(
        body,
        mesh=mesh,
        in_specs=(wide, wide) + (flat,) * 6,
        out_specs=(wide,) + (flat,) * 6,
        check_vma=False,
    )
```

```python
import functools
import itertools

import jax
import jax.numpy as jnp
import numpy as np
from jax import lax
from jax.experimental import pallas as pl
from jax.experimental.pallas import tpu as pltpu
from jax.sharding import PartitionSpec as P

C = 256
HALF = 128
EDGE = 6
OUTER = 3
TAPS = 27
SAMP = 4
ROWS = 32
ACT_ROWS = EDGE * EDGE * ROWS
PAD_ROWS = 64 * ROWS
OUT_ROWS = 16
PRE_ROWS = 9 * OUT_ROWS
MIB = 1024 * 1024
BF = jnp.bfloat16
F32 = jnp.float32

GROUP = 6
BLOCK = 32
QUARTER = (TAPS, BLOCK, C)

VM = pl.BlockSpec(memory_space=pltpu.VMEM)
SM = pl.BlockSpec(memory_space=pltpu.SMEM)
HB = pl.BlockSpec(memory_space=pltpu.HBM)


def shape(dims, dtype):
    return jax.ShapeDtypeStruct(dims, dtype)


def call(kernel, name, out_shape, in_specs, scratch, mib, flops, moved, out_spec=VM):
    single = not isinstance(out_shape, tuple)
    return pl.pallas_call(
        kernel,
        out_shape=out_shape,
        in_specs=in_specs,
        out_specs=out_spec if single else (out_spec,) * len(out_shape),
        scratch_shapes=scratch,
        compiler_params=pltpu.CompilerParams(vmem_limit_bytes=mib * MIB),
        cost_estimate=pl.CostEstimate(flops=flops, bytes_accessed=moved, transcendentals=0),
        name=name,
    )


def dot(a, b):
    return jnp.dot(a, b, preferred_element_type=F32)


def dot_t(a, b):
    return lax.dot_general(a, b, (((1,), (1,)), ((), ())), preferred_element_type=F32)


def sigmoid(v):
    return 1.0 / (1.0 + jnp.exp(-v))


def load(ref, start, count, stride=1):
    return jnp.concatenate(
        [ref[half, pl.ds(start, count, stride=stride), :] for half in range(2)], axis=1
    )


def store(ref, start, count, value, stride=1):
    for half in range(2):
        ref[half, pl.ds(start, count, stride=stride), :] = value[
            :, half * HALF : (half + 1) * HALF
        ]


def one_hot(order_row):
    return (lax.broadcasted_iota(jnp.int32, (C, C), 0) == order_row).astype(BF)


def fill_cells(source, xs):
    for i in range(EDGE):
        for j in range(EDGE):
            value = source[i, j].astype(F32)
            base = 8 + ((i + 1) * 8 + j + 1) * ROWS + 1
            for l in range(EDGE):
                store(xs, base + l, SAMP, value[l], 8)


def prep_kernel(meta, latent, other, out_grad, orders, x3a, x3b, x3o, skip, cot, xs, og):
    perm = one_hot(orders[meta[0]])
    xs[...] = jnp.zeros_like(xs)
    og[...] = jnp.zeros_like(og)
    fill_cells(latent, xs)
    for qi in range(OUTER):
        for qj in range(OUTER):
            q = (qi * 3 + qj) * OUT_ROWS
            value = out_grad[qi, qj].astype(F32)
            for ql in range(OUTER):
                store(og, q + ql, SAMP, value[ql], 4)
            base = 8 + ((2 * qi + 1) * 8 + 2 * qj + 1) * ROWS + 1
            skip[q : q + OUT_ROWS, :] = load(xs, base, OUT_ROWS, 2)
    cot[...] = load(og, 0, PRE_ROWS)
    for i in range(8):
        for dl in range(3):
            rows = dot(load(xs, 7 + dl + i * 256, 256).astype(BF), perm).astype(BF)
            x3a[dl, i] = rows[:, :HALF].reshape(8, ROWS, HALF)
            x3b[dl, i] = rows[:, HALF:].reshape(8, ROWS, HALF)
    fill_cells(other, xs)
    for i in range(8):
        for dl in range(3):
            rows = dot(load(xs, 7 + dl + i * 256, 256).astype(BF), perm[:, :HALF])
            x3o[dl, i] = rows.astype(BF).reshape(8, ROWS, HALF)


def prep(meta, latent, other, out_grad, orders):
    wide = shape((3, 8, 8, ROWS, HALF), BF)
    pre = shape((PRE_ROWS, C), F32)
    return call(
        prep_kernel, "prep", (wide, wide, wide, pre, pre), [SM] + [VM] * 4,
        [pltpu.VMEM((2, PAD_ROWS + 16, HALF), F32), pltpu.VMEM((2, PRE_ROWS, HALF), F32)],
        20, 2_000_000_000, 8_000_000,
    )(meta, latent, other, out_grad, orders)


def swap_halves(value, core):
    swapped = jnp.concatenate([value[:, HALF:], value[:, :HALF]], axis=1)
    return jnp.where(core == 1, swapped, value)


def cell_mask():
    cell = lax.broadcasted_iota(jnp.int32, (EDGE * ROWS, C), 0) % 8
    return (cell >= 1) & (cell <= EDGE)


def fetch_weights(quarters, place_of, weights, sems):
    copies = []
    for di in range(3):
        part = pl.ds(9 * di, 9)
        for k, source in enumerate(quarters):
            copies.append(
                pltpu.make_async_copy(
                    source.at[part],
                    weights.at[jnp.bitwise_xor(place_of, k), part],
                    sems.at[4 * di + k],
                )
            )
            copies[-1].start()
    return [copies[4 * di : 4 * di + 4] for di in range(3)]


def wait_all(copies):
    for copy in copies:
        copy.wait()


def half_weight(weights, t):
    return weights[:, t].reshape(HALF, C)


HALF_WEIGHTS = [pltpu.VMEM((4, *QUARTER), BF), pltpu.SemaphoreType.DMA((12,))]
WEIGHTS = HALF_WEIGHTS + HALF_WEIGHTS


def half_conv(x3, weights, copies, act, start):
    for first in range(0, TAPS, GROUP):
        taps = range(first, min(first + GROUP, TAPS))
        for di in range(3):
            if first <= 9 * di < first + GROUP or (first, di) == (0, 0):
                wait_all(copies[di])
        windows = [
            x3[t % 3, t // 9 : t // 9 + EDGE, t // 3 % 3 : t // 3 % 3 + EDGE] for t in taps
        ]
        total = dot(
            jnp.concatenate([window.reshape(ACT_ROWS, HALF) for window in windows], axis=1),
            jnp.concatenate([half_weight(weights, t) for t in taps], axis=0),
        )
        before = act if first else start
        act[...] = total if before is None else before[...] + total


def conv1_own_kernel(meta, x3a, q0, q1, q2, q3, act, weights, sems):
    copies = fetch_weights((q0, q1, q2, q3), meta[1], weights, sems)
    half_conv(x3a, weights, copies, act, None)


def conv1_own(meta, x3a, own):
    return call(
        conv1_own_kernel, "conv1_own", shape((ACT_ROWS, C), F32), [SM, VM] + [HB] * 4,
        HALF_WEIGHTS, 12, 2_000_000_000, 5_000_000,
    )(meta, x3a, *own)


def conv1_kernel(meta, x3b, part_act, q0, q1, q2, q3, act, hsel, hsend, weights, sems, hs):
    core = meta[0]
    copies = fetch_weights((q0, q1, q2, q3), meta[2], weights, sems)
    half_conv(x3b, weights, copies, act, part_act)

    hsel[:, 0] = jnp.zeros_like(hsel[:, 0])
    hsel[:, :, 0] = jnp.zeros_like(hsel[:, :, 0])
    hsend[:, 0] = jnp.zeros_like(hsend[:, 0])
    hsend[:, :, 0] = jnp.zeros_like(hsend[:, :, 0])
    store(hs, ACT_ROWS, 8, jnp.zeros((8, C), F32))
    inside = cell_mask()
    for i in range(EDGE):
        part = pl.ds(i * EDGE * ROWS, EDGE * ROWS)
        value = swap_halves(act[part, :], core)
        act[part, :] = value
        hidden = jnp.where(inside, value * sigmoid(value), 0.0)
        store(hs, i * EDGE * ROWS, EDGE * ROWS, hidden.astype(BF).astype(F32))
    for dl in range(3):
        for i in range(EDGE):
            rows = load(hs, i * EDGE * ROWS + dl, EDGE * OUT_ROWS, 2)
            rows = rows.astype(BF).reshape(EDGE, OUT_ROWS, C)
            hsel[dl, i + 1, 1:] = rows
            hsend[dl, i + 1, 1:] = rows[..., HALF:]


def conv1(meta, x3b, part_act, other):
    return call(
        conv1_kernel, "conv1",
        (
            shape((ACT_ROWS, C), F32),
            shape((3, 7, 7, OUT_ROWS, C), BF),
            shape((3, 7, 7, OUT_ROWS, HALF), BF),
        ),
        [SM, VM, VM] + [HB] * 4,
        HALF_WEIGHTS + [pltpu.VMEM((2, ACT_ROWS + 8, HALF), F32)],
        24, 2_000_000_000, 7_000_000,
    )(meta, x3b, part_act, *other)


def weight(wa, wb, t):
    return jnp.concatenate([half_weight(wa, t), half_weight(wb, t)], axis=0)


def strided_window(hsel, dl, di, dj, lanes=slice(None)):
    blocks = [
        hsel[dl, 2 * qi + di, 2 * qj + dj, :, lanes] for qi in range(OUTER) for qj in range(OUTER)
    ]
    return jnp.concatenate(blocks, axis=0)


def conv2_kernel(
    meta, skip, cot, hsel, q0, q1, q2, q3, p0, p1, p2, p3,
    block_out, grad_pre, grad_pre_t, wa, sa, wb, sb, bo,
):
    halves = (
        fetch_weights((q0, q1, q2, q3), meta[1], wa, sa),
        fetch_weights((p0, p1, p2, p3), meta[2], wb, sb),
    )
    pre = skip[...]
    for di in range(3):
        for copies in halves:
            wait_all(copies[di])
        for dj in range(3):
            for dl in range(3):
                pre = pre + dot(
                    strided_window(hsel, dl, di, dj), weight(wa, wb, di * 9 + dj * 3 + dl)
                )
    sigma = sigmoid(pre)
    store(bo, 0, PRE_ROWS, pre * sigma)
    for qi in range(OUTER):
        for qj in range(OUTER):
            for ql in range(OUTER):
                base = (qi * 3 + qj) * OUT_ROWS + ql
                block_out[qi, qj, ql] = load(bo, base, SAMP, 4).astype(BF)
    grad = (cot[...] * (sigma * (1.0 + pre * (1.0 - sigma)))).astype(BF)
    grad_pre[...] = grad
    grad_pre_t[...] = grad.astype(F32).T.astype(BF)


def conv2(meta, skip, cot, hsel, own, other):
    return call(
        conv2_kernel, "conv2",
        (
            shape((OUTER, OUTER, OUTER, SAMP, C), BF),
            shape((PRE_ROWS, C), BF),
            shape((C, PRE_ROWS), BF),
        ),
        [SM, VM, VM, VM] + [HB] * 8,
        WEIGHTS + [pltpu.VMEM((2, PRE_ROWS, HALF), F32)],
        16, 1_500_000_000, 6_000_000,
    )(meta, skip, cot, hsel, *own, *other)


def back_kernel(
    meta, act_far, grad_far, q0, q1, q2, q3, p0, p1, p2, p3,
    gat, wa, sa, wb, sb, y, gh, act, grad_pre, sems,
):
    core = meta[0]
    fetch_grad = pltpu.make_async_copy(grad_far, grad_pre, sems.at[0])
    fetch_act = pltpu.make_async_copy(act_far, act, sems.at[1])
    fetch_grad.start()
    halves = (
        fetch_weights((q0, q1, q2, q3), meta[1], wa, sa),
        fetch_weights((p0, p1, p2, p3), meta[2], wb, sb),
    )
    fetch_act.start()
    y[...] = jnp.zeros_like(y)
    fetch_grad.wait()
    grad = grad_pre[...]
    for di in range(3):
        for copies in halves:
            wait_all(copies[di])
        for dj in range(3):
            for dl in range(3):
                term = dot_t(grad, weight(wa, wb, di * 9 + dj * 3 + dl))
                term = term.reshape(9, OUT_ROWS, C)
                for qi in range(OUTER):
                    for qj in range(OUTER):
                        y[dl, 2 * qi + di, 2 * qj + dj] += term[qi * 3 + qj]
    store(gh, ACT_ROWS, 8, jnp.zeros((8, C), F32))
    count = EDGE * OUT_ROWS
    for i in range(EDGE):
        base = i * EDGE * ROWS
        store(gh, base, count, y[0, i + 1, 1:].reshape(count, C), 2)
        store(gh, base + 1, count, y[1, i + 1, 1:].reshape(count, C), 2)
    for i in range(EDGE):
        base = i * EDGE * ROWS + 2
        total = load(gh, base, count, 2) + y[2, i + 1, 1:].reshape(count, C)
        store(gh, base, count, total, 2)
    inside = cell_mask()
    fetch_act.wait()
    for i in range(EDGE):
        value = act[pl.ds(i * EDGE * ROWS, EDGE * ROWS), :]
        sigma = sigmoid(value)
        part = load(gh, i * EDGE * ROWS, EDGE * ROWS) * (sigma * (1.0 + value * (1.0 - sigma)))
        part = swap_halves(jnp.where(inside, part, 0.0), core)
        store(gh, i * EDGE * ROWS, EDGE * ROWS, part)
    for n in range(ACT_ROWS // HALF):
        gat[:, n * HALF : (n + 1) * HALF] = load(gh, n * HALF, HALF).T.astype(BF)


def back(meta, act, grad_pre, own, other):
    return call(
        back_kernel, "back", shape((C, ACT_ROWS), BF),
        [SM, HB, HB] + [HB] * 8,
        WEIGHTS
        + [
            pltpu.VMEM((3, 7, 7, OUT_ROWS, C), F32),
            pltpu.VMEM((2, ACT_ROWS + 8, HALF), F32),
            pltpu.VMEM((ACT_ROWS, C), F32),
            pltpu.VMEM((PRE_ROWS, C), BF),
            pltpu.SemaphoreType.DMA((2,)),
        ],
        20, 1_500_000_000, 8_000_000,
    )(meta, act, grad_pre, *own, *other)


def grad_loop(place_of, far, out, sems, left, windows):
    eye = (
        lax.broadcasted_iota(jnp.int32, (C, C), 0) == lax.broadcasted_iota(jnp.int32, (C, C), 1)
    ).astype(BF)

    def send(n, count):
        part = pl.ds(GROUP * n, count)
        return [
            pltpu.make_async_copy(
                out.at[jnp.bitwise_xor(place_of, k), part], quarter.at[part], sems.at[n, k]
            )
            for k, quarter in enumerate(far)
        ]

    def product(taps):
        right = [
            jnp.concatenate([window(t // 9, t // 3 % 3, t % 3) for t in taps], axis=1)
            for window in windows
        ]
        total = dot(left[...], jnp.concatenate(right, axis=0)).astype(BF)
        for n in range(0, len(taps), 2):
            two = taps[n : n + 2]
            width = HALF * len(two)
            turned = dot_t(eye[:width, :width], total[:, n * HALF : n * HALF + width]).astype(BF)
            for m, t in enumerate(two):
                out[:, t] = turned[m * HALF : (m + 1) * HALF].reshape(4, BLOCK, C)

    def step(n, carry):
        product([GROUP * n + k for k in range(GROUP)])
        for copy in send(n, GROUP):
            copy.start()
        return carry

    whole = TAPS // GROUP
    lax.fori_loop(0, whole, step, 0)
    product(list(range(GROUP * whole, TAPS)))
    for copy in send(whole, TAPS - GROUP * whole):
        copy.start()
    for n in range(whole):
        wait_all(send(n, GROUP))
    wait_all(send(whole, TAPS - GROUP * whole))


QUARTERS = (shape(QUARTER, BF),) * 4
STAGING = [pltpu.VMEM((4, *QUARTER), BF), pltpu.SemaphoreType.DMA((-(-TAPS // GROUP), 4))]


def grad2_kernel(
    meta, grad_t, grad_t_other, hsel, hsel_other, f0, f1, f2, f3, out, sems, left
):
    left[:, :PRE_ROWS] = grad_t[...]
    left[:, PRE_ROWS:] = grad_t_other[...]
    grad_loop(
        meta[1],
        (f0, f1, f2, f3),
        out,
        sems,
        left,
        (
            lambda di, dj, dl: strided_window(hsel, dl, di, dj, slice(0, HALF)),
            lambda di, dj, dl: strided_window(hsel_other, dl, di, dj),
        ),
    )


def grad2(meta, grad_t, grad_t_other, hsel, hsel_other):
    return call(
        grad2_kernel, "grad2", QUARTERS, [SM] + [VM] * 4,
        STAGING + [pltpu.VMEM((C, 2 * PRE_ROWS), BF)], 12, 1_000_000_000, 4_000_000, HB,
    )(meta, grad_t, grad_t_other, hsel, hsel_other)


def same_window(x3):
    def window(di, dj, dl):
        return x3[dl, pl.ds(di, EDGE), pl.ds(dj, EDGE)].reshape(ACT_ROWS, HALF)

    return window


def grad1_kernel(meta, gat, gat_other, x3a, x3o, f0, f1, f2, f3, out, sems, left):
    left[:, :ACT_ROWS] = gat[...]
    left[:, ACT_ROWS:] = gat_other[...]
    windows = (same_window(x3a), same_window(x3o))
    grad_loop(meta[1], (f0, f1, f2, f3), out, sems, left, windows)


def grad1(meta, gat, gat_other, x3a, x3o):
    return call(
        grad1_kernel, "grad1", QUARTERS, [SM] + [VM] * 4,
        STAGING + [pltpu.VMEM((C, 2 * ACT_ROWS), BF)], 16, 4_000_000_000, 7_000_000, HB,
    )(meta, gat, gat_other, x3a, x3o)


SHARD = (2 * TAPS, 2 * C)
FOUR = (4, *SHARD)


def pack_kernel(first, second, orders, out):
    perm = one_hot(orders[0])
    for i in range(2):
        lanes = slice(i * C, (i + 1) * C)
        one = dot(first[:, lanes].astype(BF), perm)
        out[:, lanes] = jnp.concatenate([one, second[:, lanes]], axis=0).astype(BF)


def pack(first, second, orders):
    return call(
        pack_kernel, "pack", shape(SHARD, BF), [VM] * 3, [], 56, 10_000_000, 300_000
    )(first, second, orders)


def join_kernel(meta, p0, p1, p2, p3, out):
    for k, part in enumerate((p0, p1, p2, p3)):
        out[jnp.bitwise_xor(meta[3], k)] = part[...]


def join(meta, parts):
    return call(
        join_kernel, "join", shape(FOUR, BF), [SM] + [VM] * 4, [], 4, 100_000, 500_000
    )(meta, *parts)


def spread_kernel(meta, p0, p1, p2, p3, out1, out2, stage, wide):
    for k, part in enumerate((p0, p1, p2, p3)):
        stage[jnp.bitwise_xor(meta[2], k)] = part[...]
    for m in range(4):
        for n in range(4):
            rows = stage[m, n].astype(F32)
            for i in range(2):
                start = 8 * m + 2 * n + i
                store(wide, start, 2 * TAPS, rows[:, i * C : (i + 1) * C], BLOCK)

    def step(t, carry):
        for k, out in enumerate((out1, out2)):
            start = pl.multiple_of((k * TAPS + t) * BLOCK, BLOCK)
            out[t] = load(wide, start, BLOCK).astype(BF)
        return carry

    lax.fori_loop(0, TAPS, step, 0)


def spread(meta, parts):
    return call(
        spread_kernel, "spread", (shape(QUARTER, BF),) * 2, [SM] + [VM] * 4,
        [pltpu.VMEM((4, *FOUR), BF), pltpu.VMEM((2, 2 * TAPS * BLOCK, HALF), F32)],
        8, 1_000_000, 2_000_000,
    )(meta, *parts)


def add_parts(p0, p1, p2, p3, wide):
    def step(t, carry):
        total = p0[t].astype(F32)
        for part in (p1, p2, p3):
            total = total + part[t].astype(F32)
        store(wide, pl.multiple_of(t * BLOCK, BLOCK), BLOCK, total)
        return carry

    lax.fori_loop(0, TAPS, step, 0)


def collect2(parts):
    return call(
        add_parts, "collect2", shape((2, TAPS * BLOCK, HALF), F32), [VM] * 4, [],
        4, 1_000_000, 3_000_000,
    )(*parts)


def collect_kernel(meta, p0, p1, p2, p3, second, f0, f1, f2, f3, wide, stage, sems):
    wide[:, TAPS * BLOCK :] = second[...]
    add_parts(p0, p1, p2, p3, wide)
    copies = []
    for k, far in enumerate((f0, f1, f2, f3)):
        m = jnp.bitwise_xor(meta[2], k)
        copies.append(pltpu.make_async_copy(stage.at[m], far, sems.at[k]))
    for m in range(4):
        for n in range(4):
            for i in range(2):
                rows = load(wide, 8 * m + 2 * n + i, 2 * TAPS, BLOCK)
                stage[m, n, :, i * C : (i + 1) * C] = rows.astype(BF)
    for copy in copies:
        copy.start()
    wait_all(copies)


def collect(meta, parts, second):
    return call(
        collect_kernel, "collect", (shape(FOUR, BF),) * 4, [SM] + [VM] * 5,
        [
            pltpu.VMEM((2, 2 * TAPS * BLOCK, HALF), F32),
            pltpu.VMEM((4, *FOUR), BF),
            pltpu.SemaphoreType.DMA((4,)),
        ],
        8, 1_000_000, 3_000_000, HB,
    )(meta, *parts, second)


def divide_kernel(meta, p0, p1, p2, p3, f0, f1, f2, f3):
    for k, far in enumerate((f0, f1, f2, f3)):
        n = jnp.bitwise_xor(meta[3], k)
        total = p0[n].astype(F32)
        for part in (p1, p2, p3):
            total = total + part[n].astype(F32)
        far[...] = total.astype(BF)


def divide(meta, parts):
    return call(
        divide_kernel, "divide", (shape(SHARD, BF),) * 4, [SM] + [VM] * 4, [],
        4, 1_000_000, 1_000_000,
    )(meta, *parts)


def adam_update(weight, first, second, grad):
    first_new = 0.9 * first + 0.1 * grad
    second_new = 0.999 * second + 0.001 * grad * grad
    fix_first = 1.0 - 0.9**10
    fix_second = 1.0 - 0.999**10
    weight_new = weight - 0.05 * (first_new / fix_first) / (
        jnp.sqrt(second_new / fix_second) + 1e-08
    )
    return (weight_new, first_new, second_new)


def adam_kernel(
    scale, p0, p1, p2, p3, orders, k1, m1, v1, k2, m2, v2, k1n, m1n, v1n, k2n, m2n, v2n
):
    back = one_hot(orders[0]).astype(F32)
    for i in range(2):
        lanes = slice(i * C, (i + 1) * C)
        total = p0[:, lanes].astype(F32)
        for part in (p1, p2, p3):
            total = total + part[:, lanes].astype(F32)
        total = total * scale
        grad = lax.dot_general(
            total[:TAPS],
            back,
            (((1,), (1,)), ((), ())),
            precision=lax.Precision.HIGHEST,
            preferred_element_type=F32,
        )
        k1n[:, lanes], m1n[:, lanes], v1n[:, lanes] = adam_update(
            k1[:, lanes], m1[:, lanes], v1[:, lanes], grad
        )
        k2n[:, lanes], m2n[:, lanes], v2n[:, lanes] = adam_update(
            k2[:, lanes], m2[:, lanes], v2[:, lanes], total[TAPS:]
        )


def adam(scale, parts, orders, *state):
    return call(
        functools.partial(adam_kernel, scale), "adam",
        (shape((TAPS, 2 * C), F32),) * 6, [VM] * 11, [], 6, 10_000_000, 1_000_000,
    )(*parts, orders, *state)


def place(x, y, z, c):
    return ((x * 4 + y) * 4 + z) * 2 + c


GRAY = [(0, 0), (1, 0), (1, 1), (0, 1)]
RING = {bits: at for at, bits in enumerate(GRAY)}


def label(bits):
    return bits[0] ^ 2 * bits[1] ^ 3 * bits[2]


def device(core, near, far):
    first, second = (near, far) if core == 0 else (far, near)
    return place(*(RING[pair] for pair in zip(first, second)), core)


TRIPLES = list(itertools.product(range(2), repeat=3))
DEVICES = list(itertools.product(range(2), TRIPLES, TRIPLES))


def turned(bits, which):
    return tuple(bit ^ (n in which) for n, bit in enumerate(bits))


def pairs(near=(), far=()):
    return [
        (device(c, u, v), device(c, turned(u, near), turned(v, far))) for c, u, v in DEVICES
    ]


EVERY = (0, 1, 2)
FIRST_ROUND = [pairs(far=EVERY), pairs(near=EVERY), pairs(near=EVERY, far=EVERY)]
SECOND_ROUND = [pairs(far=(k,)) for k in range(3)]
THIRD_ROUND = [pairs(near=(k,)) for k in range(3)]
PARTNERS = [(n, n ^ 1) for n in range(128)]


def tables():
    meta = np.zeros((128, 8), np.int32)
    at = {}
    for c, u, v in DEVICES:
        row = (c, label(u), label(v), 2 * u[2] + v[2])
        meta[device(c, u, v), :4] = row
        at[row] = device(c, u, v)
    halves = [
        [2 * at[(c, l, m, n)] + i for l in range(4) for m in range(4) for n in range(4) for i in range(2)]
        for c in range(2)
    ]
    orders = [halves[0] + halves[1], halves[1] + halves[0]]
    return meta, np.array(orders, np.int32).reshape(2, 1, C)


META, ORDERS = tables()


def swap(value):
    return lax.ppermute(value, "dp", PARTNERS)


def send_round(values, plan):
    return [values[0]] + [lax.ppermute(v, "dp", to) for v, to in zip(values[1:], plan)]


def gather_round(value, plan):
    return send_round([value] * 4, plan)


def after(value, *others):
    return lax.optimization_barrier((value, *others))[0]


def body(latent, out_grad, k1, m1, v1, k2, m2, v2):
    scale = 1.0 / (latent.shape[0] * lax.axis_size("dp"))
    meta = lax.dynamic_index_in_dim(jnp.asarray(META), lax.axis_index("dp"), keepdims=False)
    orders = jnp.asarray(ORDERS)

    shards = gather_round(pack(k1, k2, orders), FIRST_ROUND)
    latent = latent.transpose(1, 2, 3, 0, 4)
    x3a, x3b, x3o, skip, cot = prep(
        meta, latent, swap(latent), out_grad.transpose(1, 2, 3, 0, 4), orders
    )
    own1, own2 = spread(meta, gather_round(join(meta, shards), SECOND_ROUND))
    own1 = gather_round(own1, THIRD_ROUND)
    own2 = gather_round(after(own2, *own1[1:]), THIRD_ROUND)
    other1 = [swap(value) for value in own1]
    other2 = [swap(value) for value in own2]

    act, hsel, hsend = conv1(meta, x3b, conv1_own(meta, x3a, own1), other1)
    hsel_other = swap(hsend)
    block_out, grad_pre, grad_pre_t = conv2(meta, skip, cot, hsel, own2, other2)
    second = grad2(meta, grad_pre_t, swap(grad_pre_t), hsel, hsel_other)
    grad_pre = after(grad_pre, *second)
    second = send_round(second, THIRD_ROUND)
    gat = back(meta, act, grad_pre, own2, other2)
    first = send_round(grad1(meta, gat, swap(gat), x3a, x3o), THIRD_ROUND)
    parts = send_round(collect(meta, first, collect2(second)), SECOND_ROUND)
    parts = send_round(divide(meta, parts), FIRST_ROUND)
    new = adam(scale, parts, orders, k1, m1, v1, k2, m2, v2)
    return (block_out.transpose(3, 0, 1, 2, 4), *new)


def solution(mesh):
    wide = P("dp", None, None, None, None)
    flat = P(None, "dp")
    return jax.shard_map(
        body,
        mesh=mesh,
        in_specs=(wide, wide) + (flat,) * 6,
        out_specs=(wide,) + (flat,) * 6,
        check_vma=False,
    )
```

```python
import functools
import itertools

import jax
import jax.numpy as jnp
import numpy as np
from jax import lax
from jax.experimental import pallas as pl
from jax.experimental.pallas import tpu as pltpu
from jax.sharding import PartitionSpec as P

C = 256
HALF = 128
EDGE = 6
OUTER = 3
TAPS = 27
SAMP = 4
ROWS = 32
ACT_ROWS = EDGE * EDGE * ROWS
PAD_ROWS = 64 * ROWS
OUT_ROWS = 16
PRE_ROWS = 9 * OUT_ROWS
MEMBERS = 16
MIB = 1024 * 1024
BF = jnp.bfloat16
F32 = jnp.float32

GROUP = 6
BLOCK = 32
QUARTER = (TAPS, BLOCK, C)

VM = pl.BlockSpec(memory_space=pltpu.VMEM)


def shape(dims, dtype):
    return jax.ShapeDtypeStruct(dims, dtype)


def call(kernel, name, out_shape, in_specs, scratch, mib, flops, moved):
    single = not isinstance(out_shape, tuple)
    return pl.pallas_call(
        kernel,
        out_shape=out_shape,
        in_specs=in_specs,
        out_specs=VM if single else (VM,) * len(out_shape),
        scratch_shapes=scratch,
        compiler_params=pltpu.CompilerParams(vmem_limit_bytes=mib * MIB),
        cost_estimate=pl.CostEstimate(flops=flops, bytes_accessed=moved, transcendentals=0),
        name=name,
    )


def dot(a, b):
    return jnp.dot(a, b, preferred_element_type=F32)


def dot_t(a, b):
    return lax.dot_general(a, b, (((1,), (1,)), ((), ())), preferred_element_type=F32)


def sigmoid(v):
    return 1.0 / (1.0 + jnp.exp(-v))


def load(ref, start, count, stride=1):
    return jnp.concatenate(
        [ref[half, pl.ds(start, count, stride=stride), :] for half in range(2)], axis=1
    )


def store(ref, start, count, value, stride=1):
    for half in range(2):
        ref[half, pl.ds(start, count, stride=stride), :] = value[
            :, half * HALF : (half + 1) * HALF
        ]


def one_hot(order_row):
    return (lax.broadcasted_iota(jnp.int32, (C, C), 0) == order_row).astype(BF)


def fill_cells(source, xs):
    for i in range(EDGE):
        for j in range(EDGE):
            value = source[i, j].astype(F32)
            base = 8 + ((i + 1) * 8 + j + 1) * ROWS + 1
            for l in range(EDGE):
                store(xs, base + l, SAMP, value[l], 8)


def prep_kernel(latent, other, out_grad, table, x3a, x3b, x3o, skip, cot, xs, og):
    perm = one_hot(table[0])
    xs[...] = jnp.zeros_like(xs)
    og[...] = jnp.zeros_like(og)
    fill_cells(latent, xs)
    for qi in range(OUTER):
        for qj in range(OUTER):
            q = (qi * 3 + qj) * OUT_ROWS
            value = out_grad[qi, qj].astype(F32)
            for ql in range(OUTER):
                store(og, q + ql, SAMP, value[ql], 4)
            base = 8 + ((2 * qi + 1) * 8 + 2 * qj + 1) * ROWS + 1
            skip[q : q + OUT_ROWS, :] = load(xs, base, OUT_ROWS, 2)
    cot[...] = load(og, 0, PRE_ROWS)
    for i in range(8):
        for dl in range(3):
            rows = dot(load(xs, 7 + dl + i * 256, 256).astype(BF), perm).astype(BF)
            x3a[dl, i] = rows[:, :HALF].reshape(8, ROWS, HALF)
            x3b[dl, i] = rows[:, HALF:].reshape(8, ROWS, HALF)
    fill_cells(other, xs)
    for i in range(8):
        for dl in range(3):
            rows = dot(load(xs, 7 + dl + i * 256, 256).astype(BF), perm[:, :HALF])
            x3o[dl, i] = rows.astype(BF).reshape(8, ROWS, HALF)


def prep(latent, other, out_grad, table):
    wide = shape((3, 8, 8, ROWS, HALF), BF)
    pre = shape((PRE_ROWS, C), F32)
    return call(
        prep_kernel, "prep", (wide, wide, wide, pre, pre), [VM] * 4,
        [pltpu.VMEM((2, PAD_ROWS + 16, HALF), F32), pltpu.VMEM((2, PRE_ROWS, HALF), F32)],
        20, 2_000_000_000, 8_000_000,
    )(latent, other, out_grad, table)


def cell_mask():
    cell = lax.broadcasted_iota(jnp.int32, (EDGE * ROWS, C), 0) % 8
    return (cell >= 1) & (cell <= EDGE)


def half_weight(quarters, t):
    return jnp.concatenate([quarter[t] for quarter in quarters], axis=0)


def half_conv(x3, quarters, act, start):
    for first in range(0, TAPS, GROUP):
        taps = range(first, min(first + GROUP, TAPS))
        windows = [
            x3[t % 3, t // 9 : t // 9 + EDGE, t // 3 % 3 : t // 3 % 3 + EDGE] for t in taps
        ]
        total = dot(
            jnp.concatenate([window.reshape(ACT_ROWS, HALF) for window in windows], axis=1),
            jnp.concatenate([half_weight(quarters, t) for t in taps], axis=0),
        )
        before = act if first else start
        act[...] = total if before is None else before[...] + total


def conv1_own_kernel(x3a, q0, q1, q2, q3, act):
    half_conv(x3a, (q0, q1, q2, q3), act, None)


def conv1_own(x3a, own):
    return call(
        conv1_own_kernel, "conv1_own", shape((ACT_ROWS, C), F32), [VM] * 5,
        [], 12, 2_000_000_000, 5_000_000,
    )(x3a, *own)


def permuted(value, lanes):
    high = value.astype(BF)
    rest = value - high.astype(F32)
    middle = rest.astype(BF)
    low = (rest - middle.astype(F32)).astype(BF)
    return dot(high, lanes) + (dot(middle, lanes) + dot(low, lanes))


def conv1_kernel(x3b, part_act, q0, q1, q2, q3, table, act, hsel, hsend, hs):
    half_conv(x3b, (q0, q1, q2, q3), act, part_act)

    hsel[:, 0] = jnp.zeros_like(hsel[:, 0])
    hsel[:, :, 0] = jnp.zeros_like(hsel[:, :, 0])
    hsend[:, 0] = jnp.zeros_like(hsend[:, 0])
    hsend[:, :, 0] = jnp.zeros_like(hsend[:, :, 0])
    store(hs, ACT_ROWS, 8, jnp.zeros((8, C), F32))
    inside = cell_mask()
    lanes = one_hot(table[1])
    for i in range(EDGE):
        part = pl.ds(i * EDGE * ROWS, EDGE * ROWS)
        value = permuted(act[part, :], lanes)
        act[part, :] = value
        hidden = jnp.where(inside, value * sigmoid(value), 0.0)
        store(hs, i * EDGE * ROWS, EDGE * ROWS, hidden.astype(BF).astype(F32))
    for dl in range(3):
        for i in range(EDGE):
            rows = load(hs, i * EDGE * ROWS + dl, EDGE * OUT_ROWS, 2)
            rows = rows.astype(BF).reshape(EDGE, OUT_ROWS, C)
            hsel[dl, i + 1, 1:] = rows
            hsend[dl, i + 1, 1:] = rows[..., HALF:]


def conv1(x3b, part_act, other, table):
    return call(
        conv1_kernel, "conv1",
        (
            shape((ACT_ROWS, C), F32),
            shape((3, 7, 7, OUT_ROWS, C), BF),
            shape((3, 7, 7, OUT_ROWS, HALF), BF),
        ),
        [VM] * 7,
        [pltpu.VMEM((2, ACT_ROWS + 8, HALF), F32)],
        24, 2_000_000_000, 7_000_000,
    )(x3b, part_act, *other, table)


def strided_window(hsel, dl, di, dj, lanes=slice(None)):
    blocks = [
        hsel[dl, 2 * qi + di, 2 * qj + dj, :, lanes] for qi in range(OUTER) for qj in range(OUTER)
    ]
    return jnp.concatenate(blocks, axis=0)


def conv2_kernel(
    skip, cot, hsel, q0, q1, q2, q3, p0, p1, p2, p3, block_out, grad_pre, grad_pre_t, bo
):
    quarters = (q0, q1, q2, q3, p0, p1, p2, p3)
    pre = skip[...]
    for di in range(3):
        for dj in range(3):
            for dl in range(3):
                pre = pre + dot(
                    strided_window(hsel, dl, di, dj), half_weight(quarters, di * 9 + dj * 3 + dl)
                )
    sigma = sigmoid(pre)
    store(bo, 0, PRE_ROWS, pre * sigma)
    for qi in range(OUTER):
        for qj in range(OUTER):
            for ql in range(OUTER):
                base = (qi * 3 + qj) * OUT_ROWS + ql
                block_out[qi, qj, ql] = load(bo, base, SAMP, 4).astype(BF)
    grad = (cot[...] * (sigma * (1.0 + pre * (1.0 - sigma)))).astype(BF)
    grad_pre[...] = grad
    grad_pre_t[...] = grad.astype(F32).T.astype(BF)


def conv2(skip, cot, hsel, own, other):
    return call(
        conv2_kernel, "conv2",
        (
            shape((OUTER, OUTER, OUTER, SAMP, C), BF),
            shape((PRE_ROWS, C), BF),
            shape((C, PRE_ROWS), BF),
        ),
        [VM] * 11,
        [pltpu.VMEM((2, PRE_ROWS, HALF), F32)],
        16, 1_500_000_000, 6_000_000,
    )(skip, cot, hsel, *own, *other)


def back_kernel(
    act, grad_pre, q0, q1, q2, q3, p0, p1, p2, p3, table, gat, y, gh
):
    quarters = (q0, q1, q2, q3, p0, p1, p2, p3)
    y[...] = jnp.zeros_like(y)
    grad = grad_pre[...]
    for di in range(3):
        for dj in range(3):
            for dl in range(3):
                term = dot_t(grad, half_weight(quarters, di * 9 + dj * 3 + dl))
                term = term.reshape(9, OUT_ROWS, C)
                for qi in range(OUTER):
                    for qj in range(OUTER):
                        y[dl, 2 * qi + di, 2 * qj + dj] += term[qi * 3 + qj]
    store(gh, ACT_ROWS, 8, jnp.zeros((8, C), F32))
    count = EDGE * OUT_ROWS
    for i in range(EDGE):
        base = i * EDGE * ROWS
        store(gh, base, count, y[0, i + 1, 1:].reshape(count, C), 2)
        store(gh, base + 1, count, y[1, i + 1, 1:].reshape(count, C), 2)
    for i in range(EDGE):
        base = i * EDGE * ROWS + 2
        total = load(gh, base, count, 2) + y[2, i + 1, 1:].reshape(count, C)
        store(gh, base, count, total, 2)
    inside = cell_mask()
    lanes = one_hot(table[1])
    for i in range(0, EDGE, 2):
        grads = []
        for start in (i * EDGE * ROWS, (i + 1) * EDGE * ROWS):
            value = act[pl.ds(start, EDGE * ROWS), :]
            sigma = sigmoid(value)
            grad = load(gh, start, EDGE * ROWS) * (sigma * (1.0 + value * (1.0 - sigma)))
            grads.append(jnp.where(inside, grad, 0.0).astype(BF))
        gat[i // 2] = dot_t(lanes, jnp.concatenate(grads, axis=0)).astype(BF)


def back(act, grad_pre, own, other, table):
    return call(
        back_kernel, "back", shape((EDGE // 2, C, 2 * EDGE * ROWS), BF), [VM] * 11,
        [
            pltpu.VMEM((3, 7, 7, OUT_ROWS, C), F32),
            pltpu.VMEM((2, ACT_ROWS + 8, HALF), F32),
        ],
        16, 1_500_000_000, 8_000_000,
    )(act, grad_pre, *own, *other, table)


def grad_loop(quarters, left, windows):
    eye = (
        lax.broadcasted_iota(jnp.int32, (C, C), 0) == lax.broadcasted_iota(jnp.int32, (C, C), 1)
    ).astype(BF)

    def product(taps):
        right = [
            jnp.concatenate([window(t // 9, t // 3 % 3, t % 3) for t in taps], axis=1)
            for window in windows
        ]
        total = dot(left[...], jnp.concatenate(right, axis=0)).astype(BF)
        for n in range(0, len(taps), 2):
            two = taps[n : n + 2]
            width = HALF * len(two)
            turned = dot_t(eye[:width, :width], total[:, n * HALF : n * HALF + width]).astype(BF)
            for m, t in enumerate(two):
                for k, quarter in enumerate(quarters):
                    first = m * HALF + k * BLOCK
                    quarter[t] = turned[first : first + BLOCK]

    def step(n, carry):
        product([GROUP * n + k for k in range(GROUP)])
        return carry

    whole = TAPS // GROUP
    lax.fori_loop(0, whole, step, 0)
    product(list(range(GROUP * whole, TAPS)))


QUARTERS = (shape(QUARTER, BF),) * 4


def grad2_kernel(
    grad_t, grad_t_other, hsel, hsel_other, f0, f1, f2, f3, left
):
    left[:, :PRE_ROWS] = grad_t[...]
    left[:, PRE_ROWS:] = grad_t_other[...]
    grad_loop(
        (f0, f1, f2, f3),
        left,
        (
            lambda di, dj, dl: strided_window(hsel, dl, di, dj, slice(0, HALF)),
            lambda di, dj, dl: strided_window(hsel_other, dl, di, dj),
        ),
    )


def grad2(grad_t, grad_t_other, hsel, hsel_other):
    return call(
        grad2_kernel, "grad2", QUARTERS, [VM] * 4,
        [pltpu.VMEM((C, 2 * PRE_ROWS), BF)], 12, 1_000_000_000, 4_000_000,
    )(grad_t, grad_t_other, hsel, hsel_other)


def same_window(x3):
    def window(di, dj, dl):
        return x3[dl, pl.ds(di, EDGE), pl.ds(dj, EDGE)].reshape(ACT_ROWS, HALF)

    return window


def grad1_kernel(gat, gat_other, x3a, x3o, f0, f1, f2, f3, left):
    for n, part in enumerate((gat, gat_other)):
        for i in range(EDGE // 2):
            first = n * ACT_ROWS + 2 * i * EDGE * ROWS
            left[:, first : first + 2 * EDGE * ROWS] = part[i]
    windows = (same_window(x3a), same_window(x3o))
    grad_loop((f0, f1, f2, f3), left, windows)


def grad1(gat, gat_other, x3a, x3o):
    return call(
        grad1_kernel, "grad1", QUARTERS, [VM] * 4,
        [pltpu.VMEM((C, 2 * ACT_ROWS), BF)], 16, 4_000_000_000, 7_000_000,
    )(gat, gat_other, x3a, x3o)


SHARDS = (MEMBERS, 2 * TAPS, 2 * C)


def pack_kernel(first, second, order, out):
    perm = one_hot(order[...])
    for i in range(2):
        lanes = slice(i * C, (i + 1) * C)
        one = dot(first[:, lanes].astype(BF), perm)
        both = jnp.concatenate([one, second[:, lanes]], axis=0).astype(BF)
        for n in range(MEMBERS):
            out[n, :, lanes] = both


def pack(first, second, order):
    return call(
        pack_kernel, "pack", shape(SHARDS, BF), [VM] * 3, [], 56, 10_000_000, 1_000_000
    )(first, second, order)


def spread_kernel(shards, out1, out2, wide):
    for m in range(MEMBERS):
        rows = shards[m].astype(F32)
        for i in range(2):
            store(wide, 2 * m + i, 2 * TAPS, rows[:, i * C : (i + 1) * C], BLOCK)

    def step(t, carry):
        for k, out in enumerate((out1, out2)):
            start = pl.multiple_of((k * TAPS + t) * BLOCK, BLOCK)
            out[t] = load(wide, start, BLOCK).astype(BF)
        return carry

    lax.fori_loop(0, TAPS, step, 0)


def spread(shards):
    return call(
        spread_kernel, "spread", (shape(QUARTER, BF),) * 2, [VM],
        [pltpu.VMEM((2, 2 * TAPS * BLOCK, HALF), F32)], 8, 1_000_000, 2_000_000,
    )(shards)


def add_parts(p0, p1, p2, p3, wide):
    def step(t, carry):
        total = p0[t].astype(F32)
        for part in (p1, p2, p3):
            total = total + part[t].astype(F32)
        store(wide, pl.multiple_of(t * BLOCK, BLOCK), BLOCK, total)
        return carry

    lax.fori_loop(0, TAPS, step, 0)


def collect2(parts):
    return call(
        add_parts, "collect2", shape((2, TAPS * BLOCK, HALF), F32), [VM] * 4, [],
        4, 1_000_000, 3_000_000,
    )(*parts)


def collect_kernel(p0, p1, p2, p3, second, out, wide):
    wide[:, TAPS * BLOCK :] = second[...]
    add_parts(p0, p1, p2, p3, wide)
    for m in range(MEMBERS):
        for i in range(2):
            rows = load(wide, 2 * m + i, 2 * TAPS, BLOCK)
            out[m, :, i * C : (i + 1) * C] = rows.astype(BF)


def collect(parts, second):
    return call(
        collect_kernel, "collect", shape(SHARDS, BF), [VM] * 5,
        [pltpu.VMEM((2, 2 * TAPS * BLOCK, HALF), F32)], 8, 1_000_000, 3_000_000,
    )(*parts, second)


def adam_update(weight, first, second, grad):
    first_new = 0.9 * first + 0.1 * grad
    second_new = 0.999 * second + 0.001 * grad * grad
    fix_first = 1.0 - 0.9**10
    fix_second = 1.0 - 0.999**10
    weight_new = weight - 0.05 * (first_new / fix_first) / (
        jnp.sqrt(second_new / fix_second) + 1e-08
    )
    return (weight_new, first_new, second_new)


def adam_kernel(
    scale, parts, order, k1, m1, v1, k2, m2, v2, k1n, m1n, v1n, k2n, m2n, v2n
):
    back = one_hot(order[...]).astype(F32)
    for i in range(2):
        lanes = slice(i * C, (i + 1) * C)
        total = parts[0, :, lanes].astype(F32)
        for n in range(1, MEMBERS):
            total = total + parts[n, :, lanes].astype(F32)
        total = total * scale
        grad = lax.dot_general(
            total[:TAPS],
            back,
            (((1,), (1,)), ((), ())),
            precision=lax.Precision.HIGHEST,
            preferred_element_type=F32,
        )
        k1n[:, lanes], m1n[:, lanes], v1n[:, lanes] = adam_update(
            k1[:, lanes], m1[:, lanes], v1[:, lanes], grad
        )
        k2n[:, lanes], m2n[:, lanes], v2n[:, lanes] = adam_update(
            k2[:, lanes], m2[:, lanes], v2[:, lanes], total[TAPS:]
        )


def adam(scale, parts, order, *state):
    return call(
        functools.partial(adam_kernel, scale), "adam",
        (shape((TAPS, 2 * C), F32),) * 6, [VM] * 8, [], 6, 10_000_000, 1_000_000,
    )(parts, order, *state)


def place(x, y, z, c):
    return ((x * 4 + y) * 4 + z) * 2 + c


GRAY = [(0, 0), (1, 0), (1, 1), (0, 1)]
RING = {bits: at for at, bits in enumerate(GRAY)}


def label(bits):
    return bits[0] ^ 2 * bits[1] ^ 3 * bits[2]


def device(core, near, far):
    first, second = (near, far) if core == 0 else (far, near)
    return place(*(RING[pair] for pair in zip(first, second)), core)


TRIPLES = list(itertools.product(range(2), repeat=3))
DEVICES = list(itertools.product(range(2), TRIPLES, TRIPLES))


def turned(bits, which):
    return tuple(bit ^ (n in which) for n, bit in enumerate(bits))


NEIGHBOURS = [
    [(device(c, u, v), device(c, turned(u, (k,)), v)) for c, u, v in DEVICES] for k in range(3)
]
PARTNERS = [(n, n ^ 1) for n in range(128)]
FAR = [
    sorted(device(*d) for d in DEVICES if d[0] == c and label(d[1]) == l)
    for c in range(2)
    for l in range(4)
]


def tables():
    half = lambda c, l: [
        2 * member + i for k in range(4) for member in FAR[4 * c + (l ^ k)] for i in range(2)
    ]
    columns = half(0, 0) + half(1, 0)
    at = {channel: n for n, channel in enumerate(columns)}
    table = np.zeros((128, 2, 1, C), np.int32)
    for c, u, v in DEVICES:
        channels = half(c, label(u)) + half(1 - c, label(v))
        table[device(c, u, v), 0, 0] = channels
        table[device(c, u, v), 1, 0] = [at[channel] for channel in channels]
    return np.array(columns, np.int32).reshape(1, C), table


COLUMNS, TABLE = tables()


def exchange(value):
    return lax.all_to_all(value, "dp", 0, 0, axis_index_groups=FAR, tiled=True)


def swap(value):
    return lax.ppermute(value, "dp", PARTNERS)


def send_round(values):
    return [values[0]] + [lax.ppermute(v, "dp", to) for v, to in zip(values[1:], NEIGHBOURS)]


def after(value, *others):
    return lax.optimization_barrier((value, *others))[0]


def body(latent, out_grad, k1, m1, v1, k2, m2, v2):
    scale = 1.0 / (latent.shape[0] * lax.axis_size("dp"))
    table = lax.dynamic_index_in_dim(jnp.asarray(TABLE), lax.axis_index("dp"), keepdims=False)
    columns = jnp.asarray(COLUMNS)

    shards = exchange(pack(k1, k2, columns))
    latent = latent.transpose(1, 2, 3, 0, 4)
    cells = prep(latent, swap(latent), out_grad.transpose(1, 2, 3, 0, 4), table)
    shards, cells = lax.optimization_barrier((shards, cells))
    x3a, x3b, x3o, skip, cot = cells
    own1, own2 = spread(shards)
    own1 = send_round([own1] * 4)
    own2 = send_round([after(own2, *own1[1:])] * 4)
    other1 = [swap(value) for value in own1]
    other2 = [swap(value) for value in own2]

    act, hsel, hsend = conv1(x3b, conv1_own(x3a, own1), other1, table)
    hsel_other = swap(hsend)
    block_out, grad_pre, grad_pre_t = conv2(skip, cot, hsel, own2, other2)
    second = grad2(grad_pre_t, swap(grad_pre_t), hsel, hsel_other)
    grad_pre = after(grad_pre, *second)
    second = send_round(second)
    gat = back(act, grad_pre, own2, other2, table)
    first = send_round(grad1(gat, swap(gat), x3a, x3o))
    parts = exchange(collect(first, collect2(second)))
    new = adam(scale, parts, columns, k1, m1, v1, k2, m2, v2)
    return (block_out.transpose(3, 0, 1, 2, 4), *new)


def solution(mesh):
    wide = P("dp", None, None, None, None)
    flat = P(None, "dp")
    return jax.shard_map(
        body,
        mesh=mesh,
        in_specs=(wide, wide) + (flat,) * 6,
        out_specs=(wide,) + (flat,) * 6,
        check_vma=False,
    )
```

```python
import functools
import itertools

import jax
import jax.numpy as jnp
import numpy as np
from jax import lax
from jax.experimental import pallas as pl
from jax.experimental.pallas import tpu as pltpu
from jax.sharding import PartitionSpec as P

C = 256
HALF = 128
EDGE = 6
OUTER = 3
TAPS = 27
SAMP = 4
ROWS = 32
ACT_ROWS = EDGE * EDGE * ROWS
PAD_ROWS = 64 * ROWS
OUT_ROWS = 16
PRE_ROWS = 9 * OUT_ROWS
MEMBERS = 16
MIB = 1024 * 1024
BF = jnp.bfloat16
F32 = jnp.float32

GROUP = 6
BLOCK = 32
QUARTER = (TAPS, BLOCK, C)

VM = pl.BlockSpec(memory_space=pltpu.VMEM)


def shape(dims, dtype):
    return jax.ShapeDtypeStruct(dims, dtype)


def call(kernel, name, out_shape, in_specs, scratch, mib, flops, moved):
    single = not isinstance(out_shape, tuple)
    return pl.pallas_call(
        kernel,
        out_shape=out_shape,
        in_specs=in_specs,
        out_specs=VM if single else (VM,) * len(out_shape),
        scratch_shapes=scratch,
        compiler_params=pltpu.CompilerParams(vmem_limit_bytes=mib * MIB),
        cost_estimate=pl.CostEstimate(flops=flops, bytes_accessed=moved, transcendentals=0),
        name=name,
    )


def dot(a, b):
    return jnp.dot(a, b, preferred_element_type=F32)


def dot_t(a, b):
    return lax.dot_general(a, b, (((1,), (1,)), ((), ())), preferred_element_type=F32)


def sigmoid(v):
    return 1.0 / (1.0 + jnp.exp(-v))


def load(ref, start, count, stride=1):
    return jnp.concatenate(
        [ref[half, pl.ds(start, count, stride=stride), :] for half in range(2)], axis=1
    )


def store(ref, start, count, value, stride=1):
    for half in range(2):
        ref[half, pl.ds(start, count, stride=stride), :] = value[
            :, half * HALF : (half + 1) * HALF
        ]


def one_hot(order_row):
    return (lax.broadcasted_iota(jnp.int32, (C, C), 0) == order_row).astype(BF)


def fill_cells(source, xs):
    for i in range(EDGE):
        for j in range(EDGE):
            value = source[i, j].astype(F32)
            base = 8 + ((i + 1) * 8 + j + 1) * ROWS + 1
            for l in range(EDGE):
                store(xs, base + l, SAMP, value[l], 8)


def prep_kernel(latent, other, out_grad, table, x3a, x3b, x3o, skip, cot, xs, og):
    perm = one_hot(table[0])
    xs[...] = jnp.zeros_like(xs)
    og[...] = jnp.zeros_like(og)
    fill_cells(latent, xs)
    for qi in range(OUTER):
        for qj in range(OUTER):
            q = (qi * 3 + qj) * OUT_ROWS
            value = out_grad[qi, qj].astype(F32)
            for ql in range(OUTER):
                store(og, q + ql, SAMP, value[ql], 4)
            base = 8 + ((2 * qi + 1) * 8 + 2 * qj + 1) * ROWS + 1
            skip[q : q + OUT_ROWS, :] = load(xs, base, OUT_ROWS, 2)
    cot[...] = load(og, 0, PRE_ROWS)
    for i in range(8):
        for dl in range(3):
            rows = dot(load(xs, 7 + dl + i * 256, 256).astype(BF), perm).astype(BF)
            x3a[dl, i] = rows[:, :HALF].reshape(8, ROWS, HALF)
            x3b[dl, i] = rows[:, HALF:].reshape(8, ROWS, HALF)
    fill_cells(other, xs)
    for i in range(8):
        for dl in range(3):
            rows = dot(load(xs, 7 + dl + i * 256, 256).astype(BF), perm[:, :HALF])
            x3o[dl, i] = rows.astype(BF).reshape(8, ROWS, HALF)


def prep(latent, other, out_grad, table):
    wide = shape((3, 8, 8, ROWS, HALF), BF)
    pre = shape((PRE_ROWS, C), F32)
    return call(
        prep_kernel, "prep", (wide, wide, wide, pre, pre), [VM] * 4,
        [pltpu.VMEM((2, PAD_ROWS + 16, HALF), F32), pltpu.VMEM((2, PRE_ROWS, HALF), F32)],
        20, 2_000_000_000, 8_000_000,
    )(latent, other, out_grad, table)


def cell_mask():
    cell = lax.broadcasted_iota(jnp.int32, (EDGE * ROWS, C), 0) % 8
    return (cell >= 1) & (cell <= EDGE)


def half_weight(quarters, t):
    return jnp.concatenate([quarter[t] for quarter in quarters], axis=0)


def half_conv(x3, quarters, act, start):
    for first in range(0, TAPS, GROUP):
        taps = range(first, min(first + GROUP, TAPS))
        windows = [
            x3[t % 3, t // 9 : t // 9 + EDGE, t // 3 % 3 : t // 3 % 3 + EDGE] for t in taps
        ]
        total = dot(
            jnp.concatenate([window.reshape(ACT_ROWS, HALF) for window in windows], axis=1),
            jnp.concatenate([half_weight(quarters, t) for t in taps], axis=0),
        )
        before = act if first else start
        act[...] = total if before is None else before[...] + total


def conv1_own_kernel(x3a, q0, q1, q2, q3, act):
    half_conv(x3a, (q0, q1, q2, q3), act, None)


def conv1_own(x3a, own):
    return call(
        conv1_own_kernel, "conv1_own", shape((ACT_ROWS, C), F32), [VM] * 5,
        [], 12, 2_000_000_000, 5_000_000,
    )(x3a, *own)


def permuted(value, lanes):
    high = value.astype(BF)
    rest = value - high.astype(F32)
    middle = rest.astype(BF)
    low = (rest - middle.astype(F32)).astype(BF)
    return dot(high, lanes) + (dot(middle, lanes) + dot(low, lanes))


def conv1_kernel(x3b, part_act, q0, q1, q2, q3, table, act, hsel, hsend, hs):
    half_conv(x3b, (q0, q1, q2, q3), act, part_act)

    hsel[:, 0] = jnp.zeros_like(hsel[:, 0])
    hsel[:, :, 0] = jnp.zeros_like(hsel[:, :, 0])
    hsend[:, 0] = jnp.zeros_like(hsend[:, 0])
    hsend[:, :, 0] = jnp.zeros_like(hsend[:, :, 0])
    store(hs, ACT_ROWS, 8, jnp.zeros((8, C), F32))
    inside = cell_mask()
    lanes = one_hot(table[1])
    for i in range(EDGE):
        part = pl.ds(i * EDGE * ROWS, EDGE * ROWS)
        value = permuted(act[part, :], lanes)
        act[part, :] = value
        hidden = jnp.where(inside, value * sigmoid(value), 0.0)
        store(hs, i * EDGE * ROWS, EDGE * ROWS, hidden.astype(BF).astype(F32))
    for dl in range(3):
        for i in range(EDGE):
            rows = load(hs, i * EDGE * ROWS + dl, EDGE * OUT_ROWS, 2)
            rows = rows.astype(BF).reshape(EDGE, OUT_ROWS, C)
            hsel[dl, i + 1, 1:] = rows
            hsend[dl, i + 1, 1:] = rows[..., HALF:]


def conv1(x3b, part_act, other, table):
    return call(
        conv1_kernel, "conv1",
        (
            shape((ACT_ROWS, C), F32),
            shape((3, 7, 7, OUT_ROWS, C), BF),
            shape((3, 7, 7, OUT_ROWS, HALF), BF),
        ),
        [VM] * 7,
        [pltpu.VMEM((2, ACT_ROWS + 8, HALF), F32)],
        24, 2_000_000_000, 7_000_000,
    )(x3b, part_act, *other, table)


def strided_window(hsel, dl, di, dj, lanes=slice(None)):
    blocks = [
        hsel[dl, 2 * qi + di, 2 * qj + dj, :, lanes] for qi in range(OUTER) for qj in range(OUTER)
    ]
    return jnp.concatenate(blocks, axis=0)


def conv2_kernel(
    skip, cot, hsel, q0, q1, q2, q3, p0, p1, p2, p3, block_out, grad_pre, grad_pre_t, bo
):
    quarters = (q0, q1, q2, q3, p0, p1, p2, p3)
    pre = skip[...]
    for di in range(3):
        for dj in range(3):
            for dl in range(3):
                pre = pre + dot(
                    strided_window(hsel, dl, di, dj), half_weight(quarters, TAPS + di * 9 + dj * 3 + dl)
                )
    sigma = sigmoid(pre)
    store(bo, 0, PRE_ROWS, pre * sigma)
    for qi in range(OUTER):
        for qj in range(OUTER):
            for ql in range(OUTER):
                base = (qi * 3 + qj) * OUT_ROWS + ql
                block_out[qi, qj, ql] = load(bo, base, SAMP, 4).astype(BF)
    grad = (cot[...] * (sigma * (1.0 + pre * (1.0 - sigma)))).astype(BF)
    grad_pre[...] = grad
    grad_pre_t[...] = grad.astype(F32).T.astype(BF)


def conv2(skip, cot, hsel, own, other):
    return call(
        conv2_kernel, "conv2",
        (
            shape((OUTER, OUTER, OUTER, SAMP, C), BF),
            shape((PRE_ROWS, C), BF),
            shape((C, PRE_ROWS), BF),
        ),
        [VM] * 11,
        [pltpu.VMEM((2, PRE_ROWS, HALF), F32)],
        16, 1_500_000_000, 6_000_000,
    )(skip, cot, hsel, *own, *other)


def back_kernel(
    act, grad_pre, q0, q1, q2, q3, p0, p1, p2, p3, table, gat, y, gh
):
    quarters = (q0, q1, q2, q3, p0, p1, p2, p3)
    y[...] = jnp.zeros_like(y)
    grad = grad_pre[...]
    for di in range(3):
        for dj in range(3):
            for dl in range(3):
                term = dot_t(grad, half_weight(quarters, TAPS + di * 9 + dj * 3 + dl))
                term = term.reshape(9, OUT_ROWS, C)
                for qi in range(OUTER):
                    for qj in range(OUTER):
                        y[dl, 2 * qi + di, 2 * qj + dj] += term[qi * 3 + qj]
    store(gh, ACT_ROWS, 8, jnp.zeros((8, C), F32))
    count = EDGE * OUT_ROWS
    for i in range(EDGE):
        base = i * EDGE * ROWS
        store(gh, base, count, y[0, i + 1, 1:].reshape(count, C), 2)
        store(gh, base + 1, count, y[1, i + 1, 1:].reshape(count, C), 2)
    for i in range(EDGE):
        base = i * EDGE * ROWS + 2
        total = load(gh, base, count, 2) + y[2, i + 1, 1:].reshape(count, C)
        store(gh, base, count, total, 2)
    inside = cell_mask()
    lanes = one_hot(table[1])
    for i in range(0, EDGE, 2):
        grads = []
        for start in (i * EDGE * ROWS, (i + 1) * EDGE * ROWS):
            value = act[pl.ds(start, EDGE * ROWS), :]
            sigma = sigmoid(value)
            grad = load(gh, start, EDGE * ROWS) * (sigma * (1.0 + value * (1.0 - sigma)))
            grads.append(jnp.where(inside, grad, 0.0).astype(BF))
        gat[i // 2] = dot_t(lanes, jnp.concatenate(grads, axis=0)).astype(BF)


def back(act, grad_pre, own, other, table):
    return call(
        back_kernel, "back", shape((EDGE // 2, C, 2 * EDGE * ROWS), BF), [VM] * 11,
        [
            pltpu.VMEM((3, 7, 7, OUT_ROWS, C), F32),
            pltpu.VMEM((2, ACT_ROWS + 8, HALF), F32),
        ],
        16, 1_500_000_000, 8_000_000,
    )(act, grad_pre, *own, *other, table)


def grad_loop(quarters, left, windows):
    eye = (
        lax.broadcasted_iota(jnp.int32, (C, C), 0) == lax.broadcasted_iota(jnp.int32, (C, C), 1)
    ).astype(BF)

    def product(taps):
        right = [
            jnp.concatenate([window(t // 9, t // 3 % 3, t % 3) for t in taps], axis=1)
            for window in windows
        ]
        total = dot(left[...], jnp.concatenate(right, axis=0)).astype(BF)
        for n in range(0, len(taps), 2):
            two = taps[n : n + 2]
            width = HALF * len(two)
            turned = dot_t(eye[:width, :width], total[:, n * HALF : n * HALF + width]).astype(BF)
            for m, t in enumerate(two):
                for k, quarter in enumerate(quarters):
                    first = m * HALF + k * BLOCK
                    quarter[t] = turned[first : first + BLOCK]

    def step(n, carry):
        product([GROUP * n + k for k in range(GROUP)])
        return carry

    whole = TAPS // GROUP
    lax.fori_loop(0, whole, step, 0)
    product(list(range(GROUP * whole, TAPS)))


QUARTERS = (shape(QUARTER, BF),) * 4


def grad2_kernel(
    grad_t, grad_t_other, hsel, hsel_other, f0, f1, f2, f3, left
):
    left[:, :PRE_ROWS] = grad_t[...]
    left[:, PRE_ROWS:] = grad_t_other[...]
    grad_loop(
        (f0, f1, f2, f3),
        left,
        (
            lambda di, dj, dl: strided_window(hsel, dl, di, dj, slice(0, HALF)),
            lambda di, dj, dl: strided_window(hsel_other, dl, di, dj),
        ),
    )


def grad2(grad_t, grad_t_other, hsel, hsel_other):
    return call(
        grad2_kernel, "grad2", QUARTERS, [VM] * 4,
        [pltpu.VMEM((C, 2 * PRE_ROWS), BF)], 12, 1_000_000_000, 4_000_000,
    )(grad_t, grad_t_other, hsel, hsel_other)


def same_window(x3):
    def window(di, dj, dl):
        return x3[dl, pl.ds(di, EDGE), pl.ds(dj, EDGE)].reshape(ACT_ROWS, HALF)

    return window


def grad1_kernel(gat, gat_other, x3a, x3o, f0, f1, f2, f3, left):
    for n, part in enumerate((gat, gat_other)):
        for i in range(EDGE // 2):
            first = n * ACT_ROWS + 2 * i * EDGE * ROWS
            left[:, first : first + 2 * EDGE * ROWS] = part[i]
    windows = (same_window(x3a), same_window(x3o))
    grad_loop((f0, f1, f2, f3), left, windows)


def grad1(gat, gat_other, x3a, x3o):
    return call(
        grad1_kernel, "grad1", QUARTERS, [VM] * 4,
        [pltpu.VMEM((C, 2 * ACT_ROWS), BF)], 16, 4_000_000_000, 7_000_000,
    )(gat, gat_other, x3a, x3o)


SHARDS = (MEMBERS, 2 * TAPS, 2 * C)


def pack_kernel(first, second, order, out):
    perm = one_hot(order[...])
    for i in range(2):
        lanes = slice(i * C, (i + 1) * C)
        one = dot(first[:, lanes].astype(BF), perm)
        both = jnp.concatenate([one, second[:, lanes]], axis=0).astype(BF)
        for n in range(MEMBERS):
            out[n, :, lanes] = both


def pack(first, second, order):
    return call(
        pack_kernel, "pack", shape(SHARDS, BF), [VM] * 3, [], 56, 10_000_000, 1_000_000
    )(first, second, order)


def spread_kernel(shards, out, wide):
    for m in range(MEMBERS):
        rows = shards[m].astype(F32)
        for i in range(2):
            store(wide, 2 * m + i, 2 * TAPS, rows[:, i * C : (i + 1) * C], BLOCK)

    def step(t, carry):
        out[t] = load(wide, pl.multiple_of(t * BLOCK, BLOCK), BLOCK).astype(BF)
        return carry

    lax.fori_loop(0, 2 * TAPS, step, 0)


def spread(shards):
    return call(
        spread_kernel, "spread", shape((2 * TAPS, BLOCK, C), BF), [VM],
        [pltpu.VMEM((2, 2 * TAPS * BLOCK, HALF), F32)], 8, 1_000_000, 2_000_000,
    )(shards)


def add_parts(p0, p1, p2, p3, wide):
    def step(t, carry):
        total = p0[t].astype(F32)
        for part in (p1, p2, p3):
            total = total + part[t].astype(F32)
        store(wide, pl.multiple_of(t * BLOCK, BLOCK), BLOCK, total)
        return carry

    lax.fori_loop(0, TAPS, step, 0)


def collect2(parts):
    return call(
        add_parts, "collect2", shape((2, TAPS * BLOCK, HALF), F32), [VM] * 4, [],
        4, 1_000_000, 3_000_000,
    )(*parts)


def collect_kernel(p0, p1, p2, p3, second, out, wide):
    wide[:, TAPS * BLOCK :] = second[...]
    add_parts(p0, p1, p2, p3, wide)
    for m in range(MEMBERS):
        for i in range(2):
            rows = load(wide, 2 * m + i, 2 * TAPS, BLOCK)
            out[m, :, i * C : (i + 1) * C] = rows.astype(BF)


def collect(parts, second):
    return call(
        collect_kernel, "collect", shape(SHARDS, BF), [VM] * 5,
        [pltpu.VMEM((2, 2 * TAPS * BLOCK, HALF), F32)], 8, 1_000_000, 3_000_000,
    )(*parts, second)


def adam_update(weight, first, second, grad):
    first_new = 0.9 * first + 0.1 * grad
    second_new = 0.999 * second + 0.001 * grad * grad
    fix_first = 1.0 - 0.9**10
    fix_second = 1.0 - 0.999**10
    weight_new = weight - 0.05 * (first_new / fix_first) / (
        jnp.sqrt(second_new / fix_second) + 1e-08
    )
    return (weight_new, first_new, second_new)


def adam_kernel(
    scale, parts, order, k1, m1, v1, k2, m2, v2, k1n, m1n, v1n, k2n, m2n, v2n
):
    back = one_hot(order[...]).astype(F32)
    for i in range(2):
        lanes = slice(i * C, (i + 1) * C)
        total = parts[0, :, lanes].astype(F32)
        for n in range(1, MEMBERS):
            total = total + parts[n, :, lanes].astype(F32)
        total = total * scale
        grad = lax.dot_general(
            total[:TAPS],
            back,
            (((1,), (1,)), ((), ())),
            precision=lax.Precision.HIGHEST,
            preferred_element_type=F32,
        )
        k1n[:, lanes], m1n[:, lanes], v1n[:, lanes] = adam_update(
            k1[:, lanes], m1[:, lanes], v1[:, lanes], grad
        )
        k2n[:, lanes], m2n[:, lanes], v2n[:, lanes] = adam_update(
            k2[:, lanes], m2[:, lanes], v2[:, lanes], total[TAPS:]
        )


def adam(scale, parts, order, *state):
    return call(
        functools.partial(adam_kernel, scale), "adam",
        (shape((TAPS, 2 * C), F32),) * 6, [VM] * 8, [], 6, 10_000_000, 1_000_000,
    )(parts, order, *state)


def place(x, y, z, c):
    return ((x * 4 + y) * 4 + z) * 2 + c


GRAY = [(0, 0), (1, 0), (1, 1), (0, 1)]
RING = {bits: at for at, bits in enumerate(GRAY)}


def label(bits):
    return bits[0] ^ 2 * bits[1] ^ 3 * bits[2]


def device(core, near, far):
    first, second = (near, far) if core == 0 else (far, near)
    return place(*(RING[pair] for pair in zip(first, second)), core)


TRIPLES = list(itertools.product(range(2), repeat=3))
DEVICES = list(itertools.product(range(2), TRIPLES, TRIPLES))


def turned(bits, which):
    return tuple(bit ^ (n in which) for n, bit in enumerate(bits))


NEIGHBOURS = [
    [(device(c, u, v), device(c, turned(u, (k,)), v)) for c, u, v in DEVICES] for k in range(3)
]
PARTNERS = [(n, n ^ 1) for n in range(128)]
FAR = [
    sorted(device(*d) for d in DEVICES if d[0] == c and label(d[1]) == l)
    for c in range(2)
    for l in range(4)
]


def tables():
    half = lambda c, l: [
        2 * member + i for k in range(4) for member in FAR[4 * c + (l ^ k)] for i in range(2)
    ]
    columns = half(0, 0) + half(1, 0)
    at = {channel: n for n, channel in enumerate(columns)}
    table = np.zeros((128, 2, 1, C), np.int32)
    for c, u, v in DEVICES:
        channels = half(c, label(u)) + half(1 - c, label(v))
        table[device(c, u, v), 0, 0] = channels
        table[device(c, u, v), 1, 0] = [at[channel] for channel in channels]
    return np.array(columns, np.int32).reshape(1, C), table


COLUMNS, TABLE = tables()


def exchange(value):
    return lax.all_to_all(value, "dp", 0, 0, axis_index_groups=FAR, tiled=True)


def swap(value):
    return lax.ppermute(value, "dp", PARTNERS)


def send_round(values):
    return [values[0]] + [lax.ppermute(v, "dp", to) for v, to in zip(values[1:], NEIGHBOURS)]


def after(value, *others):
    return lax.optimization_barrier((value, *others))[0]


def body(latent, out_grad, k1, m1, v1, k2, m2, v2):
    scale = 1.0 / (latent.shape[0] * lax.axis_size("dp"))
    table = lax.dynamic_index_in_dim(jnp.asarray(TABLE), lax.axis_index("dp"), keepdims=False)
    columns = jnp.asarray(COLUMNS)

    shards = exchange(pack(k1, k2, columns))
    latent = latent.transpose(1, 2, 3, 0, 4)
    other = swap(latent)
    own = spread(shards)
    latent = after(latent, own)
    cells = prep(latent, other, out_grad.transpose(1, 2, 3, 0, 4), table)
    own = send_round([own] * 4)
    other, own[1:], cells = lax.optimization_barrier((swap(own[0]), own[1:], cells))
    other = [other] + [swap(value) for value in own[1:]]
    x3a, x3b, x3o, skip, cot = cells

    act, hsel, hsend = conv1(x3b, conv1_own(x3a, own), other, table)
    hsel_other = swap(hsend)
    block_out, grad_pre, grad_pre_t = conv2(skip, cot, hsel, own, other)
    grad_pre_t_other = swap(grad_pre_t)
    gat = back(act, grad_pre, own, other, table)
    gat_other = swap(gat)
    second = grad2(grad_pre_t, grad_pre_t_other, hsel, hsel_other)
    gat = after(gat, *second)
    second = send_round(second)
    first = send_round(grad1(gat, gat_other, x3a, x3o))
    parts = exchange(collect(first, collect2(second)))
    new = adam(scale, parts, columns, k1, m1, v1, k2, m2, v2)
    return (block_out.transpose(3, 0, 1, 2, 4), *new)


def solution(mesh):
    wide = P("dp", None, None, None, None)
    flat = P(None, "dp")
    return jax.shard_map(
        body,
        mesh=mesh,
        in_specs=(wide, wide) + (flat,) * 6,
        out_specs=(wide,) + (flat,) * 6,
        check_vma=False,
    )
```

```python
import functools
import itertools

import jax
import jax.numpy as jnp
import numpy as np
from jax import lax
from jax.experimental import pallas as pl
from jax.experimental.pallas import tpu as pltpu
from jax.sharding import PartitionSpec as P

C = 256
HALF = 128
EDGE = 6
OUTER = 3
TAPS = 27
SAMP = 4
ROWS = 32
ACT_ROWS = EDGE * EDGE * ROWS
PAD_ROWS = 64 * ROWS
OUT_ROWS = 16
PRE_ROWS = 9 * OUT_ROWS
MEMBERS = 16
MIB = 1024 * 1024
BF = jnp.bfloat16
F32 = jnp.float32

GROUP = 6
BLOCK = 32
QUARTER = (TAPS, BLOCK, C)

VM = pl.BlockSpec(memory_space=pltpu.VMEM)


def shape(dims, dtype):
    return jax.ShapeDtypeStruct(dims, dtype)


def call(kernel, name, out_shape, in_specs, scratch, mib, flops, moved):
    single = not isinstance(out_shape, tuple)
    return pl.pallas_call(
        kernel,
        out_shape=out_shape,
        in_specs=in_specs,
        out_specs=VM if single else (VM,) * len(out_shape),
        scratch_shapes=scratch,
        compiler_params=pltpu.CompilerParams(vmem_limit_bytes=mib * MIB),
        cost_estimate=pl.CostEstimate(flops=flops, bytes_accessed=moved, transcendentals=0),
        name=name,
    )


def dot(a, b):
    return jnp.dot(a, b, preferred_element_type=F32)


def dot_t(a, b):
    return lax.dot_general(a, b, (((1,), (1,)), ((), ())), preferred_element_type=F32)


def sigmoid(v):
    return 1.0 / (1.0 + jnp.exp(-v))


def load(ref, start, count, stride=1):
    return jnp.concatenate(
        [ref[half, pl.ds(start, count, stride=stride), :] for half in range(2)], axis=1
    )


def store(ref, start, count, value, stride=1):
    for half in range(2):
        ref[half, pl.ds(start, count, stride=stride), :] = value[
            :, half * HALF : (half + 1) * HALF
        ]


def one_hot(order_row):
    return (lax.broadcasted_iota(jnp.int32, (C, C), 0) == order_row).astype(BF)


def fill_cells(source, xs):
    for i in range(EDGE):
        for j in range(EDGE):
            value = source[i, j].astype(F32)
            base = 8 + ((i + 1) * 8 + j + 1) * ROWS + 1
            for l in range(EDGE):
                store(xs, base + l, SAMP, value[l], 8)


def prep_kernel(latent, other, out_grad, table, x3a, x3b, x3o, skip, cot, xs, og):
    perm = one_hot(table[0])
    xs[...] = jnp.zeros_like(xs)
    og[...] = jnp.zeros_like(og)
    fill_cells(latent, xs)
    for qi in range(OUTER):
        for qj in range(OUTER):
            q = (qi * 3 + qj) * OUT_ROWS
            value = out_grad[qi, qj].astype(F32)
            for ql in range(OUTER):
                store(og, q + ql, SAMP, value[ql], 4)
            base = 8 + ((2 * qi + 1) * 8 + 2 * qj + 1) * ROWS + 1
            skip[q : q + OUT_ROWS, :] = load(xs, base, OUT_ROWS, 2)
    cot[...] = load(og, 0, PRE_ROWS)
    for i in range(8):
        for dl in range(3):
            rows = dot(load(xs, 7 + dl + i * 256, 256).astype(BF), perm).astype(BF)
            x3a[dl, i] = rows[:, :HALF].reshape(8, ROWS, HALF)
            x3b[dl, i] = rows[:, HALF:].reshape(8, ROWS, HALF)
    fill_cells(other, xs)
    for i in range(8):
        for dl in range(3):
            rows = dot(load(xs, 7 + dl + i * 256, 256).astype(BF), perm[:, :HALF])
            x3o[dl, i] = rows.astype(BF).reshape(8, ROWS, HALF)


def prep(latent, other, out_grad, table):
    wide = shape((3, 8, 8, ROWS, HALF), BF)
    pre = shape((PRE_ROWS, C), F32)
    return call(
        prep_kernel, "prep", (wide, wide, wide, pre, pre), [VM] * 4,
        [pltpu.VMEM((2, PAD_ROWS + 16, HALF), F32), pltpu.VMEM((2, PRE_ROWS, HALF), F32)],
        20, 2_000_000_000, 8_000_000,
    )(latent, other, out_grad, table)


def cell_mask():
    cell = lax.broadcasted_iota(jnp.int32, (EDGE * ROWS, C), 0) % 8
    return (cell >= 1) & (cell <= EDGE)


def half_weight(quarters, t):
    return jnp.concatenate([quarter[t] for quarter in quarters], axis=0)


def half_conv(x3, quarters, act, start):
    for first in range(0, TAPS, GROUP):
        taps = range(first, min(first + GROUP, TAPS))
        windows = [
            x3[t % 3, t // 9 : t // 9 + EDGE, t // 3 % 3 : t // 3 % 3 + EDGE] for t in taps
        ]
        total = dot(
            jnp.concatenate([window.reshape(ACT_ROWS, HALF) for window in windows], axis=1),
            jnp.concatenate([half_weight(quarters, t) for t in taps], axis=0),
        )
        before = act if first else start
        act[...] = total if before is None else before[...] + total


def conv1_own_kernel(x3a, q0, q1, q2, q3, act):
    half_conv(x3a, (q0, q1, q2, q3), act, None)


def conv1_own(x3a, own):
    return call(
        conv1_own_kernel, "conv1_own", shape((ACT_ROWS, C), F32), [VM] * 5,
        [], 12, 2_000_000_000, 5_000_000,
    )(x3a, *own)


def permuted(value, lanes):
    high = value.astype(BF)
    rest = value - high.astype(F32)
    middle = rest.astype(BF)
    low = (rest - middle.astype(F32)).astype(BF)
    return dot(high, lanes) + (dot(middle, lanes) + dot(low, lanes))


def conv1_kernel(x3b, part_act, q0, q1, q2, q3, table, act, hsel, hsend, hs):
    half_conv(x3b, (q0, q1, q2, q3), act, part_act)

    hsel[:, 0] = jnp.zeros_like(hsel[:, 0])
    hsel[:, :, 0] = jnp.zeros_like(hsel[:, :, 0])
    hsend[:, 0] = jnp.zeros_like(hsend[:, 0])
    hsend[:, :, 0] = jnp.zeros_like(hsend[:, :, 0])
    store(hs, ACT_ROWS, 8, jnp.zeros((8, C), F32))
    inside = cell_mask()
    lanes = one_hot(table[1])
    for i in range(EDGE):
        part = pl.ds(i * EDGE * ROWS, EDGE * ROWS)
        value = permuted(act[part, :], lanes)
        act[part, :] = value
        hidden = jnp.where(inside, value * sigmoid(value), 0.0)
        store(hs, i * EDGE * ROWS, EDGE * ROWS, hidden.astype(BF).astype(F32))
    for dl in range(3):
        for i in range(EDGE):
            rows = load(hs, i * EDGE * ROWS + dl, EDGE * OUT_ROWS, 2)
            rows = rows.astype(BF).reshape(EDGE, OUT_ROWS, C)
            hsel[dl, i + 1, 1:] = rows
            hsend[dl, i + 1, 1:] = rows[..., HALF:]


def conv1(x3b, part_act, other, table):
    return call(
        conv1_kernel, "conv1",
        (
            shape((ACT_ROWS, C), F32),
            shape((3, 7, 7, OUT_ROWS, C), BF),
            shape((3, 7, 7, OUT_ROWS, HALF), BF),
        ),
        [VM] * 7,
        [pltpu.VMEM((2, ACT_ROWS + 8, HALF), F32)],
        24, 2_000_000_000, 7_000_000,
    )(x3b, part_act, *other, table)


def strided_window(hsel, dl, di, dj, lanes=slice(None)):
    blocks = [
        hsel[dl, 2 * qi + di, 2 * qj + dj, :, lanes] for qi in range(OUTER) for qj in range(OUTER)
    ]
    return jnp.concatenate(blocks, axis=0)


def conv2_kernel(
    skip, cot, hsel, q0, q1, q2, q3, p0, p1, p2, p3, block_out, grad_pre, grad_pre_t, bo
):
    quarters = (q0, q1, q2, q3, p0, p1, p2, p3)
    pre = skip[...]
    for di in range(3):
        for dj in range(3):
            for dl in range(3):
                pre = pre + dot(
                    strided_window(hsel, dl, di, dj), half_weight(quarters, TAPS + di * 9 + dj * 3 + dl)
                )
    sigma = sigmoid(pre)
    store(bo, 0, PRE_ROWS, pre * sigma)
    for qi in range(OUTER):
        for qj in range(OUTER):
            for ql in range(OUTER):
                base = (qi * 3 + qj) * OUT_ROWS + ql
                block_out[qi, qj, ql] = load(bo, base, SAMP, 4).astype(BF)
    grad = (cot[...] * (sigma * (1.0 + pre * (1.0 - sigma)))).astype(BF)
    grad_pre[...] = grad
    grad_pre_t[...] = grad.astype(F32).T.astype(BF)


def conv2(skip, cot, hsel, own, other):
    return call(
        conv2_kernel, "conv2",
        (
            shape((OUTER, OUTER, OUTER, SAMP, C), BF),
            shape((PRE_ROWS, C), BF),
            shape((C, PRE_ROWS), BF),
        ),
        [VM] * 11,
        [pltpu.VMEM((2, PRE_ROWS, HALF), F32)],
        16, 1_500_000_000, 6_000_000,
    )(skip, cot, hsel, *own, *other)


def back_kernel(
    act, grad_pre, q0, q1, q2, q3, p0, p1, p2, p3, table, gat, y, gh
):
    quarters = (q0, q1, q2, q3, p0, p1, p2, p3)
    y[...] = jnp.zeros_like(y)
    grad = grad_pre[...]
    for di in range(3):
        for dj in range(3):
            for dl in range(3):
                term = dot_t(grad, half_weight(quarters, TAPS + di * 9 + dj * 3 + dl))
                term = term.reshape(9, OUT_ROWS, C)
                for qi in range(OUTER):
                    for qj in range(OUTER):
                        y[dl, 2 * qi + di, 2 * qj + dj] += term[qi * 3 + qj]
    store(gh, ACT_ROWS, 8, jnp.zeros((8, C), F32))
    count = EDGE * OUT_ROWS
    for i in range(EDGE):
        base = i * EDGE * ROWS
        store(gh, base, count, y[0, i + 1, 1:].reshape(count, C), 2)
        store(gh, base + 1, count, y[1, i + 1, 1:].reshape(count, C), 2)
    for i in range(EDGE):
        base = i * EDGE * ROWS + 2
        total = load(gh, base, count, 2) + y[2, i + 1, 1:].reshape(count, C)
        store(gh, base, count, total, 2)
    inside = cell_mask()
    lanes = one_hot(table[1])
    for i in range(0, EDGE, 2):
        grads = []
        for start in (i * EDGE * ROWS, (i + 1) * EDGE * ROWS):
            value = act[pl.ds(start, EDGE * ROWS), :]
            sigma = sigmoid(value)
            grad = load(gh, start, EDGE * ROWS) * (sigma * (1.0 + value * (1.0 - sigma)))
            grads.append(jnp.where(inside, grad, 0.0).astype(BF))
        gat[i // 2] = dot_t(lanes, jnp.concatenate(grads, axis=0)).astype(BF)


def back(act, grad_pre, own, other, table):
    return call(
        back_kernel, "back", shape((EDGE // 2, C, 2 * EDGE * ROWS), BF), [VM] * 11,
        [
            pltpu.VMEM((3, 7, 7, OUT_ROWS, C), F32),
            pltpu.VMEM((2, ACT_ROWS + 8, HALF), F32),
        ],
        16, 1_500_000_000, 8_000_000,
    )(act, grad_pre, *own, *other, table)


def grad_loop(quarters, left, windows):
    eye = (
        lax.broadcasted_iota(jnp.int32, (C, C), 0) == lax.broadcasted_iota(jnp.int32, (C, C), 1)
    ).astype(BF)

    def product(taps):
        right = [
            jnp.concatenate([window(t // 9, t // 3 % 3, t % 3) for t in taps], axis=1)
            for window in windows
        ]
        total = dot(left[...], jnp.concatenate(right, axis=0)).astype(BF)
        for n in range(0, len(taps), 2):
            two = taps[n : n + 2]
            width = HALF * len(two)
            turned = dot_t(eye[:width, :width], total[:, n * HALF : n * HALF + width]).astype(BF)
            for m, t in enumerate(two):
                for k, quarter in enumerate(quarters):
                    first = m * HALF + k * BLOCK
                    quarter[t] = turned[first : first + BLOCK]

    def step(n, carry):
        product([GROUP * n + k for k in range(GROUP)])
        return carry

    whole = TAPS // GROUP
    lax.fori_loop(0, whole, step, 0)
    product(list(range(GROUP * whole, TAPS)))


QUARTERS = (shape(QUARTER, BF),) * 4


def grad2_kernel(
    grad_t, grad_t_other, hsel, hsel_other, f0, f1, f2, f3, left
):
    left[:, :PRE_ROWS] = grad_t[...]
    left[:, PRE_ROWS:] = grad_t_other[...]
    grad_loop(
        (f0, f1, f2, f3),
        left,
        (
            lambda di, dj, dl: strided_window(hsel, dl, di, dj, slice(0, HALF)),
            lambda di, dj, dl: strided_window(hsel_other, dl, di, dj),
        ),
    )


def grad2(grad_t, grad_t_other, hsel, hsel_other):
    return call(
        grad2_kernel, "grad2", QUARTERS, [VM] * 4,
        [pltpu.VMEM((C, 2 * PRE_ROWS), BF)], 12, 1_000_000_000, 4_000_000,
    )(grad_t, grad_t_other, hsel, hsel_other)


def same_window(x3):
    def window(di, dj, dl):
        return x3[dl, pl.ds(di, EDGE), pl.ds(dj, EDGE)].reshape(ACT_ROWS, HALF)

    return window


def grad1_kernel(gat, gat_other, x3a, x3o, f0, f1, f2, f3, left):
    for n, part in enumerate((gat, gat_other)):
        for i in range(EDGE // 2):
            first = n * ACT_ROWS + 2 * i * EDGE * ROWS
            left[:, first : first + 2 * EDGE * ROWS] = part[i]
    windows = (same_window(x3a), same_window(x3o))
    grad_loop((f0, f1, f2, f3), left, windows)


def grad1(gat, gat_other, x3a, x3o):
    return call(
        grad1_kernel, "grad1", QUARTERS, [VM] * 4,
        [pltpu.VMEM((C, 2 * ACT_ROWS), BF)], 16, 4_000_000_000, 7_000_000,
    )(gat, gat_other, x3a, x3o)


SHARDS = (MEMBERS, 2 * TAPS, 2 * C)


def pack_kernel(first, second, order, out):
    perm = one_hot(order[...])
    for i in range(2):
        lanes = slice(i * C, (i + 1) * C)
        one = dot(first[:, lanes].astype(BF), perm)
        both = jnp.concatenate([one, second[:, lanes]], axis=0).astype(BF)
        for n in range(MEMBERS):
            out[n, :, lanes] = both


def pack(first, second, order):
    return call(
        pack_kernel, "pack", shape(SHARDS, BF), [VM] * 3, [], 56, 10_000_000, 1_000_000
    )(first, second, order)


def spread_kernel(shards, out, wide):
    for m in range(MEMBERS):
        rows = shards[m].astype(F32)
        for i in range(2):
            store(wide, 2 * m + i, 2 * TAPS, rows[:, i * C : (i + 1) * C], BLOCK)

    def step(t, carry):
        out[t] = load(wide, pl.multiple_of(t * BLOCK, BLOCK), BLOCK).astype(BF)
        return carry

    lax.fori_loop(0, 2 * TAPS, step, 0)


def spread(shards):
    return call(
        spread_kernel, "spread", shape((2 * TAPS, BLOCK, C), BF), [VM],
        [pltpu.VMEM((2, 2 * TAPS * BLOCK, HALF), F32)], 8, 1_000_000, 2_000_000,
    )(shards)


def add_parts(p0, p1, p2, p3, wide):
    def step(t, carry):
        total = p0[t].astype(F32)
        for part in (p1, p2, p3):
            total = total + part[t].astype(F32)
        store(wide, pl.multiple_of(t * BLOCK, BLOCK), BLOCK, total)
        return carry

    lax.fori_loop(0, TAPS, step, 0)


def collect2(parts):
    return call(
        add_parts, "collect2", shape((2, TAPS * BLOCK, HALF), F32), [VM] * 4, [],
        4, 1_000_000, 3_000_000,
    )(*parts)


def collect_kernel(p0, p1, p2, p3, second, out, wide):
    wide[:, TAPS * BLOCK :] = second[...]
    add_parts(p0, p1, p2, p3, wide)
    for m in range(MEMBERS):
        for i in range(2):
            rows = load(wide, 2 * m + i, 2 * TAPS, BLOCK)
            out[m, :, i * C : (i + 1) * C] = rows.astype(BF)


def collect(parts, second):
    return call(
        collect_kernel, "collect", shape(SHARDS, BF), [VM] * 5,
        [pltpu.VMEM((2, 2 * TAPS * BLOCK, HALF), F32)], 8, 1_000_000, 3_000_000,
    )(*parts, second)


def adam_update(weight, first, second, grad):
    first_new = 0.9 * first + 0.1 * grad
    second_new = 0.999 * second + 0.001 * grad * grad
    fix_first = 1.0 - 0.9**10
    fix_second = 1.0 - 0.999**10
    weight_new = weight - 0.05 * (first_new / fix_first) / (
        jnp.sqrt(second_new / fix_second) + 1e-08
    )
    return (weight_new, first_new, second_new)


def adam_kernel(
    scale, parts, order, k1, m1, v1, k2, m2, v2, k1n, m1n, v1n, k2n, m2n, v2n
):
    back = one_hot(order[...]).astype(F32)
    for i in range(2):
        lanes = slice(i * C, (i + 1) * C)
        total = parts[0, :, lanes].astype(F32)
        for n in range(1, MEMBERS):
            total = total + parts[n, :, lanes].astype(F32)
        total = total * scale
        grad = lax.dot_general(
            total[:TAPS],
            back,
            (((1,), (1,)), ((), ())),
            precision=lax.Precision.HIGHEST,
            preferred_element_type=F32,
        )
        k1n[:, lanes], m1n[:, lanes], v1n[:, lanes] = adam_update(
            k1[:, lanes], m1[:, lanes], v1[:, lanes], grad
        )
        k2n[:, lanes], m2n[:, lanes], v2n[:, lanes] = adam_update(
            k2[:, lanes], m2[:, lanes], v2[:, lanes], total[TAPS:]
        )


def adam(scale, parts, order, *state):
    return call(
        functools.partial(adam_kernel, scale), "adam",
        (shape((TAPS, 2 * C), F32),) * 6, [VM] * 8, [], 6, 10_000_000, 1_000_000,
    )(parts, order, *state)


def place(x, y, z, c):
    return ((x * 4 + y) * 4 + z) * 2 + c


GRAY = [(0, 0), (1, 0), (1, 1), (0, 1)]
RING = {bits: at for at, bits in enumerate(GRAY)}


def label(bits):
    return bits[0] ^ 2 * bits[1] ^ 3 * bits[2]


def device(core, near, far):
    first, second = (near, far) if core == 0 else (far, near)
    return place(*(RING[pair] for pair in zip(first, second)), core)


TRIPLES = list(itertools.product(range(2), repeat=3))
DEVICES = list(itertools.product(range(2), TRIPLES, TRIPLES))


def turned(bits, which):
    return tuple(bit ^ (n in which) for n, bit in enumerate(bits))


NEIGHBOURS = [
    [(device(c, u, v), device(c, turned(u, (k,)), v)) for c, u, v in DEVICES] for k in range(3)
]
PARTNERS = [(n, n ^ 1) for n in range(128)]
FAR = [
    sorted(device(*d) for d in DEVICES if d[0] == c and label(d[1]) == l)
    for c in range(2)
    for l in range(4)
]


def tables():
    half = lambda c, l: [
        2 * member + i for k in range(4) for member in FAR[4 * c + (l ^ k)] for i in range(2)
    ]
    columns = half(0, 0) + half(1, 0)
    at = {channel: n for n, channel in enumerate(columns)}
    table = np.zeros((128, 2, 1, C), np.int32)
    for c, u, v in DEVICES:
        channels = half(c, label(u)) + half(1 - c, label(v))
        table[device(c, u, v), 0, 0] = channels
        table[device(c, u, v), 1, 0] = [at[channel] for channel in channels]
    return np.array(columns, np.int32).reshape(1, C), table


COLUMNS, TABLE = tables()


def exchange(value):
    return lax.all_to_all(value, "dp", 0, 0, axis_index_groups=FAR, tiled=True)


def swap(value):
    return lax.ppermute(value, "dp", PARTNERS)


def send_round(values):
    return [values[0]] + [lax.ppermute(v, "dp", to) for v, to in zip(values[1:], NEIGHBOURS)]


def after(value, *others):
    return lax.optimization_barrier((value, *others))[0]


def body(latent, out_grad, k1, m1, v1, k2, m2, v2):
    scale = 1.0 / (latent.shape[0] * lax.axis_size("dp"))
    table = lax.dynamic_index_in_dim(jnp.asarray(TABLE), lax.axis_index("dp"), keepdims=False)
    columns = jnp.asarray(COLUMNS)

    shards = exchange(pack(k1, k2, columns))
    latent = latent.transpose(1, 2, 3, 0, 4)
    other = swap(latent)
    own = spread(shards)
    latent = after(latent, own)
    cells = prep(latent, other, out_grad.transpose(1, 2, 3, 0, 4), table)
    own = send_round([own] * 4)
    own[1:], cells = lax.optimization_barrier((own[1:], cells))
    other = [swap(value) for value in own]
    x3a, x3b, x3o, skip, cot = cells

    act, hsel, hsend = conv1(x3b, conv1_own(x3a, own), other, table)
    hsel_other = swap(hsend)
    block_out, grad_pre, grad_pre_t = conv2(skip, cot, hsel, own, other)
    grad_pre_t_other = swap(grad_pre_t)
    gat = back(act, grad_pre, own, other, table)
    gat_other = swap(gat)
    second = grad2(grad_pre_t, grad_pre_t_other, hsel, hsel_other)
    gat = after(gat, *second)
    second = send_round(second)
    first = send_round(grad1(gat, gat_other, x3a, x3o))
    parts = exchange(collect(first, collect2(second)))
    new = adam(scale, parts, columns, k1, m1, v1, k2, m2, v2)
    return (block_out.transpose(3, 0, 1, 2, 4), *new)


def solution(mesh):
    wide = P("dp", None, None, None, None)
    flat = P(None, "dp")
    return jax.shard_map(
        body,
        mesh=mesh,
        in_specs=(wide, wide) + (flat,) * 6,
        out_specs=(wide,) + (flat,) * 6,
        check_vma=False,
    )
```

```python
import functools
import itertools

import jax
import jax.numpy as jnp
import numpy as np
from jax import lax
from jax.experimental import pallas as pl
from jax.experimental.pallas import tpu as pltpu
from jax.sharding import PartitionSpec as P

C = 256
HALF = 128
EDGE = 6
OUTER = 3
TAPS = 27
SAMP = 4
ROWS = 32
ACT_ROWS = EDGE * EDGE * ROWS
PAD_ROWS = 64 * ROWS
OUT_ROWS = 16
PRE_ROWS = 9 * OUT_ROWS
MEMBERS = 16
MIB = 1024 * 1024
BF = jnp.bfloat16
F32 = jnp.float32

GROUP = 6
BLOCK = 32
QUARTER = (TAPS, BLOCK, C)

VM = pl.BlockSpec(memory_space=pltpu.VMEM)


def shape(dims, dtype):
    return jax.ShapeDtypeStruct(dims, dtype)


def call(kernel, name, out_shape, in_specs, scratch, mib, flops, moved):
    single = not isinstance(out_shape, tuple)
    return pl.pallas_call(
        kernel,
        out_shape=out_shape,
        in_specs=in_specs,
        out_specs=VM if single else (VM,) * len(out_shape),
        scratch_shapes=scratch,
        compiler_params=pltpu.CompilerParams(vmem_limit_bytes=mib * MIB),
        cost_estimate=pl.CostEstimate(flops=flops, bytes_accessed=moved, transcendentals=0),
        name=name,
    )


def dot(a, b):
    return jnp.dot(a, b, preferred_element_type=F32)


def dot_t(a, b):
    return lax.dot_general(a, b, (((1,), (1,)), ((), ())), preferred_element_type=F32)


def sigmoid(v):
    return 1.0 / (1.0 + jnp.exp(-v))


def load(ref, start, count, stride=1):
    return jnp.concatenate(
        [ref[half, pl.ds(start, count, stride=stride), :] for half in range(2)], axis=1
    )


def store(ref, start, count, value, stride=1):
    for half in range(2):
        ref[half, pl.ds(start, count, stride=stride), :] = value[
            :, half * HALF : (half + 1) * HALF
        ]


def one_hot(order_row):
    return (lax.broadcasted_iota(jnp.int32, (C, C), 0) == order_row).astype(BF)


def fill_cells(source, xs):
    for i in range(EDGE):
        for j in range(EDGE):
            value = source[i, j].astype(F32)
            base = 8 + ((i + 1) * 8 + j + 1) * ROWS + 1
            for l in range(EDGE):
                store(xs, base + l, SAMP, value[l], 8)


def prep_kernel(latent, other, out_grad, table, x3a, x3b, x3o, skip, cot, xs, og):
    perm = one_hot(table[0])
    xs[...] = jnp.zeros_like(xs)
    og[...] = jnp.zeros_like(og)
    fill_cells(latent, xs)
    for qi in range(OUTER):
        for qj in range(OUTER):
            q = (qi * 3 + qj) * OUT_ROWS
            value = out_grad[qi, qj].astype(F32)
            for ql in range(OUTER):
                store(og, q + ql, SAMP, value[ql], 4)
            base = 8 + ((2 * qi + 1) * 8 + 2 * qj + 1) * ROWS + 1
            skip[q : q + OUT_ROWS, :] = load(xs, base, OUT_ROWS, 2)
    cot[...] = load(og, 0, PRE_ROWS)
    for i in range(8):
        for dl in range(3):
            rows = dot(load(xs, 7 + dl + i * 256, 256).astype(BF), perm).astype(BF)
            x3a[dl, i] = rows[:, :HALF].reshape(8, ROWS, HALF)
            x3b[dl, i] = rows[:, HALF:].reshape(8, ROWS, HALF)
    fill_cells(other, xs)
    for i in range(8):
        for dl in range(3):
            rows = dot(load(xs, 7 + dl + i * 256, 256).astype(BF), perm[:, :HALF])
            x3o[dl, i] = rows.astype(BF).reshape(8, ROWS, HALF)


def prep(latent, other, out_grad, table):
    wide = shape((3, 8, 8, ROWS, HALF), BF)
    pre = shape((PRE_ROWS, C), F32)
    return call(
        prep_kernel, "prep", (wide, wide, wide, pre, pre), [VM] * 4,
        [pltpu.VMEM((2, PAD_ROWS + 16, HALF), F32), pltpu.VMEM((2, PRE_ROWS, HALF), F32)],
        20, 2_000_000_000, 8_000_000,
    )(latent, other, out_grad, table)


def cell_mask():
    cell = lax.broadcasted_iota(jnp.int32, (EDGE * ROWS, C), 0) % 8
    return (cell >= 1) & (cell <= EDGE)


def half_weight(quarters, t):
    return jnp.concatenate([quarter[t] for quarter in quarters], axis=0)


def half_conv(x3, quarters, act, start):
    for first in range(0, TAPS, GROUP):
        taps = range(first, min(first + GROUP, TAPS))
        windows = [
            x3[t % 3, t // 9 : t // 9 + EDGE, t // 3 % 3 : t // 3 % 3 + EDGE] for t in taps
        ]
        total = dot(
            jnp.concatenate([window.reshape(ACT_ROWS, HALF) for window in windows], axis=1),
            jnp.concatenate([half_weight(quarters, t) for t in taps], axis=0),
        )
        before = act if first else start
        act[...] = total if before is None else before[...] + total


def conv1_own_kernel(x3a, q0, q1, q2, q3, act):
    half_conv(x3a, (q0, q1, q2, q3), act, None)


def conv1_own(x3a, own):
    return call(
        conv1_own_kernel, "conv1_own", shape((ACT_ROWS, C), F32), [VM] * 5,
        [], 12, 2_000_000_000, 5_000_000,
    )(x3a, *own)


def permuted(value, lanes):
    high = value.astype(BF)
    rest = value - high.astype(F32)
    middle = rest.astype(BF)
    low = (rest - middle.astype(F32)).astype(BF)
    return dot(high, lanes) + (dot(middle, lanes) + dot(low, lanes))


def conv1_kernel(x3b, part_act, q0, q1, q2, q3, table, act, hsel, hsend, hs):
    half_conv(x3b, (q0, q1, q2, q3), act, part_act)

    hsel[:, 0] = jnp.zeros_like(hsel[:, 0])
    hsel[:, :, 0] = jnp.zeros_like(hsel[:, :, 0])
    hsend[:, 0] = jnp.zeros_like(hsend[:, 0])
    hsend[:, :, 0] = jnp.zeros_like(hsend[:, :, 0])
    store(hs, ACT_ROWS, 8, jnp.zeros((8, C), F32))
    inside = cell_mask()
    lanes = one_hot(table[1])
    for i in range(EDGE):
        part = pl.ds(i * EDGE * ROWS, EDGE * ROWS)
        value = permuted(act[part, :], lanes)
        act[part, :] = value
        hidden = jnp.where(inside, value * sigmoid(value), 0.0)
        store(hs, i * EDGE * ROWS, EDGE * ROWS, hidden.astype(BF).astype(F32))
    for dl in range(3):
        for i in range(EDGE):
            rows = load(hs, i * EDGE * ROWS + dl, EDGE * OUT_ROWS, 2)
            rows = rows.astype(BF).reshape(EDGE, OUT_ROWS, C)
            hsel[dl, i + 1, 1:] = rows
            hsend[dl, i + 1, 1:] = rows[..., HALF:]


def conv1(x3b, part_act, other, table):
    return call(
        conv1_kernel, "conv1",
        (
            shape((ACT_ROWS, C), F32),
            shape((3, 7, 7, OUT_ROWS, C), BF),
            shape((3, 7, 7, OUT_ROWS, HALF), BF),
        ),
        [VM] * 7,
        [pltpu.VMEM((2, ACT_ROWS + 8, HALF), F32)],
        24, 2_000_000_000, 7_000_000,
    )(x3b, part_act, *other, table)


def strided_window(hsel, dl, di, dj, lanes=slice(None)):
    blocks = [
        hsel[dl, 2 * qi + di, 2 * qj + dj, :, lanes] for qi in range(OUTER) for qj in range(OUTER)
    ]
    return jnp.concatenate(blocks, axis=0)


def conv2_kernel(
    skip, cot, hsel, q0, q1, q2, q3, p0, p1, p2, p3, block_out, grad_pre, grad_pre_t, bo
):
    quarters = (q0, q1, q2, q3, p0, p1, p2, p3)
    pre = skip[...]
    for di in range(3):
        for dj in range(3):
            for dl in range(3):
                pre = pre + dot(
                    strided_window(hsel, dl, di, dj), half_weight(quarters, TAPS + di * 9 + dj * 3 + dl)
                )
    sigma = sigmoid(pre)
    store(bo, 0, PRE_ROWS, pre * sigma)
    for qi in range(OUTER):
        for qj in range(OUTER):
            for ql in range(OUTER):
                base = (qi * 3 + qj) * OUT_ROWS + ql
                block_out[qi, qj, ql] = load(bo, base, SAMP, 4).astype(BF)
    grad = (cot[...] * (sigma * (1.0 + pre * (1.0 - sigma)))).astype(BF)
    grad_pre[...] = grad
    grad_pre_t[...] = grad.astype(F32).T.astype(BF)


def conv2(skip, cot, hsel, own, other):
    return call(
        conv2_kernel, "conv2",
        (
            shape((OUTER, OUTER, OUTER, SAMP, C), BF),
            shape((PRE_ROWS, C), BF),
            shape((C, PRE_ROWS), BF),
        ),
        [VM] * 11,
        [pltpu.VMEM((2, PRE_ROWS, HALF), F32)],
        16, 1_500_000_000, 6_000_000,
    )(skip, cot, hsel, *own, *other)


def back_kernel(
    act, grad_pre, q0, q1, q2, q3, p0, p1, p2, p3, table, gat, y, gh
):
    quarters = (q0, q1, q2, q3, p0, p1, p2, p3)
    y[...] = jnp.zeros_like(y)
    grad = grad_pre[...]
    for di in range(3):
        for dj in range(3):
            for dl in range(3):
                term = dot_t(grad, half_weight(quarters, TAPS + di * 9 + dj * 3 + dl))
                term = term.reshape(9, OUT_ROWS, C)
                for qi in range(OUTER):
                    for qj in range(OUTER):
                        y[dl, 2 * qi + di, 2 * qj + dj] += term[qi * 3 + qj]
    store(gh, ACT_ROWS, 8, jnp.zeros((8, C), F32))
    count = EDGE * OUT_ROWS
    for i in range(EDGE):
        base = i * EDGE * ROWS
        store(gh, base, count, y[0, i + 1, 1:].reshape(count, C), 2)
        store(gh, base + 1, count, y[1, i + 1, 1:].reshape(count, C), 2)
    for i in range(EDGE):
        base = i * EDGE * ROWS + 2
        total = load(gh, base, count, 2) + y[2, i + 1, 1:].reshape(count, C)
        store(gh, base, count, total, 2)
    inside = cell_mask()
    lanes = one_hot(table[1])
    for i in range(0, EDGE, 2):
        grads = []
        for start in (i * EDGE * ROWS, (i + 1) * EDGE * ROWS):
            value = act[pl.ds(start, EDGE * ROWS), :]
            sigma = sigmoid(value)
            grad = load(gh, start, EDGE * ROWS) * (sigma * (1.0 + value * (1.0 - sigma)))
            grads.append(jnp.where(inside, grad, 0.0).astype(BF))
        gat[i // 2] = dot_t(lanes, jnp.concatenate(grads, axis=0)).astype(BF)


def back(act, grad_pre, own, other, table):
    return call(
        back_kernel, "back", shape((EDGE // 2, C, 2 * EDGE * ROWS), BF), [VM] * 11,
        [
            pltpu.VMEM((3, 7, 7, OUT_ROWS, C), F32),
            pltpu.VMEM((2, ACT_ROWS + 8, HALF), F32),
        ],
        16, 1_500_000_000, 8_000_000,
    )(act, grad_pre, *own, *other, table)


def grad_loop(quarters, left, windows):
    eye = (
        lax.broadcasted_iota(jnp.int32, (C, C), 0) == lax.broadcasted_iota(jnp.int32, (C, C), 1)
    ).astype(BF)

    def product(taps):
        right = [
            jnp.concatenate([window(t // 9, t // 3 % 3, t % 3) for t in taps], axis=1)
            for window in windows
        ]
        total = dot(left[...], jnp.concatenate(right, axis=0)).astype(BF)
        for n in range(0, len(taps), 2):
            two = taps[n : n + 2]
            width = HALF * len(two)
            turned = dot_t(eye[:width, :width], total[:, n * HALF : n * HALF + width]).astype(BF)
            for m, t in enumerate(two):
                for k, quarter in enumerate(quarters):
                    first = m * HALF + k * BLOCK
                    quarter[t] = turned[first : first + BLOCK]

    def step(n, carry):
        product([GROUP * n + k for k in range(GROUP)])
        return carry

    whole = TAPS // GROUP
    lax.fori_loop(0, whole, step, 0)
    product(list(range(GROUP * whole, TAPS)))


QUARTERS = (shape(QUARTER, BF),) * 4


def grad2_kernel(
    grad_t, grad_t_other, hsel, hsel_other, f0, f1, f2, f3, left
):
    left[:, :PRE_ROWS] = grad_t[...]
    left[:, PRE_ROWS:] = grad_t_other[...]
    grad_loop(
        (f0, f1, f2, f3),
        left,
        (
            lambda di, dj, dl: strided_window(hsel, dl, di, dj, slice(0, HALF)),
            lambda di, dj, dl: strided_window(hsel_other, dl, di, dj),
        ),
    )


def grad2(grad_t, grad_t_other, hsel, hsel_other):
    return call(
        grad2_kernel, "grad2", QUARTERS, [VM] * 4,
        [pltpu.VMEM((C, 2 * PRE_ROWS), BF)], 12, 1_000_000_000, 4_000_000,
    )(grad_t, grad_t_other, hsel, hsel_other)


def same_window(x3):
    def window(di, dj, dl):
        return x3[dl, pl.ds(di, EDGE), pl.ds(dj, EDGE)].reshape(ACT_ROWS, HALF)

    return window


def grad1_kernel(gat, gat_other, x3a, x3o, f0, f1, f2, f3, left):
    for n, part in enumerate((gat, gat_other)):
        for i in range(EDGE // 2):
            first = n * ACT_ROWS + 2 * i * EDGE * ROWS
            left[:, first : first + 2 * EDGE * ROWS] = part[i]
    windows = (same_window(x3a), same_window(x3o))
    grad_loop((f0, f1, f2, f3), left, windows)


def grad1(gat, gat_other, x3a, x3o):
    return call(
        grad1_kernel, "grad1", QUARTERS, [VM] * 4,
        [pltpu.VMEM((C, 2 * ACT_ROWS), BF)], 16, 4_000_000_000, 7_000_000,
    )(gat, gat_other, x3a, x3o)


SHARDS = (MEMBERS, 2 * TAPS, 2 * C)


def pack_kernel(first, second, order, out):
    perm = one_hot(order[...])
    for i in range(2):
        lanes = slice(i * C, (i + 1) * C)
        one = dot(first[:, lanes].astype(BF), perm)
        both = jnp.concatenate([one, second[:, lanes]], axis=0).astype(BF)
        for n in range(MEMBERS):
            out[n, :, lanes] = both


def pack(first, second, order):
    return call(
        pack_kernel, "pack", shape(SHARDS, BF), [VM] * 3, [], 56, 10_000_000, 1_000_000
    )(first, second, order)


def spread_kernel(shards, out, wide):
    for m in range(MEMBERS):
        rows = shards[m].astype(F32)
        for i in range(2):
            store(wide, 2 * m + i, 2 * TAPS, rows[:, i * C : (i + 1) * C], BLOCK)

    def step(t, carry):
        out[t] = load(wide, pl.multiple_of(t * BLOCK, BLOCK), BLOCK).astype(BF)
        return carry

    lax.fori_loop(0, 2 * TAPS, step, 0)


def spread(shards):
    return call(
        spread_kernel, "spread", shape((2 * TAPS, BLOCK, C), BF), [VM],
        [pltpu.VMEM((2, 2 * TAPS * BLOCK, HALF), F32)], 8, 1_000_000, 2_000_000,
    )(shards)


def add_parts(p0, p1, p2, p3, wide):
    def step(t, carry):
        total = p0[t].astype(F32)
        for part in (p1, p2, p3):
            total = total + part[t].astype(F32)
        store(wide, pl.multiple_of(t * BLOCK, BLOCK), BLOCK, total)
        return carry

    lax.fori_loop(0, TAPS, step, 0)


def collect2(parts):
    return call(
        add_parts, "collect2", shape((2, TAPS * BLOCK, HALF), F32), [VM] * 4, [],
        4, 1_000_000, 3_000_000,
    )(*parts)


def collect_kernel(p0, p1, p2, p3, second, out, wide):
    wide[:, TAPS * BLOCK :] = second[...]
    add_parts(p0, p1, p2, p3, wide)
    for m in range(MEMBERS):
        for i in range(2):
            rows = load(wide, 2 * m + i, 2 * TAPS, BLOCK)
            out[m, :, i * C : (i + 1) * C] = rows.astype(BF)


def collect(parts, second):
    return call(
        collect_kernel, "collect", shape(SHARDS, BF), [VM] * 5,
        [pltpu.VMEM((2, 2 * TAPS * BLOCK, HALF), F32)], 8, 1_000_000, 3_000_000,
    )(*parts, second)


def adam_update(weight, first, second, grad):
    first_new = 0.9 * first + 0.1 * grad
    second_new = 0.999 * second + 0.001 * grad * grad
    fix_first = 1.0 - 0.9**10
    fix_second = 1.0 - 0.999**10
    weight_new = weight - 0.05 * (first_new / fix_first) / (
        jnp.sqrt(second_new / fix_second) + 1e-08
    )
    return (weight_new, first_new, second_new)


def adam_kernel(
    scale, parts, order, k1, m1, v1, k2, m2, v2, k1n, m1n, v1n, k2n, m2n, v2n
):
    back = one_hot(order[...]).astype(F32)
    for i in range(2):
        lanes = slice(i * C, (i + 1) * C)
        total = parts[0, :, lanes].astype(F32)
        for n in range(1, MEMBERS):
            total = total + parts[n, :, lanes].astype(F32)
        total = total * scale
        grad = lax.dot_general(
            total[:TAPS],
            back,
            (((1,), (1,)), ((), ())),
            precision=lax.Precision.HIGHEST,
            preferred_element_type=F32,
        )
        k1n[:, lanes], m1n[:, lanes], v1n[:, lanes] = adam_update(
            k1[:, lanes], m1[:, lanes], v1[:, lanes], grad
        )
        k2n[:, lanes], m2n[:, lanes], v2n[:, lanes] = adam_update(
            k2[:, lanes], m2[:, lanes], v2[:, lanes], total[TAPS:]
        )


def adam(scale, parts, order, *state):
    return call(
        functools.partial(adam_kernel, scale), "adam",
        (shape((TAPS, 2 * C), F32),) * 6, [VM] * 8, [], 6, 10_000_000, 1_000_000,
    )(parts, order, *state)


def place(x, y, z, c):
    return ((x * 4 + y) * 4 + z) * 2 + c


GRAY = [(0, 0), (1, 0), (1, 1), (0, 1)]
RING = {bits: at for at, bits in enumerate(GRAY)}


def label(bits):
    return bits[0] ^ 2 * bits[1] ^ 3 * bits[2]


TWIST = (0, 1, 2)


def kind(near, far):
    twist = 0
    for bit, turn in zip(far, TWIST):
        twist ^= bit * turn
    return label(near) ^ twist


def device(core, near, far):
    first, second = (near, far) if core == 0 else (far, near)
    return place(*(RING[pair] for pair in zip(first, second)), core)


TRIPLES = list(itertools.product(range(2), repeat=3))
DEVICES = list(itertools.product(range(2), TRIPLES, TRIPLES))


def turned(bits, which):
    return tuple(bit ^ (n in which) for n, bit in enumerate(bits))


NEIGHBOURS = [
    [(device(c, u, v), device(c, turned(u, (k,)), v)) for c, u, v in DEVICES] for k in range(3)
]
PARTNERS = [(n, n ^ 1) for n in range(128)]
FAR = [
    sorted(device(*d) for d in DEVICES if d[0] == c and kind(*d[1:]) == l)
    for c in range(2)
    for l in range(4)
]


def tables():
    half = lambda c, l: [
        2 * member + i for k in range(4) for member in FAR[4 * c + (l ^ k)] for i in range(2)
    ]
    columns = half(0, 0) + half(1, 0)
    at = {channel: n for n, channel in enumerate(columns)}
    table = np.zeros((128, 2, 1, C), np.int32)
    for c, u, v in DEVICES:
        channels = half(c, kind(u, v)) + half(1 - c, kind(v, u))
        table[device(c, u, v), 0, 0] = channels
        table[device(c, u, v), 1, 0] = [at[channel] for channel in channels]
    return np.array(columns, np.int32).reshape(1, C), table


COLUMNS, TABLE = tables()


def exchange(value):
    return lax.all_to_all(value, "dp", 0, 0, axis_index_groups=FAR, tiled=True)


def swap(value):
    return lax.ppermute(value, "dp", PARTNERS)


def send_round(values):
    return [values[0]] + [lax.ppermute(v, "dp", to) for v, to in zip(values[1:], NEIGHBOURS)]


def after(value, *others):
    return lax.optimization_barrier((value, *others))[0]


def body(latent, out_grad, k1, m1, v1, k2, m2, v2):
    scale = 1.0 / (latent.shape[0] * lax.axis_size("dp"))
    table = lax.dynamic_index_in_dim(jnp.asarray(TABLE), lax.axis_index("dp"), keepdims=False)
    columns = jnp.asarray(COLUMNS)

    shards = exchange(pack(k1, k2, columns))
    latent = latent.transpose(1, 2, 3, 0, 4)
    other = swap(latent)
    own = spread(shards)
    latent = after(latent, own)
    cells = prep(latent, other, out_grad.transpose(1, 2, 3, 0, 4), table)
    own = send_round([own] * 4)
    own[1:] = [after(value, cells[0]) for value in own[1:]]
    other = [swap(value) for value in own]
    x3a, x3b, x3o, skip, cot = cells

    act, hsel, hsend = conv1(x3b, conv1_own(x3a, own), other, table)
    hsel_other = swap(hsend)
    block_out, grad_pre, grad_pre_t = conv2(skip, cot, hsel, own, other)
    grad_pre_t_other = swap(grad_pre_t)
    gat = back(act, grad_pre, own, other, table)
    gat_other = swap(gat)
    second = grad2(grad_pre_t, grad_pre_t_other, hsel, hsel_other)
    gat = after(gat, *second)
    second = send_round(second)
    first = send_round(grad1(gat, gat_other, x3a, x3o))
    parts = exchange(collect(first, collect2(second)))
    new = adam(scale, parts, columns, k1, m1, v1, k2, m2, v2)
    return (block_out.transpose(3, 0, 1, 2, 4), *new)


def solution(mesh):
    wide = P("dp", None, None, None, None)
    flat = P(None, "dp")
    return jax.shard_map(
        body,
        mesh=mesh,
        in_specs=(wide, wide) + (flat,) * 6,
        out_specs=(wide,) + (flat,) * 6,
        check_vma=False,
    )
```

```python
import functools
import itertools

import jax
import jax.numpy as jnp
import numpy as np
from jax import lax
from jax.experimental import pallas as pl
from jax.experimental.pallas import tpu as pltpu
from jax.sharding import PartitionSpec as P

C = 256
HALF = 128
EDGE = 6
OUTER = 3
TAPS = 27
SAMP = 4
ROWS = 32
ACT_ROWS = EDGE * EDGE * ROWS
PAD_ROWS = 64 * ROWS
OUT_ROWS = 16
PRE_ROWS = 9 * OUT_ROWS
MEMBERS = 16
MIB = 1024 * 1024
BF = jnp.bfloat16
F32 = jnp.float32

GROUP = 6
BLOCK = 32
QUARTER = (TAPS, BLOCK, C)

VM = pl.BlockSpec(memory_space=pltpu.VMEM)


def shape(dims, dtype):
    return jax.ShapeDtypeStruct(dims, dtype)


def call(kernel, name, out_shape, in_specs, scratch, mib, flops, moved):
    single = not isinstance(out_shape, tuple)
    return pl.pallas_call(
        kernel,
        out_shape=out_shape,
        in_specs=in_specs,
        out_specs=VM if single else (VM,) * len(out_shape),
        scratch_shapes=scratch,
        compiler_params=pltpu.CompilerParams(vmem_limit_bytes=mib * MIB),
        cost_estimate=pl.CostEstimate(flops=flops, bytes_accessed=moved, transcendentals=0),
        name=name,
    )


def dot(a, b):
    return jnp.dot(a, b, preferred_element_type=F32)


def dot_t(a, b):
    return lax.dot_general(a, b, (((1,), (1,)), ((), ())), preferred_element_type=F32)


def sigmoid(v):
    return 1.0 / (1.0 + jnp.exp(-v))


def load(ref, start, count, stride=1):
    return jnp.concatenate(
        [ref[half, pl.ds(start, count, stride=stride), :] for half in range(2)], axis=1
    )


def store(ref, start, count, value, stride=1):
    for half in range(2):
        ref[half, pl.ds(start, count, stride=stride), :] = value[
            :, half * HALF : (half + 1) * HALF
        ]


def one_hot(order_row):
    return (lax.broadcasted_iota(jnp.int32, (C, C), 0) == order_row).astype(BF)


def fill_cells(source, xs):
    for i in range(EDGE):
        for j in range(EDGE):
            value = source[i, j].astype(F32)
            base = 8 + ((i + 1) * 8 + j + 1) * ROWS + 1
            for l in range(EDGE):
                store(xs, base + l, SAMP, value[l], 8)


def prep_kernel(latent, other, out_grad, table, x3a, x3b, x3o, skip, cot, xs, og):
    perm = one_hot(table[0])
    xs[...] = jnp.zeros_like(xs)
    og[...] = jnp.zeros_like(og)
    fill_cells(latent, xs)
    for qi in range(OUTER):
        for qj in range(OUTER):
            q = (qi * 3 + qj) * OUT_ROWS
            value = out_grad[qi, qj].astype(F32)
            for ql in range(OUTER):
                store(og, q + ql, SAMP, value[ql], 4)
            base = 8 + ((2 * qi + 1) * 8 + 2 * qj + 1) * ROWS + 1
            skip[q : q + OUT_ROWS, :] = load(xs, base, OUT_ROWS, 2)
    cot[...] = load(og, 0, PRE_ROWS)
    for i in range(8):
        for dl in range(3):
            rows = dot(load(xs, 7 + dl + i * 256, 256).astype(BF), perm).astype(BF)
            x3a[dl, i] = rows[:, :HALF].reshape(8, ROWS, HALF)
            x3b[dl, i] = rows[:, HALF:].reshape(8, ROWS, HALF)
    fill_cells(other, xs)
    for i in range(8):
        for dl in range(3):
            rows = dot(load(xs, 7 + dl + i * 256, 256).astype(BF), perm[:, :HALF])
            x3o[dl, i] = rows.astype(BF).reshape(8, ROWS, HALF)


def prep(latent, other, out_grad, table):
    wide = shape((3, 8, 8, ROWS, HALF), BF)
    pre = shape((PRE_ROWS, C), F32)
    return call(
        prep_kernel, "prep", (wide, wide, wide, pre, pre), [VM] * 4,
        [pltpu.VMEM((2, PAD_ROWS + 16, HALF), F32), pltpu.VMEM((2, PRE_ROWS, HALF), F32)],
        20, 2_000_000_000, 8_000_000,
    )(latent, other, out_grad, table)


def cell_mask():
    cell = lax.broadcasted_iota(jnp.int32, (EDGE * ROWS, C), 0) % 8
    return (cell >= 1) & (cell <= EDGE)


def half_weight(quarters, t):
    return jnp.concatenate([quarter[t] for quarter in quarters], axis=0)


def half_conv(x3, quarters, act, start):
    for first in range(0, TAPS, GROUP):
        taps = range(first, min(first + GROUP, TAPS))
        windows = [
            x3[t % 3, t // 9 : t // 9 + EDGE, t // 3 % 3 : t // 3 % 3 + EDGE] for t in taps
        ]
        total = dot(
            jnp.concatenate([window.reshape(ACT_ROWS, HALF) for window in windows], axis=1),
            jnp.concatenate([half_weight(quarters, t) for t in taps], axis=0),
        )
        before = act if first else start
        act[...] = total if before is None else before[...] + total


def conv1_own_kernel(x3a, q0, q1, q2, q3, act):
    half_conv(x3a, (q0, q1, q2, q3), act, None)


def conv1_own(x3a, own):
    return call(
        conv1_own_kernel, "conv1_own", shape((ACT_ROWS, C), F32), [VM] * 5,
        [], 12, 2_000_000_000, 5_000_000,
    )(x3a, *own)


def permuted(value, lanes):
    high = value.astype(BF)
    rest = value - high.astype(F32)
    middle = rest.astype(BF)
    low = (rest - middle.astype(F32)).astype(BF)
    return dot(high, lanes) + (dot(middle, lanes) + dot(low, lanes))


def conv1_kernel(x3b, part_act, q0, q1, q2, q3, table, act, hsel, hsend, hs):
    half_conv(x3b, (q0, q1, q2, q3), act, part_act)

    hsel[:, 0] = jnp.zeros_like(hsel[:, 0])
    hsel[:, :, 0] = jnp.zeros_like(hsel[:, :, 0])
    hsend[:, 0] = jnp.zeros_like(hsend[:, 0])
    hsend[:, :, 0] = jnp.zeros_like(hsend[:, :, 0])
    store(hs, ACT_ROWS, 8, jnp.zeros((8, C), F32))
    inside = cell_mask()
    lanes = one_hot(table[1])
    for i in range(EDGE):
        part = pl.ds(i * EDGE * ROWS, EDGE * ROWS)
        value = permuted(act[part, :], lanes)
        act[part, :] = value
        hidden = jnp.where(inside, value * sigmoid(value), 0.0)
        store(hs, i * EDGE * ROWS, EDGE * ROWS, hidden.astype(BF).astype(F32))
    for dl in range(3):
        for i in range(EDGE):
            rows = load(hs, i * EDGE * ROWS + dl, EDGE * OUT_ROWS, 2)
            rows = rows.astype(BF).reshape(EDGE, OUT_ROWS, C)
            hsel[dl, i + 1, 1:] = rows
            hsend[dl, i + 1, 1:] = rows[..., HALF:]


def conv1(x3b, part_act, other, table):
    return call(
        conv1_kernel, "conv1",
        (
            shape((ACT_ROWS, C), F32),
            shape((3, 7, 7, OUT_ROWS, C), BF),
            shape((3, 7, 7, OUT_ROWS, HALF), BF),
        ),
        [VM] * 7,
        [pltpu.VMEM((2, ACT_ROWS + 8, HALF), F32)],
        24, 2_000_000_000, 7_000_000,
    )(x3b, part_act, *other, table)


def strided_window(hsel, dl, di, dj, lanes=slice(None)):
    blocks = [
        hsel[dl, 2 * qi + di, 2 * qj + dj, :, lanes] for qi in range(OUTER) for qj in range(OUTER)
    ]
    return jnp.concatenate(blocks, axis=0)


def conv2_kernel(
    skip, cot, hsel, q0, q1, q2, q3, p0, p1, p2, p3, block_out, grad_pre, grad_pre_t, bo
):
    quarters = (q0, q1, q2, q3, p0, p1, p2, p3)
    pre = skip[...]
    for di in range(3):
        for dj in range(3):
            for dl in range(3):
                pre = pre + dot(
                    strided_window(hsel, dl, di, dj), half_weight(quarters, TAPS + di * 9 + dj * 3 + dl)
                )
    sigma = sigmoid(pre)
    store(bo, 0, PRE_ROWS, pre * sigma)
    for qi in range(OUTER):
        for qj in range(OUTER):
            for ql in range(OUTER):
                base = (qi * 3 + qj) * OUT_ROWS + ql
                block_out[qi, qj, ql] = load(bo, base, SAMP, 4).astype(BF)
    grad = (cot[...] * (sigma * (1.0 + pre * (1.0 - sigma)))).astype(BF)
    grad_pre[...] = grad
    grad_pre_t[...] = grad.astype(F32).T.astype(BF)


def conv2(skip, cot, hsel, own, other):
    return call(
        conv2_kernel, "conv2",
        (
            shape((OUTER, OUTER, OUTER, SAMP, C), BF),
            shape((PRE_ROWS, C), BF),
            shape((C, PRE_ROWS), BF),
        ),
        [VM] * 11,
        [pltpu.VMEM((2, PRE_ROWS, HALF), F32)],
        16, 1_500_000_000, 6_000_000,
    )(skip, cot, hsel, *own, *other)


def back_kernel(
    act, grad_pre, q0, q1, q2, q3, p0, p1, p2, p3, table, gat, y, gh
):
    quarters = (q0, q1, q2, q3, p0, p1, p2, p3)
    y[...] = jnp.zeros_like(y)
    grad = grad_pre[...]
    for di in range(3):
        for dj in range(3):
            for dl in range(3):
                term = dot_t(grad, half_weight(quarters, TAPS + di * 9 + dj * 3 + dl))
                term = term.reshape(9, OUT_ROWS, C)
                for qi in range(OUTER):
                    for qj in range(OUTER):
                        y[dl, 2 * qi + di, 2 * qj + dj] += term[qi * 3 + qj]
    store(gh, ACT_ROWS, 8, jnp.zeros((8, C), F32))
    count = EDGE * OUT_ROWS
    for i in range(EDGE):
        base = i * EDGE * ROWS
        store(gh, base, count, y[0, i + 1, 1:].reshape(count, C), 2)
        store(gh, base + 1, count, y[1, i + 1, 1:].reshape(count, C), 2)
    for i in range(EDGE):
        base = i * EDGE * ROWS + 2
        total = load(gh, base, count, 2) + y[2, i + 1, 1:].reshape(count, C)
        store(gh, base, count, total, 2)
    inside = cell_mask()
    lanes = one_hot(table[1])
    for i in range(0, EDGE, 2):
        grads = []
        for start in (i * EDGE * ROWS, (i + 1) * EDGE * ROWS):
            value = act[pl.ds(start, EDGE * ROWS), :]
            sigma = sigmoid(value)
            grad = load(gh, start, EDGE * ROWS) * (sigma * (1.0 + value * (1.0 - sigma)))
            grads.append(jnp.where(inside, grad, 0.0).astype(BF))
        gat[i // 2] = dot_t(lanes, jnp.concatenate(grads, axis=0)).astype(BF)


def back(act, grad_pre, own, other, table):
    return call(
        back_kernel, "back", shape((EDGE // 2, C, 2 * EDGE * ROWS), BF), [VM] * 11,
        [
            pltpu.VMEM((3, 7, 7, OUT_ROWS, C), F32),
            pltpu.VMEM((2, ACT_ROWS + 8, HALF), F32),
        ],
        16, 1_500_000_000, 8_000_000,
    )(act, grad_pre, *own, *other, table)


def grad_loop(quarters, left, windows):
    eye = (
        lax.broadcasted_iota(jnp.int32, (C, C), 0) == lax.broadcasted_iota(jnp.int32, (C, C), 1)
    ).astype(BF)

    right = [
        jnp.concatenate(
            [window(t // 9, t // 3 % 3, t % 3) for t in range(TAPS)], axis=1
        )
        for window in windows
    ]
    total = dot(left[...], jnp.concatenate(right, axis=0)).astype(BF)
    for first in range(0, TAPS, 2):
        taps = range(first, min(first + 2, TAPS))
        width = HALF * len(taps)
        part = total[:, first * HALF : first * HALF + width]
        turned = dot_t(eye[:width, :width], part).astype(BF)
        for t in taps:
            for k, quarter in enumerate(quarters):
                row = (t - first) * HALF + k * BLOCK
                quarter[t] = turned[row : row + BLOCK]


QUARTERS = (shape(QUARTER, BF),) * 4


def grad2_kernel(
    grad_t, grad_t_other, hsel, hsel_other, f0, f1, f2, f3, left
):
    left[:, :PRE_ROWS] = grad_t[...]
    left[:, PRE_ROWS:] = grad_t_other[...]
    grad_loop(
        (f0, f1, f2, f3),
        left,
        (
            lambda di, dj, dl: strided_window(hsel, dl, di, dj, slice(0, HALF)),
            lambda di, dj, dl: strided_window(hsel_other, dl, di, dj),
        ),
    )


def grad2(grad_t, grad_t_other, hsel, hsel_other):
    return call(
        grad2_kernel, "grad2", QUARTERS, [VM] * 4,
        [pltpu.VMEM((C, 2 * PRE_ROWS), BF)], 20, 1_000_000_000, 4_000_000,
    )(grad_t, grad_t_other, hsel, hsel_other)


def same_window(x3):
    def window(di, dj, dl):
        return x3[dl, pl.ds(di, EDGE), pl.ds(dj, EDGE)].reshape(ACT_ROWS, HALF)

    return window


def grad1_kernel(gat, gat_other, x3a, x3o, f0, f1, f2, f3, left):
    for n, part in enumerate((gat, gat_other)):
        for i in range(EDGE // 2):
            first = n * ACT_ROWS + 2 * i * EDGE * ROWS
            left[:, first : first + 2 * EDGE * ROWS] = part[i]
    windows = (same_window(x3a), same_window(x3o))
    grad_loop((f0, f1, f2, f3), left, windows)


def grad1(gat, gat_other, x3a, x3o):
    return call(
        grad1_kernel, "grad1", QUARTERS, [VM] * 4,
        [pltpu.VMEM((C, 2 * ACT_ROWS), BF)], 24, 4_000_000_000, 7_000_000,
    )(gat, gat_other, x3a, x3o)


SHARDS = (MEMBERS, 2 * TAPS, 2 * C)


def pack_kernel(first, second, order, out):
    perm = one_hot(order[...])
    for i in range(2):
        lanes = slice(i * C, (i + 1) * C)
        one = dot(first[:, lanes].astype(BF), perm)
        both = jnp.concatenate([one, second[:, lanes]], axis=0).astype(BF)
        for n in range(MEMBERS):
            out[n, :, lanes] = both


def pack(first, second, order):
    return call(
        pack_kernel, "pack", shape(SHARDS, BF), [VM] * 3, [], 56, 10_000_000, 1_000_000
    )(first, second, order)


def spread_kernel(shards, out, wide):
    for m in range(MEMBERS):
        rows = shards[m].astype(F32)
        for i in range(2):
            store(wide, 2 * m + i, 2 * TAPS, rows[:, i * C : (i + 1) * C], BLOCK)

    def step(n, carry):
        for k in range(GROUP):
            t = n * GROUP + k
            out[t] = load(wide, pl.multiple_of(t * BLOCK, BLOCK), BLOCK).astype(BF)
        return carry

    lax.fori_loop(0, 2 * TAPS // GROUP, step, 0)


def spread(shards):
    return call(
        spread_kernel, "spread", shape((2 * TAPS, BLOCK, C), BF), [VM],
        [pltpu.VMEM((2, 2 * TAPS * BLOCK, HALF), F32)], 8, 1_000_000, 2_000_000,
    )(shards)


def add_parts(p0, p1, p2, p3, wide):
    def step(n, carry):
        for k in range(3):
            t = n * 3 + k
            total = p0[t].astype(F32)
            for part in (p1, p2, p3):
                total = total + part[t].astype(F32)
            store(wide, pl.multiple_of(t * BLOCK, BLOCK), BLOCK, total)
        return carry

    lax.fori_loop(0, TAPS // 3, step, 0)


def collect2(parts):
    return call(
        add_parts, "collect2", shape((2, TAPS * BLOCK, HALF), F32), [VM] * 4, [],
        4, 1_000_000, 3_000_000,
    )(*parts)


def collect_kernel(p0, p1, p2, p3, second, out, wide):
    wide[:, TAPS * BLOCK :] = second[...]
    add_parts(p0, p1, p2, p3, wide)
    for m in range(MEMBERS):
        for i in range(2):
            rows = load(wide, 2 * m + i, 2 * TAPS, BLOCK)
            out[m, :, i * C : (i + 1) * C] = rows.astype(BF)


def collect(parts, second):
    return call(
        collect_kernel, "collect", shape(SHARDS, BF), [VM] * 5,
        [pltpu.VMEM((2, 2 * TAPS * BLOCK, HALF), F32)], 8, 1_000_000, 3_000_000,
    )(*parts, second)


def adam_update(weight, first, second, grad):
    first_new = 0.9 * first + 0.1 * grad
    second_new = 0.999 * second + 0.001 * grad * grad
    fix_first = 1.0 - 0.9**10
    fix_second = 1.0 - 0.999**10
    weight_new = weight - 0.05 * (first_new / fix_first) / (
        jnp.sqrt(second_new / fix_second) + 1e-08
    )
    return (weight_new, first_new, second_new)


def adam_kernel(
    scale, parts, order, k1, m1, v1, k2, m2, v2, k1n, m1n, v1n, k2n, m2n, v2n
):
    back = one_hot(order[...]).astype(F32)
    for i in range(2):
        lanes = slice(i * C, (i + 1) * C)
        total = parts[0, :, lanes].astype(F32)
        for n in range(1, MEMBERS):
            total = total + parts[n, :, lanes].astype(F32)
        total = total * scale
        grad = lax.dot_general(
            total[:TAPS],
            back,
            (((1,), (1,)), ((), ())),
            precision=lax.Precision.HIGHEST,
            preferred_element_type=F32,
        )
        k1n[:, lanes], m1n[:, lanes], v1n[:, lanes] = adam_update(
            k1[:, lanes], m1[:, lanes], v1[:, lanes], grad
        )
        k2n[:, lanes], m2n[:, lanes], v2n[:, lanes] = adam_update(
            k2[:, lanes], m2[:, lanes], v2[:, lanes], total[TAPS:]
        )


def adam(scale, parts, order, *state):
    return call(
        functools.partial(adam_kernel, scale), "adam",
        (shape((TAPS, 2 * C), F32),) * 6, [VM] * 8, [], 6, 10_000_000, 1_000_000,
    )(parts, order, *state)


def place(x, y, z, c):
    return ((x * 4 + y) * 4 + z) * 2 + c


GRAY = [(0, 0), (1, 0), (1, 1), (0, 1)]
RING = {bits: at for at, bits in enumerate(GRAY)}


def label(bits):
    return bits[0] ^ 2 * bits[1] ^ 3 * bits[2]


TWIST = (0, 1, 2)


def kind(near, far):
    twist = 0
    for bit, turn in zip(far, TWIST):
        twist ^= bit * turn
    return label(near) ^ twist


def device(core, near, far):
    first, second = (near, far) if core == 0 else (far, near)
    return place(*(RING[pair] for pair in zip(first, second)), core)


TRIPLES = list(itertools.product(range(2), repeat=3))
DEVICES = list(itertools.product(range(2), TRIPLES, TRIPLES))


def turned(bits, which):
    return tuple(bit ^ (n in which) for n, bit in enumerate(bits))


NEIGHBOURS = [
    [(device(c, u, v), device(c, turned(u, (k,)), v)) for c, u, v in DEVICES] for k in range(3)
]
PARTNERS = [(n, n ^ 1) for n in range(128)]
FAR = [
    sorted(device(*d) for d in DEVICES if d[0] == c and kind(*d[1:]) == l)
    for c in range(2)
    for l in range(4)
]


def tables():
    half = lambda c, l: [
        2 * member + i for k in range(4) for member in FAR[4 * c + (l ^ k)] for i in range(2)
    ]
    columns = half(0, 0) + half(1, 0)
    at = {channel: n for n, channel in enumerate(columns)}
    table = np.zeros((128, 2, 1, C), np.int32)
    for c, u, v in DEVICES:
        channels = half(c, kind(u, v)) + half(1 - c, kind(v, u))
        table[device(c, u, v), 0, 0] = channels
        table[device(c, u, v), 1, 0] = [at[channel] for channel in channels]
    return np.array(columns, np.int32).reshape(1, C), table


COLUMNS, TABLE = tables()


def exchange(value):
    return lax.all_to_all(value, "dp", 0, 0, axis_index_groups=FAR, tiled=True)


def swap(value):
    return lax.ppermute(value, "dp", PARTNERS)


def send_round(values):
    return [values[0]] + [lax.ppermute(v, "dp", to) for v, to in zip(values[1:], NEIGHBOURS)]


def after(value, *others):
    return lax.optimization_barrier((value, *others))[0]


def body(latent, out_grad, k1, m1, v1, k2, m2, v2):
    scale = 1.0 / (latent.shape[0] * lax.axis_size("dp"))
    table = lax.dynamic_index_in_dim(jnp.asarray(TABLE), lax.axis_index("dp"), keepdims=False)
    columns = jnp.asarray(COLUMNS)

    shards = exchange(pack(k1, k2, columns))
    latent = latent.transpose(1, 2, 3, 0, 4)
    other = swap(latent)
    own = spread(shards)
    latent = after(latent, own)
    cells = prep(latent, other, out_grad.transpose(1, 2, 3, 0, 4), table)
    own = send_round([own] * 4)
    own[1:] = [after(value, cells[0]) for value in own[1:]]
    other = [swap(value) for value in own]
    x3a, x3b, x3o, skip, cot = cells

    act, hsel, hsend = conv1(x3b, conv1_own(x3a, own), other, table)
    hsel_other = swap(hsend)
    block_out, grad_pre, grad_pre_t = conv2(skip, cot, hsel, own, other)
    grad_pre_t_other = swap(grad_pre_t)
    gat = back(act, grad_pre, own, other, table)
    gat_other = swap(gat)
    second = grad2(grad_pre_t, grad_pre_t_other, hsel, hsel_other)
    gat = after(gat, *second)
    second = send_round(second)
    first = send_round(grad1(gat, gat_other, x3a, x3o))
    parts = exchange(collect(first, collect2(second)))
    new = adam(scale, parts, columns, k1, m1, v1, k2, m2, v2)
    return (block_out.transpose(3, 0, 1, 2, 4), *new)


def solution(mesh):
    wide = P("dp", None, None, None, None)
    flat = P(None, "dp")
    return jax.shard_map(
        body,
        mesh=mesh,
        in_specs=(wide, wide) + (flat,) * 6,
        out_specs=(wide,) + (flat,) * 6,
        check_vma=False,
    )
```

```python
import functools
import itertools

import jax
import jax.numpy as jnp
import numpy as np
from jax import lax
from jax.experimental import pallas as pl
from jax.experimental.pallas import tpu as pltpu
from jax.sharding import PartitionSpec as P

C = 256
HALF = 128
EDGE = 6
OUTER = 3
TAPS = 27
SAMP = 4
ROWS = 32
ACT_ROWS = EDGE * EDGE * ROWS
PAD_ROWS = 64 * ROWS
OUT_ROWS = 16
PRE_ROWS = 9 * OUT_ROWS
MEMBERS = 16
MIB = 1024 * 1024
BF = jnp.bfloat16
F32 = jnp.float32

GROUP = 6
BLOCK = 32
QUARTER = (TAPS, BLOCK, C)

VM = pl.BlockSpec(memory_space=pltpu.VMEM)


def shape(dims, dtype):
    return jax.ShapeDtypeStruct(dims, dtype)


def call(kernel, name, out_shape, in_specs, scratch, mib, flops, moved):
    single = not isinstance(out_shape, tuple)
    return pl.pallas_call(
        kernel,
        out_shape=out_shape,
        in_specs=in_specs,
        out_specs=VM if single else (VM,) * len(out_shape),
        scratch_shapes=scratch,
        compiler_params=pltpu.CompilerParams(vmem_limit_bytes=mib * MIB),
        cost_estimate=pl.CostEstimate(flops=flops, bytes_accessed=moved, transcendentals=0),
        name=name,
    )


def dot(a, b):
    return jnp.dot(a, b, preferred_element_type=F32)


def dot_t(a, b):
    return lax.dot_general(a, b, (((1,), (1,)), ((), ())), preferred_element_type=F32)


def sigmoid(v):
    return 1.0 / (1.0 + jnp.exp(-v))


def load(ref, start, count, stride=1):
    return jnp.concatenate(
        [ref[half, pl.ds(start, count, stride=stride), :] for half in range(2)], axis=1
    )


def store(ref, start, count, value, stride=1):
    for half in range(2):
        ref[half, pl.ds(start, count, stride=stride), :] = value[
            :, half * HALF : (half + 1) * HALF
        ]


def one_hot(order_row):
    return (lax.broadcasted_iota(jnp.int32, (C, C), 0) == order_row).astype(BF)


def fill_cells(source, xs):
    for i in range(EDGE):
        for j in range(EDGE):
            value = source[i, j].astype(F32)
            base = 8 + ((i + 1) * 8 + j + 1) * ROWS + 1
            for l in range(EDGE):
                store(xs, base + l, SAMP, value[l], 8)


def prep_kernel(latent, other, out_grad, table, x3a, x3b, x3o, skip, cot, xs, og):
    perm = one_hot(table[0])
    xs[...] = jnp.zeros_like(xs)
    og[...] = jnp.zeros_like(og)
    fill_cells(latent, xs)
    for qi in range(OUTER):
        for qj in range(OUTER):
            q = (qi * 3 + qj) * OUT_ROWS
            value = out_grad[qi, qj].astype(F32)
            for ql in range(OUTER):
                store(og, q + ql, SAMP, value[ql], 4)
            base = 8 + ((2 * qi + 1) * 8 + 2 * qj + 1) * ROWS + 1
            skip[q : q + OUT_ROWS, :] = load(xs, base, OUT_ROWS, 2)
    cot[...] = load(og, 0, PRE_ROWS)
    for i in range(8):
        for dl in range(3):
            rows = dot(load(xs, 7 + dl + i * 256, 256).astype(BF), perm).astype(BF)
            x3a[dl, i] = rows[:, :HALF].reshape(8, ROWS, HALF)
            x3b[dl, i] = rows[:, HALF:].reshape(8, ROWS, HALF)
    fill_cells(other, xs)
    for i in range(8):
        for dl in range(3):
            rows = dot(load(xs, 7 + dl + i * 256, 256).astype(BF), perm[:, :HALF])
            x3o[dl, i] = rows.astype(BF).reshape(8, ROWS, HALF)


def prep(latent, other, out_grad, table):
    wide = shape((3, 8, 8, ROWS, HALF), BF)
    pre = shape((PRE_ROWS, C), F32)
    return call(
        prep_kernel, "prep", (wide, wide, wide, pre, pre), [VM] * 4,
        [pltpu.VMEM((2, PAD_ROWS + 16, HALF), F32), pltpu.VMEM((2, PRE_ROWS, HALF), F32)],
        20, 2_000_000_000, 8_000_000,
    )(latent, other, out_grad, table)


def cell_mask():
    cell = lax.broadcasted_iota(jnp.int32, (EDGE * ROWS, C), 0) % 8
    return (cell >= 1) & (cell <= EDGE)


def half_weight(quarters, t):
    return jnp.concatenate([quarter[t] for quarter in quarters], axis=0)


def half_conv(x3, quarters, act, start):
    for first in range(0, TAPS, GROUP):
        taps = range(first, min(first + GROUP, TAPS))
        windows = [
            x3[t % 3, t // 9 : t // 9 + EDGE, t // 3 % 3 : t // 3 % 3 + EDGE] for t in taps
        ]
        total = dot(
            jnp.concatenate([window.reshape(ACT_ROWS, HALF) for window in windows], axis=1),
            jnp.concatenate([half_weight(quarters, t) for t in taps], axis=0),
        )
        before = act if first else start
        act[...] = total if before is None else before[...] + total


def conv1_own_kernel(x3a, q0, q1, q2, q3, act):
    half_conv(x3a, (q0, q1, q2, q3), act, None)


def conv1_own(x3a, own):
    return call(
        conv1_own_kernel, "conv1_own", shape((ACT_ROWS, C), F32), [VM] * 5,
        [], 12, 2_000_000_000, 5_000_000,
    )(x3a, *own)


def permuted(value, lanes):
    high = value.astype(BF)
    rest = value - high.astype(F32)
    middle = rest.astype(BF)
    low = (rest - middle.astype(F32)).astype(BF)
    return dot(high, lanes) + (dot(middle, lanes) + dot(low, lanes))


def conv1_kernel(x3b, part_act, q0, q1, q2, q3, table, act, hsel, hsend, hs):
    half_conv(x3b, (q0, q1, q2, q3), act, part_act)

    hsel[:, 0] = jnp.zeros_like(hsel[:, 0])
    hsel[:, :, 0] = jnp.zeros_like(hsel[:, :, 0])
    hsend[:, 0] = jnp.zeros_like(hsend[:, 0])
    hsend[:, :, 0] = jnp.zeros_like(hsend[:, :, 0])
    store(hs, ACT_ROWS, 8, jnp.zeros((8, C), F32))
    inside = cell_mask()
    lanes = one_hot(table[1])
    for i in range(EDGE):
        part = pl.ds(i * EDGE * ROWS, EDGE * ROWS)
        value = permuted(act[part, :], lanes)
        act[part, :] = value
        hidden = jnp.where(inside, value * sigmoid(value), 0.0)
        store(hs, i * EDGE * ROWS, EDGE * ROWS, hidden.astype(BF).astype(F32))
    for dl in range(3):
        for i in range(EDGE):
            rows = load(hs, i * EDGE * ROWS + dl, EDGE * OUT_ROWS, 2)
            rows = rows.astype(BF).reshape(EDGE, OUT_ROWS, C)
            hsel[dl, i + 1, 1:] = rows
            hsend[dl, i + 1, 1:] = rows[..., HALF:]


def conv1(x3b, part_act, other, table):
    return call(
        conv1_kernel, "conv1",
        (
            shape((ACT_ROWS, C), F32),
            shape((3, 7, 7, OUT_ROWS, C), BF),
            shape((3, 7, 7, OUT_ROWS, HALF), BF),
        ),
        [VM] * 7,
        [pltpu.VMEM((2, ACT_ROWS + 8, HALF), F32)],
        24, 2_000_000_000, 7_000_000,
    )(x3b, part_act, *other, table)


def strided_window(hsel, dl, di, dj, lanes=slice(None)):
    blocks = [
        hsel[dl, 2 * qi + di, 2 * qj + dj, :, lanes] for qi in range(OUTER) for qj in range(OUTER)
    ]
    return jnp.concatenate(blocks, axis=0)


def middle_kernel(
    skip, cot, hsel, act, q0, q1, q2, q3, p0, p1, p2, p3, table,
    block_out, grad_pre_t, gat, bo, y, gh,
):
    quarters = (q0, q1, q2, q3, p0, p1, p2, p3)
    pre = skip[...]
    for di in range(3):
        for dj in range(3):
            for dl in range(3):
                pre = pre + dot(
                    strided_window(hsel, dl, di, dj), half_weight(quarters, TAPS + di * 9 + dj * 3 + dl)
                )
    sigma = sigmoid(pre)
    store(bo, 0, PRE_ROWS, pre * sigma)
    for qi in range(OUTER):
        for qj in range(OUTER):
            for ql in range(OUTER):
                base = (qi * 3 + qj) * OUT_ROWS + ql
                block_out[qi, qj, ql] = load(bo, base, SAMP, 4).astype(BF)
    grad = (cot[...] * (sigma * (1.0 + pre * (1.0 - sigma)))).astype(BF)
    grad_pre_t[...] = grad.astype(F32).T.astype(BF)

    y[...] = jnp.zeros_like(y)
    for di in range(3):
        for dj in range(3):
            for dl in range(3):
                term = dot_t(grad, half_weight(quarters, TAPS + di * 9 + dj * 3 + dl))
                term = term.reshape(9, OUT_ROWS, C)
                for qi in range(OUTER):
                    for qj in range(OUTER):
                        y[dl, 2 * qi + di, 2 * qj + dj] += term[qi * 3 + qj]
    store(gh, ACT_ROWS, 8, jnp.zeros((8, C), F32))
    count = EDGE * OUT_ROWS
    for i in range(EDGE):
        base = i * EDGE * ROWS
        store(gh, base, count, y[0, i + 1, 1:].reshape(count, C), 2)
        store(gh, base + 1, count, y[1, i + 1, 1:].reshape(count, C), 2)
    for i in range(EDGE):
        base = i * EDGE * ROWS + 2
        total = load(gh, base, count, 2) + y[2, i + 1, 1:].reshape(count, C)
        store(gh, base, count, total, 2)
    inside = cell_mask()
    lanes = one_hot(table[1])
    for i in range(0, EDGE, 2):
        grads = []
        for start in (i * EDGE * ROWS, (i + 1) * EDGE * ROWS):
            value = act[pl.ds(start, EDGE * ROWS), :]
            sigma = sigmoid(value)
            grad = load(gh, start, EDGE * ROWS) * (sigma * (1.0 + value * (1.0 - sigma)))
            grads.append(jnp.where(inside, grad, 0.0).astype(BF))
        gat[i // 2] = dot_t(lanes, jnp.concatenate(grads, axis=0)).astype(BF)


def middle(skip, cot, hsel, act, own, other, table):
    return call(
        middle_kernel, "middle",
        (
            shape((OUTER, OUTER, OUTER, SAMP, C), BF),
            shape((C, PRE_ROWS), BF),
            shape((EDGE // 2, C, 2 * EDGE * ROWS), BF),
        ),
        [VM] * 13,
        [
            pltpu.VMEM((2, PRE_ROWS, HALF), F32),
            pltpu.VMEM((3, 7, 7, OUT_ROWS, C), F32),
            pltpu.VMEM((2, ACT_ROWS + 8, HALF), F32),
        ],
        16, 3_000_000_000, 14_000_000,
    )(skip, cot, hsel, act, *own, *other, table)


def grad_loop(quarters, left, windows):
    eye = (
        lax.broadcasted_iota(jnp.int32, (C, C), 0) == lax.broadcasted_iota(jnp.int32, (C, C), 1)
    ).astype(BF)

    right = [
        jnp.concatenate(
            [window(t // 9, t // 3 % 3, t % 3) for t in range(TAPS)], axis=1
        )
        for window in windows
    ]
    total = dot(left[...], jnp.concatenate(right, axis=0)).astype(BF)
    for first in range(0, TAPS, 2):
        taps = range(first, min(first + 2, TAPS))
        width = HALF * len(taps)
        part = total[:, first * HALF : first * HALF + width]
        turned = dot_t(eye[:width, :width], part).astype(BF)
        for t in taps:
            for k, quarter in enumerate(quarters):
                row = (t - first) * HALF + k * BLOCK
                quarter[t] = turned[row : row + BLOCK]


QUARTERS = (shape(QUARTER, BF),) * 4


def grad2_kernel(
    grad_t, grad_t_other, hsel, hsel_other, f0, f1, f2, f3, left
):
    left[:, :PRE_ROWS] = grad_t[...]
    left[:, PRE_ROWS:] = grad_t_other[...]
    grad_loop(
        (f0, f1, f2, f3),
        left,
        (
            lambda di, dj, dl: strided_window(hsel, dl, di, dj, slice(0, HALF)),
            lambda di, dj, dl: strided_window(hsel_other, dl, di, dj),
        ),
    )


def grad2(grad_t, grad_t_other, hsel, hsel_other):
    return call(
        grad2_kernel, "grad2", QUARTERS, [VM] * 4,
        [pltpu.VMEM((C, 2 * PRE_ROWS), BF)], 20, 1_000_000_000, 4_000_000,
    )(grad_t, grad_t_other, hsel, hsel_other)


def same_window(x3):
    def window(di, dj, dl):
        return x3[dl, pl.ds(di, EDGE), pl.ds(dj, EDGE)].reshape(ACT_ROWS, HALF)

    return window


def grad1_kernel(gat, gat_other, x3a, x3o, f0, f1, f2, f3, left):
    for n, part in enumerate((gat, gat_other)):
        for i in range(EDGE // 2):
            first = n * ACT_ROWS + 2 * i * EDGE * ROWS
            left[:, first : first + 2 * EDGE * ROWS] = part[i]
    windows = (same_window(x3a), same_window(x3o))
    grad_loop((f0, f1, f2, f3), left, windows)


def grad1(gat, gat_other, x3a, x3o):
    return call(
        grad1_kernel, "grad1", QUARTERS, [VM] * 4,
        [pltpu.VMEM((C, 2 * ACT_ROWS), BF)], 24, 4_000_000_000, 7_000_000,
    )(gat, gat_other, x3a, x3o)


SHARDS = (MEMBERS, 2 * TAPS, 2 * C)


def pack_kernel(first, second, order, out):
    perm = one_hot(order[...])
    for i in range(2):
        lanes = slice(i * C, (i + 1) * C)
        one = dot(first[:, lanes].astype(BF), perm)
        both = jnp.concatenate([one, second[:, lanes]], axis=0).astype(BF)
        for n in range(MEMBERS):
            out[n, :, lanes] = both


def pack(first, second, order):
    return call(
        pack_kernel, "pack", shape(SHARDS, BF), [VM] * 3, [], 56, 10_000_000, 1_000_000
    )(first, second, order)


def spread_kernel(shards, out, wide):
    for m in range(MEMBERS):
        rows = shards[m].astype(F32)
        for i in range(2):
            store(wide, 2 * m + i, 2 * TAPS, rows[:, i * C : (i + 1) * C], BLOCK)

    def step(n, carry):
        for k in range(GROUP):
            t = n * GROUP + k
            out[t] = load(wide, pl.multiple_of(t * BLOCK, BLOCK), BLOCK).astype(BF)
        return carry

    lax.fori_loop(0, 2 * TAPS // GROUP, step, 0)


def spread(shards):
    return call(
        spread_kernel, "spread", shape((2 * TAPS, BLOCK, C), BF), [VM],
        [pltpu.VMEM((2, 2 * TAPS * BLOCK, HALF), F32)], 8, 1_000_000, 2_000_000,
    )(shards)


def add_parts(p0, p1, p2, p3, wide):
    def step(n, carry):
        for k in range(3):
            t = n * 3 + k
            total = p0[t].astype(F32)
            for part in (p1, p2, p3):
                total = total + part[t].astype(F32)
            store(wide, pl.multiple_of(t * BLOCK, BLOCK), BLOCK, total)
        return carry

    lax.fori_loop(0, TAPS // 3, step, 0)


def collect2(parts):
    return call(
        add_parts, "collect2", shape((2, TAPS * BLOCK, HALF), F32), [VM] * 4, [],
        4, 1_000_000, 3_000_000,
    )(*parts)


def collect_kernel(p0, p1, p2, p3, second, out, wide):
    wide[:, TAPS * BLOCK :] = second[...]
    add_parts(p0, p1, p2, p3, wide)
    for m in range(MEMBERS):
        for i in range(2):
            rows = load(wide, 2 * m + i, 2 * TAPS, BLOCK)
            out[m, :, i * C : (i + 1) * C] = rows.astype(BF)


def collect(parts, second):
    return call(
        collect_kernel, "collect", shape(SHARDS, BF), [VM] * 5,
        [pltpu.VMEM((2, 2 * TAPS * BLOCK, HALF), F32)], 8, 1_000_000, 3_000_000,
    )(*parts, second)


def adam_update(weight, first, second, grad):
    first_new = 0.9 * first + 0.1 * grad
    second_new = 0.999 * second + 0.001 * grad * grad
    fix_first = 1.0 - 0.9**10
    fix_second = 1.0 - 0.999**10
    weight_new = weight - 0.05 * (first_new / fix_first) / (
        jnp.sqrt(second_new / fix_second) + 1e-08
    )
    return (weight_new, first_new, second_new)


def adam_kernel(
    scale, parts, order, k1, m1, v1, k2, m2, v2, k1n, m1n, v1n, k2n, m2n, v2n
):
    back = one_hot(order[...]).astype(F32)
    for i in range(2):
        lanes = slice(i * C, (i + 1) * C)
        total = parts[0, :, lanes].astype(F32)
        for n in range(1, MEMBERS):
            total = total + parts[n, :, lanes].astype(F32)
        total = total * scale
        grad = lax.dot_general(
            total[:TAPS],
            back,
            (((1,), (1,)), ((), ())),
            precision=lax.Precision.HIGHEST,
            preferred_element_type=F32,
        )
        k1n[:, lanes], m1n[:, lanes], v1n[:, lanes] = adam_update(
            k1[:, lanes], m1[:, lanes], v1[:, lanes], grad
        )
        k2n[:, lanes], m2n[:, lanes], v2n[:, lanes] = adam_update(
            k2[:, lanes], m2[:, lanes], v2[:, lanes], total[TAPS:]
        )


def adam(scale, parts, order, *state):
    return call(
        functools.partial(adam_kernel, scale), "adam",
        (shape((TAPS, 2 * C), F32),) * 6, [VM] * 8, [], 6, 10_000_000, 1_000_000,
    )(parts, order, *state)


def place(x, y, z, c):
    return ((x * 4 + y) * 4 + z) * 2 + c


GRAY = [(0, 0), (1, 0), (1, 1), (0, 1)]
RING = {bits: at for at, bits in enumerate(GRAY)}


def label(bits):
    return bits[0] ^ 2 * bits[1] ^ 3 * bits[2]


TWIST = (0, 1, 2)


def kind(near, far):
    twist = 0
    for bit, turn in zip(far, TWIST):
        twist ^= bit * turn
    return label(near) ^ twist


def device(core, near, far):
    first, second = (near, far) if core == 0 else (far, near)
    return place(*(RING[pair] for pair in zip(first, second)), core)


TRIPLES = list(itertools.product(range(2), repeat=3))
DEVICES = list(itertools.product(range(2), TRIPLES, TRIPLES))


def turned(bits, which):
    return tuple(bit ^ (n in which) for n, bit in enumerate(bits))


NEIGHBOURS = [
    [(device(c, u, v), device(c, turned(u, (k,)), v)) for c, u, v in DEVICES] for k in range(3)
]
PARTNERS = [(n, n ^ 1) for n in range(128)]
FAR = [
    sorted(device(*d) for d in DEVICES if d[0] == c and kind(*d[1:]) == l)
    for c in range(2)
    for l in range(4)
]


def tables():
    half = lambda c, l: [
        2 * member + i for k in range(4) for member in FAR[4 * c + (l ^ k)] for i in range(2)
    ]
    columns = half(0, 0) + half(1, 0)
    at = {channel: n for n, channel in enumerate(columns)}
    table = np.zeros((128, 2, 1, C), np.int32)
    for c, u, v in DEVICES:
        channels = half(c, kind(u, v)) + half(1 - c, kind(v, u))
        table[device(c, u, v), 0, 0] = channels
        table[device(c, u, v), 1, 0] = [at[channel] for channel in channels]
    return np.array(columns, np.int32).reshape(1, C), table


COLUMNS, TABLE = tables()


def exchange(value):
    return lax.all_to_all(value, "dp", 0, 0, axis_index_groups=FAR, tiled=True)


def swap(value):
    return lax.ppermute(value, "dp", PARTNERS)


def send_round(values):
    return [values[0]] + [lax.ppermute(v, "dp", to) for v, to in zip(values[1:], NEIGHBOURS)]


def after(value, *others):
    return lax.optimization_barrier((value, *others))[0]


def body(latent, out_grad, k1, m1, v1, k2, m2, v2):
    scale = 1.0 / (latent.shape[0] * lax.axis_size("dp"))
    table = lax.dynamic_index_in_dim(jnp.asarray(TABLE), lax.axis_index("dp"), keepdims=False)
    columns = jnp.asarray(COLUMNS)

    shards = exchange(pack(k1, k2, columns))
    latent = latent.transpose(1, 2, 3, 0, 4)
    other = swap(latent)
    own = spread(shards)
    latent = after(latent, own)
    cells = prep(latent, other, out_grad.transpose(1, 2, 3, 0, 4), table)
    own = send_round([own] * 4)
    own[1:] = [after(value, cells[0]) for value in own[1:]]
    other = [swap(value) for value in own]
    x3a, x3b, x3o, skip, cot = cells

    act, hsel, hsend = conv1(x3b, conv1_own(x3a, own), other, table)
    hsel_other = swap(hsend)
    block_out, grad_pre_t, gat = middle(skip, cot, hsel, act, own, other, table)
    grad_pre_t_other = swap(grad_pre_t)
    gat_other = swap(gat)
    second = grad2(grad_pre_t, grad_pre_t_other, hsel, hsel_other)
    gat = after(gat, *second)
    second = send_round(second)
    first = send_round(grad1(gat, gat_other, x3a, x3o))
    parts = exchange(collect(first, collect2(second)))
    new = adam(scale, parts, columns, k1, m1, v1, k2, m2, v2)
    return (block_out.transpose(3, 0, 1, 2, 4), *new)


def solution(mesh):
    wide = P("dp", None, None, None, None)
    flat = P(None, "dp")
    return jax.shard_map(
        body,
        mesh=mesh,
        in_specs=(wide, wide) + (flat,) * 6,
        out_specs=(wide,) + (flat,) * 6,
        check_vma=False,
    )
```

```python
import functools
import itertools

import jax
import jax.numpy as jnp
import numpy as np
from jax import lax
from jax.experimental import pallas as pl
from jax.experimental.pallas import tpu as pltpu
from jax.sharding import PartitionSpec as P

C = 256
HALF = 128
EDGE = 6
OUTER = 3
TAPS = 27
SAMP = 4
ROWS = 32
ACT_ROWS = EDGE * EDGE * ROWS
PAD_ROWS = 64 * ROWS
OUT_ROWS = 16
PRE_ROWS = 9 * OUT_ROWS
MEMBERS = 16
MIB = 1024 * 1024
BF = jnp.bfloat16
F32 = jnp.float32

GROUP = 6
BLOCK = 32
QUARTER = (TAPS, BLOCK, C)

VM = pl.BlockSpec(memory_space=pltpu.VMEM)


def shape(dims, dtype):
    return jax.ShapeDtypeStruct(dims, dtype)


def call(kernel, name, out_shape, in_specs, scratch, mib, flops, moved):
    single = not isinstance(out_shape, tuple)
    return pl.pallas_call(
        kernel,
        out_shape=out_shape,
        in_specs=in_specs,
        out_specs=VM if single else (VM,) * len(out_shape),
        scratch_shapes=scratch,
        compiler_params=pltpu.CompilerParams(vmem_limit_bytes=mib * MIB),
        cost_estimate=pl.CostEstimate(flops=flops, bytes_accessed=moved, transcendentals=0),
        name=name,
    )


def dot(a, b):
    return jnp.dot(a, b, preferred_element_type=F32)


def dot_t(a, b):
    return lax.dot_general(a, b, (((1,), (1,)), ((), ())), preferred_element_type=F32)


def sigmoid(v):
    return 1.0 / (1.0 + jnp.exp(-v))


def load(ref, start, count, stride=1):
    return jnp.concatenate(
        [ref[half, pl.ds(start, count, stride=stride), :] for half in range(2)], axis=1
    )


def store(ref, start, count, value, stride=1):
    for half in range(2):
        ref[half, pl.ds(start, count, stride=stride), :] = value[
            :, half * HALF : (half + 1) * HALF
        ]


def one_hot(order_row):
    return (lax.broadcasted_iota(jnp.int32, (C, C), 0) == order_row).astype(BF)


def fill_cells(source, xs):
    for i in range(EDGE):
        for j in range(EDGE):
            value = source[i, j].astype(F32)
            base = 8 + ((i + 1) * 8 + j + 1) * ROWS + 1
            for l in range(EDGE):
                store(xs, base + l, SAMP, value[l], 8)


def prep_kernel(latent, other, out_grad, table, x3a, x3b, x3o, skip, cot, xs, og):
    perm = one_hot(table[0])
    xs[...] = jnp.zeros_like(xs)
    og[...] = jnp.zeros_like(og)
    fill_cells(latent, xs)
    for qi in range(OUTER):
        for qj in range(OUTER):
            q = (qi * 3 + qj) * OUT_ROWS
            value = out_grad[qi, qj].astype(F32)
            for ql in range(OUTER):
                store(og, q + ql, SAMP, value[ql], 4)
            base = 8 + ((2 * qi + 1) * 8 + 2 * qj + 1) * ROWS + 1
            skip[q : q + OUT_ROWS, :] = load(xs, base, OUT_ROWS, 2)
    cot[...] = load(og, 0, PRE_ROWS)
    for i in range(8):
        for dl in range(3):
            rows = dot(load(xs, 7 + dl + i * 256, 256).astype(BF), perm).astype(BF)
            x3a[dl, i] = rows[:, :HALF].reshape(8, ROWS, HALF)
            x3b[dl, i] = rows[:, HALF:].reshape(8, ROWS, HALF)
    fill_cells(other, xs)
    for i in range(8):
        for dl in range(3):
            rows = dot(load(xs, 7 + dl + i * 256, 256).astype(BF), perm[:, :HALF])
            x3o[dl, i] = rows.astype(BF).reshape(8, ROWS, HALF)


def prep(latent, other, out_grad, table):
    wide = shape((3, 8, 8, ROWS, HALF), BF)
    pre = shape((PRE_ROWS, C), F32)
    return call(
        prep_kernel, "prep", (wide, wide, wide, pre, pre), [VM] * 4,
        [pltpu.VMEM((2, PAD_ROWS + 16, HALF), F32), pltpu.VMEM((2, PRE_ROWS, HALF), F32)],
        20, 2_000_000_000, 8_000_000,
    )(latent, other, out_grad, table)


def cell_mask():
    cell = lax.broadcasted_iota(jnp.int32, (EDGE * ROWS, C), 0) % 8
    return (cell >= 1) & (cell <= EDGE)


def half_weight(quarters, t):
    return jnp.concatenate([quarter[t] for quarter in quarters], axis=0)


def half_conv(x3, quarters, act, start):
    for first in range(0, TAPS, GROUP):
        taps = range(first, min(first + GROUP, TAPS))
        windows = [
            x3[t % 3, t // 9 : t // 9 + EDGE, t // 3 % 3 : t // 3 % 3 + EDGE] for t in taps
        ]
        total = dot(
            jnp.concatenate([window.reshape(ACT_ROWS, HALF) for window in windows], axis=1),
            jnp.concatenate([half_weight(quarters, t) for t in taps], axis=0),
        )
        before = act if first else start
        act[...] = total if before is None else before[...] + total


def conv1_own_kernel(x3a, q0, q1, q2, q3, act):
    half_conv(x3a, (q0, q1, q2, q3), act, None)


def conv1_own(x3a, own):
    return call(
        conv1_own_kernel, "conv1_own", shape((ACT_ROWS, C), F32), [VM] * 5,
        [], 12, 2_000_000_000, 5_000_000,
    )(x3a, *own)


def permuted(value, lanes):
    high = value.astype(BF)
    rest = value - high.astype(F32)
    middle = rest.astype(BF)
    low = (rest - middle.astype(F32)).astype(BF)
    return dot(high, lanes) + (dot(middle, lanes) + dot(low, lanes))


def conv1_kernel(x3b, part_act, q0, q1, q2, q3, table, act, hsel, hsend, hs):
    half_conv(x3b, (q0, q1, q2, q3), act, part_act)

    hsel[:, 0] = jnp.zeros_like(hsel[:, 0])
    hsel[:, :, 0] = jnp.zeros_like(hsel[:, :, 0])
    hsend[:, 0] = jnp.zeros_like(hsend[:, 0])
    hsend[:, :, 0] = jnp.zeros_like(hsend[:, :, 0])
    store(hs, ACT_ROWS, 8, jnp.zeros((8, C), F32))
    inside = cell_mask()
    lanes = one_hot(table[1])
    for i in range(EDGE):
        part = pl.ds(i * EDGE * ROWS, EDGE * ROWS)
        value = permuted(act[part, :], lanes)
        act[part, :] = value
        hidden = jnp.where(inside, value * sigmoid(value), 0.0)
        store(hs, i * EDGE * ROWS, EDGE * ROWS, hidden.astype(BF).astype(F32))
    for dl in range(3):
        for i in range(EDGE):
            rows = load(hs, i * EDGE * ROWS + dl, EDGE * OUT_ROWS, 2)
            rows = rows.astype(BF).reshape(EDGE, OUT_ROWS, C)
            hsel[dl, i + 1, 1:] = rows
            hsend[dl, i + 1, 1:] = rows[..., HALF:]


def conv1(x3b, part_act, other, table):
    return call(
        conv1_kernel, "conv1",
        (
            shape((ACT_ROWS, C), F32),
            shape((3, 7, 7, OUT_ROWS, C), BF),
            shape((3, 7, 7, OUT_ROWS, HALF), BF),
        ),
        [VM] * 7,
        [pltpu.VMEM((2, ACT_ROWS + 8, HALF), F32)],
        24, 2_000_000_000, 7_000_000,
    )(x3b, part_act, *other, table)


def strided_window(hsel, dl, di, dj, lanes=slice(None)):
    blocks = [
        hsel[dl, 2 * qi + di, 2 * qj + dj, :, lanes] for qi in range(OUTER) for qj in range(OUTER)
    ]
    return jnp.concatenate(blocks, axis=0)


def conv2_kernel(
    skip, cot, hsel, q0, q1, q2, q3, p0, p1, p2, p3, block_out, grad_pre, grad_pre_t, bo
):
    quarters = (q0, q1, q2, q3, p0, p1, p2, p3)
    windows = [strided_window(hsel, t % 3, t // 9, t // 3 % 3) for t in range(TAPS)]
    weights = [half_weight(quarters, TAPS + t) for t in range(TAPS)]
    pre = skip[...] + dot(
        jnp.concatenate(windows, axis=1), jnp.concatenate(weights, axis=0)
    )
    sigma = sigmoid(pre)
    store(bo, 0, PRE_ROWS, pre * sigma)
    for qi in range(OUTER):
        for qj in range(OUTER):
            for ql in range(OUTER):
                base = (qi * 3 + qj) * OUT_ROWS + ql
                block_out[qi, qj, ql] = load(bo, base, SAMP, 4).astype(BF)
    grad = (cot[...] * (sigma * (1.0 + pre * (1.0 - sigma)))).astype(BF)
    grad_pre[...] = grad
    grad_pre_t[...] = grad.astype(F32).T.astype(BF)


def conv2(skip, cot, hsel, own, other):
    return call(
        conv2_kernel, "conv2",
        (
            shape((OUTER, OUTER, OUTER, SAMP, C), BF),
            shape((PRE_ROWS, C), BF),
            shape((C, PRE_ROWS), BF),
        ),
        [VM] * 11,
        [pltpu.VMEM((2, PRE_ROWS, HALF), F32)],
        16, 1_500_000_000, 6_000_000,
    )(skip, cot, hsel, *own, *other)


def back_kernel(
    act, grad_pre, q0, q1, q2, q3, p0, p1, p2, p3, table, gat, y, gh
):
    quarters = (q0, q1, q2, q3, p0, p1, p2, p3)
    y[...] = jnp.zeros_like(y)
    weights = [half_weight(quarters, TAPS + t) for t in range(TAPS)]
    terms = dot_t(grad_pre[...], jnp.concatenate(weights, axis=0))
    for t in range(TAPS):
        di, dj, dl = t // 9, t // 3 % 3, t % 3
        term = terms[:, t * C : (t + 1) * C].reshape(9, OUT_ROWS, C)
        for qi in range(OUTER):
            for qj in range(OUTER):
                y[dl, 2 * qi + di, 2 * qj + dj] += term[qi * 3 + qj]
    store(gh, ACT_ROWS, 8, jnp.zeros((8, C), F32))
    count = EDGE * OUT_ROWS
    for i in range(EDGE):
        base = i * EDGE * ROWS
        store(gh, base, count, y[0, i + 1, 1:].reshape(count, C), 2)
        store(gh, base + 1, count, y[1, i + 1, 1:].reshape(count, C), 2)
    for i in range(EDGE):
        base = i * EDGE * ROWS + 2
        total = load(gh, base, count, 2) + y[2, i + 1, 1:].reshape(count, C)
        store(gh, base, count, total, 2)
    inside = cell_mask()
    lanes = one_hot(table[1])
    for i in range(0, EDGE, 2):
        grads = []
        for start in (i * EDGE * ROWS, (i + 1) * EDGE * ROWS):
            value = act[pl.ds(start, EDGE * ROWS), :]
            sigma = sigmoid(value)
            grad = load(gh, start, EDGE * ROWS) * (sigma * (1.0 + value * (1.0 - sigma)))
            grads.append(jnp.where(inside, grad, 0.0).astype(BF))
        gat[i // 2] = dot_t(lanes, jnp.concatenate(grads, axis=0)).astype(BF)


def back(act, grad_pre, own, other, table):
    return call(
        back_kernel, "back", shape((EDGE // 2, C, 2 * EDGE * ROWS), BF), [VM] * 11,
        [
            pltpu.VMEM((3, 7, 7, OUT_ROWS, C), F32),
            pltpu.VMEM((2, ACT_ROWS + 8, HALF), F32),
        ],
        16, 1_500_000_000, 8_000_000,
    )(act, grad_pre, *own, *other, table)


def grad_loop(quarters, left, windows):
    eye = (
        lax.broadcasted_iota(jnp.int32, (C, C), 0) == lax.broadcasted_iota(jnp.int32, (C, C), 1)
    ).astype(BF)

    right = [
        jnp.concatenate(
            [window(t // 9, t // 3 % 3, t % 3) for t in range(TAPS)], axis=1
        )
        for window in windows
    ]
    total = dot(left[...], jnp.concatenate(right, axis=0)).astype(BF)
    for first in range(0, TAPS, 2):
        taps = range(first, min(first + 2, TAPS))
        width = HALF * len(taps)
        part = total[:, first * HALF : first * HALF + width]
        turned = dot_t(eye[:width, :width], part).astype(BF)
        for t in taps:
            for k, quarter in enumerate(quarters):
                row = (t - first) * HALF + k * BLOCK
                quarter[t] = turned[row : row + BLOCK]


QUARTERS = (shape(QUARTER, BF),) * 4


def grad2_kernel(
    grad_t, grad_t_other, hsel, hsel_other, f0, f1, f2, f3, left
):
    left[:, :PRE_ROWS] = grad_t[...]
    left[:, PRE_ROWS:] = grad_t_other[...]
    grad_loop(
        (f0, f1, f2, f3),
        left,
        (
            lambda di, dj, dl: strided_window(hsel, dl, di, dj, slice(0, HALF)),
            lambda di, dj, dl: strided_window(hsel_other, dl, di, dj),
        ),
    )


def grad2(grad_t, grad_t_other, hsel, hsel_other):
    return call(
        grad2_kernel, "grad2", QUARTERS, [VM] * 4,
        [pltpu.VMEM((C, 2 * PRE_ROWS), BF)], 20, 1_000_000_000, 4_000_000,
    )(grad_t, grad_t_other, hsel, hsel_other)


def same_window(x3):
    def window(di, dj, dl):
        return x3[dl, pl.ds(di, EDGE), pl.ds(dj, EDGE)].reshape(ACT_ROWS, HALF)

    return window


def grad1_kernel(gat, gat_other, x3a, x3o, f0, f1, f2, f3, left):
    for n, part in enumerate((gat, gat_other)):
        for i in range(EDGE // 2):
            first = n * ACT_ROWS + 2 * i * EDGE * ROWS
            left[:, first : first + 2 * EDGE * ROWS] = part[i]
    windows = (same_window(x3a), same_window(x3o))
    grad_loop((f0, f1, f2, f3), left, windows)


def grad1(gat, gat_other, x3a, x3o):
    return call(
        grad1_kernel, "grad1", QUARTERS, [VM] * 4,
        [pltpu.VMEM((C, 2 * ACT_ROWS), BF)], 24, 4_000_000_000, 7_000_000,
    )(gat, gat_other, x3a, x3o)


SHARDS = (MEMBERS, 2 * TAPS, 2 * C)


def pack_kernel(first, second, order, out):
    perm = one_hot(order[...])
    for i in range(2):
        lanes = slice(i * C, (i + 1) * C)
        one = dot(first[:, lanes].astype(BF), perm)
        both = jnp.concatenate([one, second[:, lanes]], axis=0).astype(BF)
        for n in range(MEMBERS):
            out[n, :, lanes] = both


def pack(first, second, order):
    return call(
        pack_kernel, "pack", shape(SHARDS, BF), [VM] * 3, [], 56, 10_000_000, 1_000_000
    )(first, second, order)


def spread_kernel(shards, out, wide):
    for m in range(MEMBERS):
        rows = shards[m].astype(F32)
        for i in range(2):
            store(wide, 2 * m + i, 2 * TAPS, rows[:, i * C : (i + 1) * C], BLOCK)

    def step(n, carry):
        for k in range(GROUP):
            t = n * GROUP + k
            out[t] = load(wide, pl.multiple_of(t * BLOCK, BLOCK), BLOCK).astype(BF)
        return carry

    lax.fori_loop(0, 2 * TAPS // GROUP, step, 0)


def spread(shards):
    return call(
        spread_kernel, "spread", shape((2 * TAPS, BLOCK, C), BF), [VM],
        [pltpu.VMEM((2, 2 * TAPS * BLOCK, HALF), F32)], 8, 1_000_000, 2_000_000,
    )(shards)


def add_parts(p0, p1, p2, p3, wide):
    def step(n, carry):
        for k in range(3):
            t = n * 3 + k
            total = p0[t].astype(F32)
            for part in (p1, p2, p3):
                total = total + part[t].astype(F32)
            store(wide, pl.multiple_of(t * BLOCK, BLOCK), BLOCK, total)
        return carry

    lax.fori_loop(0, TAPS // 3, step, 0)


def collect2(parts):
    return call(
        add_parts, "collect2", shape((2, TAPS * BLOCK, HALF), F32), [VM] * 4, [],
        4, 1_000_000, 3_000_000,
    )(*parts)


def collect_kernel(p0, p1, p2, p3, second, out, wide):
    wide[:, TAPS * BLOCK :] = second[...]
    add_parts(p0, p1, p2, p3, wide)
    for m in range(MEMBERS):
        for i in range(2):
            rows = load(wide, 2 * m + i, 2 * TAPS, BLOCK)
            out[m, :, i * C : (i + 1) * C] = rows.astype(BF)


def collect(parts, second):
    return call(
        collect_kernel, "collect", shape(SHARDS, BF), [VM] * 5,
        [pltpu.VMEM((2, 2 * TAPS * BLOCK, HALF), F32)], 8, 1_000_000, 3_000_000,
    )(*parts, second)


def adam_update(weight, first, second, grad):
    first_new = 0.9 * first + 0.1 * grad
    second_new = 0.999 * second + 0.001 * grad * grad
    fix_first = 1.0 - 0.9**10
    fix_second = 1.0 - 0.999**10
    weight_new = weight - 0.05 * (first_new / fix_first) / (
        jnp.sqrt(second_new / fix_second) + 1e-08
    )
    return (weight_new, first_new, second_new)


def adam_kernel(
    scale, parts, order, k1, m1, v1, k2, m2, v2, k1n, m1n, v1n, k2n, m2n, v2n
):
    back = one_hot(order[...]).astype(F32)
    for i in range(2):
        lanes = slice(i * C, (i + 1) * C)
        total = parts[0, :, lanes].astype(F32)
        for n in range(1, MEMBERS):
            total = total + parts[n, :, lanes].astype(F32)
        total = total * scale
        grad = lax.dot_general(
            total[:TAPS],
            back,
            (((1,), (1,)), ((), ())),
            precision=lax.Precision.HIGHEST,
            preferred_element_type=F32,
        )
        k1n[:, lanes], m1n[:, lanes], v1n[:, lanes] = adam_update(
            k1[:, lanes], m1[:, lanes], v1[:, lanes], grad
        )
        k2n[:, lanes], m2n[:, lanes], v2n[:, lanes] = adam_update(
            k2[:, lanes], m2[:, lanes], v2[:, lanes], total[TAPS:]
        )


def adam(scale, parts, order, *state):
    return call(
        functools.partial(adam_kernel, scale), "adam",
        (shape((TAPS, 2 * C), F32),) * 6, [VM] * 8, [], 6, 10_000_000, 1_000_000,
    )(parts, order, *state)


def place(x, y, z, c):
    return ((x * 4 + y) * 4 + z) * 2 + c


GRAY = [(0, 0), (1, 0), (1, 1), (0, 1)]
RING = {bits: at for at, bits in enumerate(GRAY)}


def label(bits):
    return bits[0] ^ 2 * bits[1] ^ 3 * bits[2]


TWIST = (0, 1, 2)


def kind(near, far):
    twist = 0
    for bit, turn in zip(far, TWIST):
        twist ^= bit * turn
    return label(near) ^ twist


def device(core, near, far):
    first, second = (near, far) if core == 0 else (far, near)
    return place(*(RING[pair] for pair in zip(first, second)), core)


TRIPLES = list(itertools.product(range(2), repeat=3))
DEVICES = list(itertools.product(range(2), TRIPLES, TRIPLES))


def turned(bits, which):
    return tuple(bit ^ (n in which) for n, bit in enumerate(bits))


NEIGHBOURS = [
    [(device(c, u, v), device(c, turned(u, (k,)), v)) for c, u, v in DEVICES] for k in range(3)
]
PARTNERS = [(n, n ^ 1) for n in range(128)]
FAR = [
    sorted(device(*d) for d in DEVICES if d[0] == c and kind(*d[1:]) == l)
    for c in range(2)
    for l in range(4)
]


def tables():
    half = lambda c, l: [
        2 * member + i for k in range(4) for member in FAR[4 * c + (l ^ k)] for i in range(2)
    ]
    columns = half(0, 0) + half(1, 0)
    at = {channel: n for n, channel in enumerate(columns)}
    table = np.zeros((128, 2, 1, C), np.int32)
    for c, u, v in DEVICES:
        channels = half(c, kind(u, v)) + half(1 - c, kind(v, u))
        table[device(c, u, v), 0, 0] = channels
        table[device(c, u, v), 1, 0] = [at[channel] for channel in channels]
    return np.array(columns, np.int32).reshape(1, C), table


COLUMNS, TABLE = tables()


def exchange(value):
    return lax.all_to_all(value, "dp", 0, 0, axis_index_groups=FAR, tiled=True)


def swap(value):
    return lax.ppermute(value, "dp", PARTNERS)


def send_round(values):
    return [values[0]] + [lax.ppermute(v, "dp", to) for v, to in zip(values[1:], NEIGHBOURS)]


def after(value, *others):
    return lax.optimization_barrier((value, *others))[0]


def body(latent, out_grad, k1, m1, v1, k2, m2, v2):
    scale = 1.0 / (latent.shape[0] * lax.axis_size("dp"))
    table = lax.dynamic_index_in_dim(jnp.asarray(TABLE), lax.axis_index("dp"), keepdims=False)
    columns = jnp.asarray(COLUMNS)

    shards = exchange(pack(k1, k2, columns))
    latent = latent.transpose(1, 2, 3, 0, 4)
    other = swap(latent)
    own = spread(shards)
    latent = after(latent, own)
    cells = prep(latent, other, out_grad.transpose(1, 2, 3, 0, 4), table)
    own = send_round([own] * 4)
    own[1:] = [after(value, cells[0]) for value in own[1:]]
    other = [swap(value) for value in own]
    x3a, x3b, x3o, skip, cot = cells

    act, hsel, hsend = conv1(x3b, conv1_own(x3a, own), other, table)
    hsel_other = swap(hsend)
    block_out, grad_pre, grad_pre_t = conv2(skip, cot, hsel, own, other)
    grad_pre_t_other = swap(grad_pre_t)
    gat = back(act, grad_pre, own, other, table)
    gat_other = swap(gat)
    second = grad2(grad_pre_t, grad_pre_t_other, hsel, hsel_other)
    gat = after(gat, *second)
    second = send_round(second)
    first = send_round(grad1(gat, gat_other, x3a, x3o))
    parts = exchange(collect(first, collect2(second)))
    new = adam(scale, parts, columns, k1, m1, v1, k2, m2, v2)
    return (block_out.transpose(3, 0, 1, 2, 4), *new)


def solution(mesh):
    wide = P("dp", None, None, None, None)
    flat = P(None, "dp")
    return jax.shard_map(
        body,
        mesh=mesh,
        in_specs=(wide, wide) + (flat,) * 6,
        out_specs=(wide,) + (flat,) * 6,
        check_vma=False,
    )
```
